32 devices in a mesh: gz: 4 (over z), gx: 4 (over y, core), gy: 2 (over x).
Axes of the slice: x: 2, y: 2, z: 4, core: 2. Of those that a mesh axis runs over, the one named last changes fastest.
Arguments:
- right_side: float32 [40, 32, 6, 1024], P('gz', 'gy', None, 'gx'), may hold values from -0.0625 to 0.0625
- previous: float32 [40, 32, 6, 1024], P('gz', 'gy', None, 'gx'), may hold values from -0.15625 to 0.15625
- diag_inverse: bfloat16 [40, 32, 6, 6, 1024], P('gz', 'gy', None, None, 'gx'), may hold values from -0.6 to 2.6, as said below
- jacobians: bfloat16 [40, 32, 6, 6, 6, 1024], P('gz', 'gy', None, None, None, 'gx'), may hold values from -3 to 3, as said below
Outputs:
- update: float32 [40, 32, 6, 1024], P('gz', 'gy', None, 'gx')
The draws below stay inside these ranges and needn't reach their ends.
Inputs may be any that keep to these rules, and one draw needn't show every extreme that they name: `diag_inverse`: entries of the cells' inverted diagonal blocks. `jacobians`: entries of the cells' coupling blocks.
All inputs are finite; a program needn't handle non-finite values.
Results may differ from the reference program's by a relative error of at most 0.0003.
Values sent between devices are 32-bit elements; how exact they have to be, the bound alone decides.
No kernel may reach another device: no remote copies, remote signals or barrier semaphores. Data moves between devices by JAX's collectives and lax.ppermute only.
A program may use at most 128 MiB of HBM per device.

```python
import math
import jax
import jax.numpy as jnp
from jax import lax

VARS = 6
NX = 1024
NY = 32
DEPTH_LAYERS = 40


def cell_blocks(key):
    base = jax.random.fold_in(key, 4711)
    parallel_columns = jax.random.split(base, 10)
    unit = jnp.eye(6, dtype=jnp.float32)[:, :, None]
    scale = jnp.exp(jax.random.uniform(parallel_columns[0], (DEPTH_LAYERS, NY, 1, 1, NX), minval=math.log(0.5), maxval=math.log(2.0)))
    offdiag = 0.07 * jnp.clip(jax.random.normal(parallel_columns[1], (DEPTH_LAYERS, NY, 6, 6, NX)), -4.0, 4.0) * (1.0 - unit)
    inverse = scale * (unit + offdiag)
    series = jnp.broadcast_to(unit, (DEPTH_LAYERS, NY, 6, 6, NX))
    for term_index in range(4):
        series = unit - jnp.einsum('zyabx,zybcx->zyacx', offdiag, series)
    fraction = 0.5
    slow = jax.random.uniform(parallel_columns[2], (1, NY, 1, 1, NX)) < fraction
    cell_shape = (DEPTH_LAYERS, NY, 1, 1, NX)
    rate_lower = jnp.where(slow, jax.random.uniform(parallel_columns[3], cell_shape, minval=0.99, maxval=0.998), jax.random.uniform(parallel_columns[4], cell_shape, minval=0.92, maxval=0.96))
    rate_upper = jnp.where(slow, jax.random.uniform(parallel_columns[5], cell_shape, minval=0.99, maxval=0.998), jax.random.uniform(parallel_columns[6], cell_shape, minval=0.92, maxval=0.96))
    layer_indices = jnp.arange(DEPTH_LAYERS)
    forward_triangular_solve = jax.random.randint(parallel_columns[7], (2,), 0, DEPTH_LAYERS)
    backward_triangular_solve = jax.random.randint(parallel_columns[8], (2,), 0, DEPTH_LAYERS)
    subdiagonal_matrices = jnp.where(jnp.any(layer_indices[:, None] == forward_triangular_solve[None, :], axis=1), 0.7, 1.0).reshape(DEPTH_LAYERS, 1, 1, 1, 1)
    superdiagonal_matrices = jnp.where(jnp.any(layer_indices[:, None] == backward_triangular_solve[None, :], axis=1), 0.7, 1.0).reshape(DEPTH_LAYERS, 1, 1, 1, 1)
    lower_z = -(rate_lower * subdiagonal_matrices / scale) * series
    upper_z = -(rate_upper * superdiagonal_matrices / scale) * series
    neighbours = 0.1 * jnp.clip(jax.random.normal(parallel_columns[9], (DEPTH_LAYERS, NY, 4, 6, 6, NX)), -5.0, 5.0)
    coupling = jnp.concatenate([neighbours, lower_z[:, :, None], upper_z[:, :, None]], axis=2)
    return (inverse, coupling)


def draw_diag_inverse(key, part):
    inverse, coupling = cell_blocks(key)
    return inverse.astype(jnp.bfloat16)


def draw_jacobians(key, part):
    inverse, coupling = cell_blocks(key)
    return coupling.astype(jnp.bfloat16)


def block_scale(rng, shape, cuts, low, top_value):
    def one(position, blocks):
        heights = jax.random.uniform(jax.random.fold_in(jax.random.fold_in(rng, 6), position), (blocks,), jnp.float32, low / len(cuts), top_value / len(cuts))
        return jnp.repeat(jnp.exp(heights), shape[position] // blocks).reshape((-1,) + (1,) * (len(shape) - position - 1))

    loudness = one(*cuts[0])
    for cut in cuts[1:]:
        loudness = loudness * one(*cut)
    return loudness


def centred(stream_key, extent, scale, limit, shards=(), kind=jnp.bfloat16):
    values = jax.random.normal(stream_key, extent, jnp.float32) * scale
    if len(shards) > 0:
        values = block_scale(stream_key, extent, shards, -0.22, 0.18) * values
    return jnp.clip(values, min=-limit, max=limit).astype(kind)


def setup_inputs(seed: int = 0) -> dict:
    key_list = jax.random.split(jax.random.key(seed), 5)
    right_side = centred(key_list[0], (DEPTH_LAYERS, NY, VARS, NX), 0.004, 0.0625, ((0, 4), (1, 2), (3, 4)), jnp.float32)
    previous = centred(key_list[1], (DEPTH_LAYERS, NY, VARS, NX), 0.01, 0.15625, ((0, 4), (1, 2), (3, 4)), jnp.float32)
    diag_inverse = draw_diag_inverse(jax.random.fold_in(key_list[4], 71), 0)
    jacobians = draw_jacobians(jax.random.fold_in(key_list[4], 71), 0)
    return dict(right_side=right_side, previous=previous, diag_inverse=diag_inverse, jacobians=jacobians)


def block_apply(blocks, vector):
    return jnp.sum(blocks * vector[..., None, :, :], axis=-2)


def inplane_terms(coupling, padded):
    total = block_apply(coupling[:, 0], padded[1:-1, :, :-2])
    total = total + block_apply(coupling[:, 1], padded[1:-1, :, 2:])
    total = total + block_apply(coupling[:, 2], padded[:-2, :, 1:-1])
    total = total + block_apply(coupling[:, 3], padded[2:, :, 1:-1])
    return total


def pad_plane(plane):
    return jnp.pad(plane, ((1, 1), (0, 0), (1, 1)))


def reference(right_side, previous, diag_inverse, jacobians):
    zeros_plane = jnp.zeros((NY, 6, NX), jnp.float32)

    def forward_step(earlier, planes):
        source, before, inverse, coupling = planes
        inverse = inverse.astype(jnp.float32)
        coupling = coupling.astype(jnp.float32)
        source = source - inplane_terms(coupling, pad_plane(before)) - block_apply(coupling[:, 4], earlier)
        result = block_apply(inverse, source)
        return result, result

    final_plane, sweep_values = lax.scan(forward_step, zeros_plane, (right_side, previous, diag_inverse, jacobians))

    def backward_step(later, planes):
        forward_plane, before, inverse, coupling = planes
        inverse = inverse.astype(jnp.float32)
        coupling = coupling.astype(jnp.float32)
        change = block_apply(coupling[:, 5], later) + inplane_terms(coupling, pad_plane(forward_plane - before))
        result = forward_plane - block_apply(inverse, change)
        return result, result

    last_plane, update = lax.scan(backward_step, zeros_plane, (sweep_values, previous, diag_inverse, jacobians), reverse=True)
    return update
```

```python
import functools

import jax
import jax.numpy as jnp
from jax import lax
from jax.experimental import pallas as pl
from jax.experimental.pallas import tpu as pltpu
from jax.sharding import PartitionSpec as P

VARS = 6
LANES = 128
F32 = jnp.float32
WHOLE = pl.BlockSpec(memory_space=pltpu.VMEM)


def in_vmem(x):
    return pltpu.with_memory_space_constraint(x, pltpu.VMEM)


def call(body, outs, *args, flops, limit=16 << 20):
    moved = sum(a.size * a.dtype.itemsize for a in args)
    return pl.pallas_call(
        body,
        out_shape=[pltpu.VMEM(s, F32) for s in outs],
        in_specs=[WHOLE] * len(args),
        out_specs=[WHOLE] * len(outs),
        cost_estimate=pl.CostEstimate(flops=flops, bytes_accessed=moved, transcendentals=0),
        compiler_params=pltpu.CompilerParams(vmem_limit_bytes=limit),
    )(*[in_vmem(a) for a in args])


def lane_iota(rows):
    return lax.broadcasted_iota(jnp.int32, (rows, LANES), 1)


def row_iota(rows):
    return lax.broadcasted_iota(jnp.int32, (rows, LANES), 0)


def dot6(blocks, values):
    terms = [b.astype(F32) * v for b, v in zip(blocks, values)]
    return (terms[0] + terms[1]) + (terms[2] + terms[3]) + (terms[4] + terms[5])


def block(ref, *index, at):
    return lambda r, c: ref[(*index, r, c, slice(None), at)]


def apply_block(get, values):
    return [dot6([get(r, c) for c in range(VARS)], values) for r in range(VARS)]


def write_faces(value, left, right, rows, z_count, swap):
    y_count = value.shape[2]
    x_count = value.shape[3]
    lane = lane_iota(y_count)
    for face, start, source_lane in ((left, 0, 0), (right, x_count - LANES, LANES - 1)):
        for group in range(face.shape[0]):
            held = jnp.zeros((y_count, LANES), F32)
            for slot in range(min(LANES, z_count * VARS - group * LANES)):
                z, var = divmod(group * LANES + slot, VARS)
                tile = value[z, var, :, start : start + LANES]
                moved = pltpu.roll(tile, (slot - source_lane) % LANES, 1)
                held = jnp.where(lane == slot, moved, held)
            face[group] = held
    if swap:
        first = lax.axis_index("gy") == 0
        for j in range(z_count * VARS):
            z, var = divmod(j, VARS)
            low = value[z, var, 0:1, :]
            high = value[z, var, y_count - 1 : y_count, :]
            rows[0][z, var : var + 1, :] = jnp.where(first, high, low)
    else:
        for j in range(z_count * VARS):
            z, var = divmod(j, VARS)
            rows[0][z, var : var + 1, :] = value[z, var, 0:1, :]
            rows[1][z, var : var + 1, :] = value[z, var, y_count - 1 : y_count, :]


def halo_reader(before_x, after_x, rows, swap):
    def column(face, z, var, lane):
        j = z * VARS + var
        return pltpu.roll(face[j // LANES], (lane - j % LANES) % LANES, 1)

    def row(which, z, var, at):
        if not swap:
            return rows[which][z, var : var + 1, at]
        here = rows[0][z, var : var + 1, at]
        wanted = lax.axis_index("gy") == 1 - which
        return jnp.where(wanted, here, jnp.zeros_like(here))

    return (
        lambda z, var: column(before_x, z, var, 0),
        lambda z, var: column(after_x, z, var, LANES - 1),
        lambda z, var, at: row(0, z, var, at),
        lambda z, var, at: row(1, z, var, at),
    )


def neighbours(value, z, tile, tiles, halo):
    y_count = value.shape[2]
    lane = lane_iota(y_count)
    row = row_iota(y_count)
    at = slice(tile * LANES, (tile + 1) * LANES)
    result = ([], [], [], [])
    for var in range(VARS):
        here = value[z, var, :, at]
        if tile > 0:
            before = pltpu.roll(value[z, var, :, at.start - LANES : at.start], 1, 1)
        else:
            before = halo[0](z, var)
        if tile < tiles - 1:
            after = pltpu.roll(value[z, var, :, at.stop : at.stop + LANES], LANES - 1, 1)
        else:
            after = halo[1](z, var)
        result[0].append(jnp.where(lane == 0, before, pltpu.roll(here, 1, 1)))
        result[1].append(jnp.where(lane == LANES - 1, after, pltpu.roll(here, LANES - 1, 1)))
        result[2].append(jnp.where(row == 0, halo[2](z, var, at), pltpu.roll(here, 1, 0)))
        result[3].append(
            jnp.where(row == y_count - 1, halo[3](z, var, at), pltpu.roll(here, y_count - 1, 0))
        )
    return result


def inplane(jacobians, value, z, tile, tiles, halo):
    at = slice(tile * LANES, (tile + 1) * LANES)
    total = None
    for n, values in enumerate(neighbours(value, z, tile, tiles, halo)):
        part = apply_block(block(jacobians, z, n, at=at), values)
        total = part if total is None else [a + b for a, b in zip(total, part)]
    return total


def planes_of(ref, z, at):
    return [ref[z, var, :, at] for var in range(VARS)]


def solution(mesh):
    gz, gx, gy = (mesh.shape[a] for a in ("gz", "gx", "gy"))
    swap = gy == 2

    def body(right_side, previous, diag_inverse, jacobians):
        rhs = jnp.transpose(right_side, (0, 2, 1, 3))
        prev = jnp.transpose(previous, (0, 2, 1, 3))
        inv = jnp.transpose(diag_inverse, (0, 2, 3, 1, 4))
        jac = jnp.transpose(jacobians, (0, 2, 3, 4, 1, 5))
        nz, _, ny, nx = rhs.shape
        tiles = nx // LANES
        assert nx % LANES == 0
        spans = [slice(t * LANES, (t + 1) * LANES) for t in range(tiles)]
        plane = (VARS, ny, nx)
        volume = (nz, VARS, ny, nx)
        x_face = (-(-nz * VARS // LANES), ny, LANES)
        y_face = (nz, VARS, nx)
        face_shapes = [x_face, x_face] + [y_face] * (1 if swap else 2)
        cells = nz * ny * nx
        block_flops = 2 * VARS * VARS * cells

        def exchange(left, right, *rows):
            up = [(i, i + 1) for i in range(gx - 1)]
            before_x = lax.ppermute(right, "gx", up)
            after_x = lax.ppermute(left, "gx", [(j, i) for i, j in up])
            if swap:
                return before_x, after_x, lax.ppermute(rows[0], "gy", [(0, 1), (1, 0)])
            up = [(i, i + 1) for i in range(gy - 1)]
            before_y = lax.ppermute(rows[1], "gy", up)
            after_y = lax.ppermute(rows[0], "gy", [(j, i) for i, j in up])
            return before_x, after_x, before_y, after_y

        def faces_kernel(value, left, right, *rows):
            write_faces(value, left, right, rows, nz, swap)

        def forward_plane(source, inv_ref, jac_ref, z, at, earlier):
            lagged = apply_block(block(jac_ref, z, 4, at=at), earlier)
            return apply_block(block(inv_ref, z, at=at), [a - b for a, b in zip(source, lagged)])

        def first_kernel(rhs_ref, prev_ref, inv_ref, jac_ref, *rest):
            halo_refs, (source_ref, top_ref) = rest[:-2], rest[-2:]
            halo = halo_reader(halo_refs[0], halo_refs[1], halo_refs[2:], swap)
            for tile, at in enumerate(spans):

                def step(z, earlier, tile=tile, at=at):
                    lagged = inplane(jac_ref, prev_ref, z, tile, tiles, halo)
                    source = [a - b for a, b in zip(planes_of(rhs_ref, z, at), lagged)]
                    for var in range(VARS):
                        source_ref[z, var, :, at] = source[var]
                    return tuple(forward_plane(source, inv_ref, jac_ref, z, at, earlier))

                zero = tuple(jnp.zeros((ny, LANES), F32) for _ in range(VARS))
                top = lax.fori_loop(0, nz, step, zero)
                for var in range(VARS):
                    top_ref[var, :, at] = top[var]

        def incoming(refs, at):
            total = [refs[0][var, :, at] for var in range(VARS)]
            for ref in refs[1:]:
                total = [a + ref[var, :, at] for var, a in enumerate(total)]
            return tuple(total)

        def forward_kernel(source_ref, inv_ref, jac_ref, *rest):
            came, top_ref = rest[:-1], rest[-1]
            for at in spans:

                def step(z, earlier, at=at):
                    source = planes_of(source_ref, z, at)
                    return tuple(forward_plane(source, inv_ref, jac_ref, z, at, earlier))

                top = lax.fori_loop(0, nz, step, incoming(came, at))
                for var in range(VARS):
                    top_ref[var, :, at] = top[var]

        def forward_last_kernel(source_ref, prev_ref, inv_ref, jac_ref, *rest):
            came, (sweep_ref, change_ref, left, right, *rows) = rest[: gz - 1], rest[gz - 1 :]
            for at in spans:

                def step(z, earlier, at=at):
                    source = planes_of(source_ref, z, at)
                    result = forward_plane(source, inv_ref, jac_ref, z, at, earlier)
                    before = planes_of(prev_ref, z, at)
                    for var in range(VARS):
                        sweep_ref[z, var, :, at] = result[var]
                        change_ref[z, var, :, at] = result[var] - before[var]
                    return tuple(result)

                lax.fori_loop(0, nz, step, incoming(came, at))
            write_faces(change_ref, left, right, rows, nz, swap)

        def backward_plane(sweep, inner, inv_ref, jac_ref, z, at, later):
            change = apply_block(block(jac_ref, z, 5, at=at), later)
            change = apply_block(block(inv_ref, z, at=at), [a + b for a, b in zip(change, inner)])
            return [a - b for a, b in zip(sweep, change)]

        def inner_kernel(sweep_ref, change_ref, inv_ref, jac_ref, *rest):
            halo_refs, (inner_ref, low_ref) = rest[:-2], rest[-2:]
            halo = halo_reader(halo_refs[0], halo_refs[1], halo_refs[2:], swap)
            for tile, at in enumerate(spans):

                def step(i, later, tile=tile, at=at):
                    z = nz - 1 - i
                    inner = inplane(jac_ref, change_ref, z, tile, tiles, halo)
                    for var in range(VARS):
                        inner_ref[z, var, :, at] = inner[var]
                    sweep = planes_of(sweep_ref, z, at)
                    return tuple(backward_plane(sweep, inner, inv_ref, jac_ref, z, at, later))

                zero = tuple(jnp.zeros((ny, LANES), F32) for _ in range(VARS))
                low = lax.fori_loop(0, nz, step, zero)
                for var in range(VARS):
                    low_ref[var, :, at] = low[var]

        def backward_kernel(keep, sweep_ref, inner_ref, inv_ref, jac_ref, *rest):
            came, out_ref = rest[:-1], rest[-1]
            for at in spans:

                def step(i, later, at=at):
                    z = nz - 1 - i
                    sweep, inner = planes_of(sweep_ref, z, at), planes_of(inner_ref, z, at)
                    result = backward_plane(sweep, inner, inv_ref, jac_ref, z, at, later)
                    if keep:
                        for var in range(VARS):
                            out_ref[z, var, :, at] = result[var]
                    return tuple(result)

                low = lax.fori_loop(0, nz, step, incoming(came, at))
                if not keep:
                    for var in range(VARS):
                        out_ref[var, :, at] = low[var]

        faces = call(faces_kernel, face_shapes, prev, flops=cells)
        halo = exchange(*faces)
        source, top = call(
            first_kernel, [volume, plane], rhs, prev, inv, jac, *halo, flops=6 * block_flops
        )
        came = []
        for hop in range(gz - 1):
            if hop:
                (top,) = call(
                    forward_kernel, [plane], source, inv, jac, *came, flops=2 * block_flops
                )
            came.append(lax.ppermute(top, "gz", [(hop, hop + 1)]))
        sweep, change, *faces = call(
            forward_last_kernel,
            [volume, volume, *face_shapes],
            source,
            prev,
            inv,
            jac,
            *came,
            flops=2 * block_flops,
        )
        halo = exchange(*faces)
        inner, low = call(
            inner_kernel, [volume, plane], sweep, change, inv, jac, *halo, flops=6 * block_flops
        )
        came = []
        for hop in range(gz - 1, 0, -1):
            if came:
                (low,) = call(
                    functools.partial(backward_kernel, False),
                    [plane],
                    sweep,
                    inner,
                    inv,
                    jac,
                    *came,
                    flops=2 * block_flops,
                )
            came.append(lax.ppermute(low, "gz", [(hop, hop - 1)]))
        (update,) = call(
            functools.partial(backward_kernel, True),
            [volume],
            sweep,
            inner,
            inv,
            jac,
            *came,
            flops=2 * block_flops,
        )
        return jnp.transpose(update, (0, 2, 1, 3))

    placed = (
        P("gz", "gy", None, "gx"),
        P("gz", "gy", None, "gx"),
        P("gz", "gy", None, None, "gx"),
        P("gz", "gy", None, None, None, "gx"),
    )
    return jax.shard_map(
        body, mesh=mesh, in_specs=placed, out_specs=P("gz", "gy", None, "gx"), check_vma=False
    )
```

```python
import jax
import jax.numpy as jnp
from jax import lax
from jax.experimental import pallas as pl
from jax.experimental.pallas import tpu as pltpu
from jax.sharding import PartitionSpec as P

VARS = 6
LANES = 128
F32 = jnp.float32
WHOLE = pl.BlockSpec(memory_space=pltpu.VMEM)


def call(body, outs, *args, flops, limit=16 << 20, scratch=(), in_hbm=(), out_hbm=()):
    far = pl.BlockSpec(memory_space=pl.ANY)
    shapes = [
        jax.ShapeDtypeStruct(o[0], o[1]) if i in out_hbm else pltpu.VMEM(o[0], o[1])
        for i, o in enumerate(outs)
    ]
    moved = sum(a.size * a.dtype.itemsize for a in args)
    return pl.pallas_call(
        body,
        out_shape=shapes,
        in_specs=[far if i in in_hbm else WHOLE for i in range(len(args))],
        out_specs=[far if i in out_hbm else WHOLE for i in range(len(outs))],
        scratch_shapes=scratch,
        cost_estimate=pl.CostEstimate(flops=flops, bytes_accessed=moved, transcendentals=0),
        compiler_params=pltpu.CompilerParams(vmem_limit_bytes=limit),
    )(*[
        pltpu.with_memory_space_constraint(a, pltpu.HBM if i in in_hbm else pltpu.VMEM)
        for i, a in enumerate(args)
    ])


def lane_iota(rows):
    return lax.broadcasted_iota(jnp.int32, (rows, LANES), 1)


def row_iota(rows):
    return lax.broadcasted_iota(jnp.int32, (rows, LANES), 0)


def dot6(blocks, values):
    terms = [b.astype(F32) * v for b, v in zip(blocks, values)]
    return (terms[0] + terms[1]) + (terms[2] + terms[3]) + (terms[4] + terms[5])


def block(ref, *index, at):
    return lambda r, c: ref[(*index, r, c, slice(None), at)]


def apply_block(get, values):
    return [dot6([get(r, c) for c in range(VARS)], values) for r in range(VARS)]


def write_faces(value, x_face, y_face, z_count):
    y_count = value.shape[2]
    x_count = value.shape[3]
    lane = lane_iota(y_count)
    for side, start, source_lane in ((0, 0, 0), (1, x_count - LANES, LANES - 1)):
        for group in range(x_face.shape[1]):
            held = jnp.zeros((y_count, LANES), F32)
            for slot in range(min(LANES, z_count * VARS - group * LANES)):
                z, var = divmod(group * LANES + slot, VARS)
                tile = value[z, var, :, start : start + LANES]
                moved = pltpu.roll(tile, (slot - source_lane) % LANES, 1)
                held = jnp.where(lane == slot, moved, held)
            x_face[side, group] = held
    if y_face.shape[0] == 1:
        first = lax.axis_index("gy") == 0
        for z in range(z_count):
            for var in range(VARS):
                low = value[z, var, 0:1, :]
                high = value[z, var, y_count - 1 : y_count, :]
                y_face[0, z, var : var + 1, :] = jnp.where(first, high, low)
    else:
        for z in range(z_count):
            for var in range(VARS):
                y_face[0, z, var : var + 1, :] = value[z, var, 0:1, :]
                y_face[1, z, var : var + 1, :] = value[z, var, y_count - 1 : y_count, :]


def neighbours(value, z, tile, tiles):
    y_count = value.shape[2]
    lane = lane_iota(y_count)
    row = row_iota(y_count)
    at = slice(tile * LANES, (tile + 1) * LANES)
    zero = jnp.zeros((y_count, LANES), F32)
    result = ([], [], [], [])
    for var in range(VARS):
        here = value[z, var, :, at]
        before, after = zero, zero
        if tile > 0:
            before = pltpu.roll(value[z, var, :, at.start - LANES : at.start], 1, 1)
        if tile < tiles - 1:
            after = pltpu.roll(value[z, var, :, at.stop : at.stop + LANES], LANES - 1, 1)
        result[0].append(jnp.where(lane == 0, before, pltpu.roll(here, 1, 1)))
        result[1].append(jnp.where(lane == LANES - 1, after, pltpu.roll(here, LANES - 1, 1)))
        result[2].append(jnp.where(row == 0, zero, pltpu.roll(here, 1, 0)))
        result[3].append(jnp.where(row == y_count - 1, zero, pltpu.roll(here, y_count - 1, 0)))
    return result


def inplane(jacobians, value, z, tile, tiles):
    at = slice(tile * LANES, (tile + 1) * LANES)
    total = None
    for n, values in enumerate(neighbours(value, z, tile, tiles)):
        part = apply_block(block(jacobians, z, n, at=at), values)
        total = part if total is None else [a + b for a, b in zip(total, part)]
    return total


def halo_terms(jacobians, x_all, y_all, z, tile, tiles, gx, gy):
    y_count = jacobians.shape[-2]
    lane = lane_iota(y_count)
    row = row_iota(y_count)
    at = slice(tile * LANES, (tile + 1) * LANES)
    zero = jnp.zeros((y_count, LANES), F32)
    parts = []

    def columns(there, side, mask, to_lane):
        exists = (there >= 0) & (there < gx)
        device = jnp.clip(there, 0, gx - 1)
        values = []
        for var in range(VARS):
            j = z * VARS + var
            face = x_all[device, side, j // LANES]
            moved = pltpu.roll(face, (to_lane + LANES - j % LANES) % LANES, 1)
            values.append(jnp.where(mask & exists, moved, zero))
        return values

    def rows(there, side, mask):
        exists = (there >= 0) & (there < gy)
        device = jnp.clip(there, 0, gy - 1)
        return [
            jnp.where(mask & exists, y_all[device, side, z, var : var + 1, at], zero)
            for var in range(VARS)
        ]

    me_x, me_y = lax.axis_index("gx"), lax.axis_index("gy")
    if tile == 0:
        values = columns(me_x - 1, 1, lane == 0, 0)
        parts.append(apply_block(block(jacobians, z, 0, at=at), values))
    if tile == tiles - 1:
        values = columns(me_x + 1, 0, lane == LANES - 1, LANES - 1)
        parts.append(apply_block(block(jacobians, z, 1, at=at), values))
    if gy == 2:
        edge = jnp.where(me_y == 0, y_count - 1, 0)
        values = rows(1 - me_y, 0, row == edge)
        parts.append(apply_block(block(jacobians, z, 3 - me_y, at=at), values))
    else:
        parts.append(apply_block(block(jacobians, z, 2, at=at), rows(me_y - 1, 1, row == 0)))
        last = row == y_count - 1
        parts.append(apply_block(block(jacobians, z, 3, at=at), rows(me_y + 1, 0, last)))
    total = parts[0]
    for part in parts[1:]:
        total = [a + b for a, b in zip(total, part)]
    return total


def planes_of(ref, z, at):
    return [ref[z, var, :, at] for var in range(VARS)]


def solution(mesh):
    gz, gx, gy = (mesh.shape[a] for a in ("gz", "gx", "gy"))

    def body(right_side, previous, diag_inverse, jacobians):
        rhs = jnp.transpose(right_side, (0, 2, 1, 3))
        prev = jnp.transpose(previous, (0, 2, 1, 3))
        inv = jnp.transpose(diag_inverse, (0, 2, 3, 1, 4))
        jac = jnp.transpose(jacobians, (0, 2, 3, 4, 1, 5))
        nz, _, ny, nx = rhs.shape
        tiles = nx // LANES
        assert nx % LANES == 0
        spans = [slice(t * LANES, (t + 1) * LANES) for t in range(tiles)]
        plane = (VARS, ny, nx)
        volume = (nz, VARS, ny, nx)
        x_face = ((2, -(-nz * VARS // LANES), ny, LANES), F32)
        y_face = ((1 if gy == 2 else 2, nz, VARS, nx), F32)
        plane, volume = (plane, F32), (volume, F32)
        cells = nz * ny * nx
        block_flops = 2 * VARS * VARS * cells

        def exchange(x_face, y_face):
            return lax.all_gather(x_face, "gx"), lax.all_gather(y_face, "gy")

        def faces_kernel(prev_hbm, prev_ref, x_face, y_face, sem):
            copy = pltpu.make_async_copy(prev_hbm, prev_ref, sem)
            copy.start()
            copy.wait()
            write_faces(prev_ref, x_face, y_face, nz)

        def forward_plane(source, inv_ref, jac_ref, z, at, earlier):
            lagged = apply_block(block(jac_ref, z, 4, at=at), earlier)
            return apply_block(block(inv_ref, z, at=at), [a - b for a, b in zip(source, lagged)])

        def load_kernel(rhs_hbm, inv_hbm, jac_hbm, prev_ref, source_ref, inv_ref, jac_ref, rhs_ref, sems):
            def copies(z):
                pairs = ((jac_hbm, jac_ref), (rhs_hbm, rhs_ref), (inv_hbm, inv_ref))
                return [
                    pltpu.make_async_copy(far.at[z], near.at[z], sems.at[i, z])
                    for i, (far, near) in enumerate(pairs)
                ]

            for z in range(nz):
                for copy in copies(z):
                    copy.start()

            def step(z, carry):
                waits = copies(z)
                waits[0].wait()
                waits[1].wait()
                for tile, at in enumerate(spans):
                    lagged = inplane(jac_ref, prev_ref, z, tile, tiles)
                    source = planes_of(rhs_ref, z, at)
                    for var in range(VARS):
                        source_ref[z, var, :, at] = source[var] - lagged[var]
                waits[2].wait()
                return carry

            lax.fori_loop(0, nz, step, 0)

        def first_kernel(part_ref, inv_ref, jac_ref, x_all, y_all, source_ref, top_ref):
            for tile, at in enumerate(spans):

                def step(z, earlier, tile=tile, at=at):
                    extra = halo_terms(jac_ref, x_all, y_all, z, tile, tiles, gx, gy)
                    source = [a - b for a, b in zip(planes_of(part_ref, z, at), extra)]
                    for var in range(VARS):
                        source_ref[z, var, :, at] = source[var]
                    return tuple(forward_plane(source, inv_ref, jac_ref, z, at, earlier))

                zero = tuple(jnp.zeros((ny, LANES), F32) for _ in range(VARS))
                top = lax.fori_loop(0, nz, step, zero)
                for var in range(VARS):
                    top_ref[var, :, at] = top[var]

        def incoming(refs, at):
            total = [refs[0][var, :, at] for var in range(VARS)]
            for ref in refs[1:]:
                total = [a + ref[var, :, at] for var, a in enumerate(total)]
            return tuple(total)

        def forward_kernel(source_ref, inv_ref, jac_ref, *rest):
            came, top_ref = rest[:-1], rest[-1]
            for at in spans:

                def step(z, earlier, at=at):
                    source = planes_of(source_ref, z, at)
                    return tuple(forward_plane(source, inv_ref, jac_ref, z, at, earlier))

                top = lax.fori_loop(0, nz, step, incoming(came, at))
                for var in range(VARS):
                    top_ref[var, :, at] = top[var]

        def forward_last_kernel(source_ref, prev_ref, inv_ref, jac_ref, *rest):
            came, (sweep_ref, change_ref, x_face, y_face) = rest[:-4], rest[-4:]
            for at in spans:

                def step(z, earlier, at=at):
                    source = planes_of(source_ref, z, at)
                    result = forward_plane(source, inv_ref, jac_ref, z, at, earlier)
                    before = planes_of(prev_ref, z, at)
                    for var in range(VARS):
                        sweep_ref[z, var, :, at] = result[var]
                        change_ref[z, var, :, at] = result[var] - before[var]
                    return tuple(result)

                lax.fori_loop(0, nz, step, incoming(came, at))
            write_faces(change_ref, x_face, y_face, nz)

        def backward_plane(sweep, inner, inv_ref, jac_ref, z, at, later):
            change = apply_block(block(jac_ref, z, 5, at=at), later)
            change = apply_block(block(inv_ref, z, at=at), [a + b for a, b in zip(change, inner)])
            return [a - b for a, b in zip(sweep, change)]

        def inner_kernel(change_ref, jac_ref, inner_ref):
            def step(z, carry):
                for tile, at in enumerate(spans):
                    inner = inplane(jac_ref, change_ref, z, tile, tiles)
                    for var in range(VARS):
                        inner_ref[z, var, :, at] = inner[var]
                return carry

            lax.fori_loop(0, nz, step, 0)

        def turn_kernel(sweep_ref, part_ref, inv_ref, jac_ref, x_all, y_all, inner_ref, low_ref):
            for tile, at in enumerate(spans):

                def step(i, later, tile=tile, at=at):
                    z = nz - 1 - i
                    extra = halo_terms(jac_ref, x_all, y_all, z, tile, tiles, gx, gy)
                    inner = [a + b for a, b in zip(planes_of(part_ref, z, at), extra)]
                    for var in range(VARS):
                        inner_ref[z, var, :, at] = inner[var]
                    sweep = planes_of(sweep_ref, z, at)
                    return tuple(backward_plane(sweep, inner, inv_ref, jac_ref, z, at, later))

                zero = tuple(jnp.zeros((ny, LANES), F32) for _ in range(VARS))
                low = lax.fori_loop(0, nz, step, zero)
                for var in range(VARS):
                    low_ref[var, :, at] = low[var]

        def backward_kernel(sweep_ref, inner_ref, inv_ref, jac_ref, *rest):
            came, low_ref = rest[:-1], rest[-1]
            for at in spans:

                def step(i, later, at=at):
                    z = nz - 1 - i
                    sweep, inner = planes_of(sweep_ref, z, at), planes_of(inner_ref, z, at)
                    return tuple(backward_plane(sweep, inner, inv_ref, jac_ref, z, at, later))

                low = lax.fori_loop(0, nz, step, incoming(came, at))
                for var in range(VARS):
                    low_ref[var, :, at] = low[var]

        def update_kernel(sweep_ref, inner_ref, inv_ref, jac_ref, *rest):
            came, (out_hbm, held, sems) = rest[:-3], rest[-3:]

            def out_copy(z):
                return pltpu.make_async_copy(held.at[z], out_hbm.at[z], sems.at[z])

            def step(i, later):
                z = nz - 1 - i
                results = []
                for tile, at in enumerate(spans):
                    sweep, inner = planes_of(sweep_ref, z, at), planes_of(inner_ref, z, at)
                    result = backward_plane(sweep, inner, inv_ref, jac_ref, z, at, later[tile])
                    for var in range(VARS):
                        held[z, var, :, at] = result[var]
                    results.append(tuple(result))
                out_copy(z).start()
                return tuple(results)

            lax.fori_loop(0, nz, step, tuple(incoming(came, at) for at in spans))
            for z in range(nz):
                out_copy(z).wait()

        prev, *faces = call(
            faces_kernel,
            [volume, x_face, y_face],
            prev,
            flops=cells,
            in_hbm=(0,),
            scratch=[pltpu.SemaphoreType.DMA],
        )
        halo = exchange(*faces)
        part, inv, jac = call(
            load_kernel,
            [volume, (inv.shape, inv.dtype), (jac.shape, jac.dtype)],
            rhs,
            inv,
            jac,
            prev,
            flops=4 * block_flops,
            in_hbm=(0, 1, 2),
            scratch=[pltpu.VMEM(rhs.shape, F32), pltpu.SemaphoreType.DMA((3, nz))],
        )
        source, top = call(first_kernel, [volume, plane], part, inv, jac, *halo, flops=4 * block_flops)
        came = []
        for hop in range(gz - 1):
            if hop:
                (top,) = call(forward_kernel, [plane], source, inv, jac, *came, flops=2 * block_flops)
            came.append(lax.ppermute(top, "gz", [(hop, hop + 1)]))
        sweep, change, *faces = call(
            forward_last_kernel,
            [volume, volume, x_face, y_face],
            source,
            prev,
            inv,
            jac,
            *came,
            flops=2 * block_flops,
        )
        halo = exchange(*faces)
        (part,) = call(inner_kernel, [volume], change, jac, flops=4 * block_flops)
        inner, low = call(
            turn_kernel, [volume, plane], sweep, part, inv, jac, *halo, flops=4 * block_flops
        )
        came = []
        for hop in range(gz - 1, 0, -1):
            if came:
                (low,) = call(
                    backward_kernel, [plane], sweep, inner, inv, jac, *came, flops=2 * block_flops
                )
            came.append(lax.ppermute(low, "gz", [(hop, hop - 1)]))
        (update,) = call(
            update_kernel,
            [volume],
            sweep,
            inner,
            inv,
            jac,
            *came,
            flops=2 * block_flops,
            out_hbm=(0,),
            scratch=[pltpu.VMEM(volume[0], F32), pltpu.SemaphoreType.DMA((nz,))],
        )
        return jnp.transpose(update, (0, 2, 1, 3))

    placed = (
        P("gz", "gy", None, "gx"),
        P("gz", "gy", None, "gx"),
        P("gz", "gy", None, None, "gx"),
        P("gz", "gy", None, None, None, "gx"),
    )
    return jax.shard_map(
        body, mesh=mesh, in_specs=placed, out_specs=P("gz", "gy", None, "gx"), check_vma=False
    )
```

```python
import jax
import jax.numpy as jnp
from jax import lax
from jax.experimental import pallas as pl
from jax.experimental.pallas import tpu as pltpu
from jax.sharding import PartitionSpec as P

VARS = 6
LANES = 128
F32 = jnp.float32
WHOLE = pl.BlockSpec(memory_space=pltpu.VMEM)


def call(body, outs, *args, flops, limit=16 << 20, scratch=(), in_hbm=(), out_hbm=()):
    far = pl.BlockSpec(memory_space=pl.ANY)
    shapes = [
        jax.ShapeDtypeStruct(o[0], o[1]) if i in out_hbm else pltpu.VMEM(o[0], o[1])
        for i, o in enumerate(outs)
    ]
    moved = sum(a.size * a.dtype.itemsize for a in args)
    return pl.pallas_call(
        body,
        out_shape=shapes,
        in_specs=[far if i in in_hbm else WHOLE for i in range(len(args))],
        out_specs=[far if i in out_hbm else WHOLE for i in range(len(outs))],
        scratch_shapes=scratch,
        cost_estimate=pl.CostEstimate(flops=flops, bytes_accessed=moved, transcendentals=0),
        compiler_params=pltpu.CompilerParams(vmem_limit_bytes=limit),
    )(*[
        pltpu.with_memory_space_constraint(a, pltpu.HBM if i in in_hbm else pltpu.VMEM)
        for i, a in enumerate(args)
    ])


def lane_iota(rows):
    return lax.broadcasted_iota(jnp.int32, (rows, LANES), 1)


def row_iota(rows):
    return lax.broadcasted_iota(jnp.int32, (rows, LANES), 0)


def dot6(blocks, values):
    terms = [b.astype(F32) * v for b, v in zip(blocks, values)]
    return (terms[0] + terms[1]) + (terms[2] + terms[3]) + (terms[4] + terms[5])


def block(ref, *index, at):
    return lambda r, c: ref[(*index, r, c, slice(None), at)]


def apply_block(get, values):
    return [dot6([get(r, c) for c in range(VARS)], values) for r in range(VARS)]


def write_faces(value, x_face, y_face, z_count):
    y_count = value.shape[2]
    x_count = value.shape[3]
    lane = lane_iota(y_count)
    for side, start, source_lane in ((0, 0, 0), (1, x_count - LANES, LANES - 1)):
        for group in range(x_face.shape[1]):
            held = jnp.zeros((y_count, LANES), F32)
            for slot in range(min(LANES, z_count * VARS - group * LANES)):
                z, var = divmod(group * LANES + slot, VARS)
                tile = value[z, var, :, start : start + LANES]
                moved = pltpu.roll(tile, (slot - source_lane) % LANES, 1)
                held = jnp.where(lane == slot, moved, held)
            x_face[side, group] = held
    if y_face.shape[0] == 1:
        first = lax.axis_index("gy") == 0
        for z in range(z_count):
            for var in range(VARS):
                low = value[z, var, 0:1, :]
                high = value[z, var, y_count - 1 : y_count, :]
                y_face[0, z, var : var + 1, :] = jnp.where(first, high, low)
    else:
        for z in range(z_count):
            for var in range(VARS):
                y_face[0, z, var : var + 1, :] = value[z, var, 0:1, :]
                y_face[1, z, var : var + 1, :] = value[z, var, y_count - 1 : y_count, :]


def halo_reader(x_all, y_rows, gx, gy):
    me_x = lax.axis_index("gx")

    def column(there, side, to_lane):
        exists = (there >= 0) & (there < gx)
        device = jnp.clip(there, 0, gx - 1)

        def read(z, var):
            j = z * VARS + var
            face = x_all[device, side, j // LANES]
            moved = pltpu.roll(face, (to_lane + LANES - j % LANES) % LANES, 1)
            return jnp.where(exists, moved, jnp.zeros_like(moved))

        return read

    def row(which):
        def read(z, var, at):
            if len(y_rows) > 1:
                return y_rows[which][z, var : var + 1, at]
            here = y_rows[0][z, var : var + 1, at]
            return jnp.where(lax.axis_index("gy") == 1 - which, here, jnp.zeros_like(here))

        return read

    return column(me_x - 1, 1, 0), column(me_x + 1, 0, LANES - 1), row(0), row(1)


def neighbours(value, z, tile, tiles, halo):
    y_count = value.shape[2]
    lane = lane_iota(y_count)
    row = row_iota(y_count)
    at = slice(tile * LANES, (tile + 1) * LANES)
    result = ([], [], [], [])
    for var in range(VARS):
        here = value[z, var, :, at]
        if tile > 0:
            before = pltpu.roll(value[z, var, :, at.start - LANES : at.start], 1, 1)
        else:
            before = halo[0](z, var)
        if tile < tiles - 1:
            after = pltpu.roll(value[z, var, :, at.stop : at.stop + LANES], LANES - 1, 1)
        else:
            after = halo[1](z, var)
        result[0].append(jnp.where(lane == 0, before, pltpu.roll(here, 1, 1)))
        result[1].append(jnp.where(lane == LANES - 1, after, pltpu.roll(here, LANES - 1, 1)))
        result[2].append(jnp.where(row == 0, halo[2](z, var, at), pltpu.roll(here, 1, 0)))
        result[3].append(
            jnp.where(row == y_count - 1, halo[3](z, var, at), pltpu.roll(here, y_count - 1, 0))
        )
    return result


def inplane(jacobians, value, z, tile, tiles, halo):
    at = slice(tile * LANES, (tile + 1) * LANES)
    total = None
    for n, values in enumerate(neighbours(value, z, tile, tiles, halo)):
        part = apply_block(block(jacobians, z, n, at=at), values)
        total = part if total is None else [a + b for a, b in zip(total, part)]
    return total


def planes_of(ref, z, at):
    return [ref[z, var, :, at] for var in range(VARS)]


def solution(mesh):
    gz, gx, gy = (mesh.shape[a] for a in ("gz", "gx", "gy"))

    def body(right_side, previous, diag_inverse, jacobians):
        rhs = jnp.transpose(right_side, (0, 2, 1, 3))
        prev = jnp.transpose(previous, (0, 2, 1, 3))
        inv = jnp.transpose(diag_inverse, (0, 2, 3, 1, 4))
        jac = jnp.transpose(jacobians, (0, 2, 3, 4, 1, 5))
        nz, _, ny, nx = rhs.shape
        tiles = nx // LANES
        assert nx % LANES == 0
        spans = [slice(t * LANES, (t + 1) * LANES) for t in range(tiles)]
        plane = (VARS, ny, nx)
        volume = (nz, VARS, ny, nx)
        x_face = ((2, -(-nz * VARS // LANES), ny, LANES), F32)
        y_face = ((1 if gy == 2 else 2, nz, VARS, nx), F32)
        plane, volume = (plane, F32), (volume, F32)
        cells = nz * ny * nx
        block_flops = 2 * VARS * VARS * cells

        def exchange(x_face, y_face):
            if gy == 2:
                rows = [lax.ppermute(y_face[0], "gy", [(0, 1), (1, 0)])]
            else:
                up = [(i, i + 1) for i in range(gy - 1)]
                rows = [
                    lax.ppermute(y_face[1], "gy", up),
                    lax.ppermute(y_face[0], "gy", [(j, i) for i, j in up]),
                ]
            return lax.all_gather(x_face, "gx"), *rows

        def faces_kernel(prev_hbm, prev_ref, x_face, y_face, sem):
            copy = pltpu.make_async_copy(prev_hbm, prev_ref, sem)
            copy.start()
            copy.wait()
            write_faces(prev_ref, x_face, y_face, nz)

        def forward_plane(source, inv_ref, jac_ref, z, at, earlier):
            lagged = apply_block(block(jac_ref, z, 4, at=at), earlier)
            return apply_block(block(inv_ref, z, at=at), [a - b for a, b in zip(source, lagged)])

        def first_kernel(rhs_hbm, inv_hbm, jac_hbm, prev_ref, x_all, *rest):
            y_rows, (source_ref, top_ref, inv_ref, jac_ref, rhs_ref, sems) = rest[:-6], rest[-6:]
            halo = halo_reader(x_all, y_rows, gx, gy)

            def copies(z):
                pairs = ((jac_hbm, jac_ref), (rhs_hbm, rhs_ref), (inv_hbm, inv_ref))
                return [
                    pltpu.make_async_copy(far.at[z], near.at[z], sems.at[i, z])
                    for i, (far, near) in enumerate(pairs)
                ]

            for z in range(nz):
                for copy in copies(z):
                    copy.start()

            def step(z, earlier):
                for copy in copies(z):
                    copy.wait()
                results = []
                for tile, at in enumerate(spans):
                    lagged = inplane(jac_ref, prev_ref, z, tile, tiles, halo)
                    source = [a - b for a, b in zip(planes_of(rhs_ref, z, at), lagged)]
                    for var in range(VARS):
                        source_ref[z, var, :, at] = source[var]
                    result = forward_plane(source, inv_ref, jac_ref, z, at, earlier[tile])
                    results.append(tuple(result))
                return tuple(results)

            zero = tuple(jnp.zeros((ny, LANES), F32) for _ in range(VARS))
            top = lax.fori_loop(0, nz, step, (zero,) * tiles)
            for tile, at in enumerate(spans):
                for var in range(VARS):
                    top_ref[var, :, at] = top[tile][var]

        def incoming(refs, at):
            total = [refs[0][var, :, at] for var in range(VARS)]
            for ref in refs[1:]:
                total = [a + ref[var, :, at] for var, a in enumerate(total)]
            return tuple(total)

        def forward_kernel(source_ref, inv_ref, jac_ref, *rest):
            came, top_ref = rest[:-1], rest[-1]
            for at in spans:

                def step(z, earlier, at=at):
                    source = planes_of(source_ref, z, at)
                    return tuple(forward_plane(source, inv_ref, jac_ref, z, at, earlier))

                top = lax.fori_loop(0, nz, step, incoming(came, at))
                for var in range(VARS):
                    top_ref[var, :, at] = top[var]

        def forward_last_kernel(source_ref, prev_ref, inv_ref, jac_ref, *rest):
            came, (sweep_ref, change_ref, x_face, y_face) = rest[:-4], rest[-4:]
            for at in spans:

                def step(z, earlier, at=at):
                    source = planes_of(source_ref, z, at)
                    result = forward_plane(source, inv_ref, jac_ref, z, at, earlier)
                    before = planes_of(prev_ref, z, at)
                    for var in range(VARS):
                        sweep_ref[z, var, :, at] = result[var]
                        change_ref[z, var, :, at] = result[var] - before[var]
                    return tuple(result)

                lax.fori_loop(0, nz, step, incoming(came, at))
            write_faces(change_ref, x_face, y_face, nz)

        def backward_plane(sweep, inner, inv_ref, jac_ref, z, at, later):
            change = apply_block(block(jac_ref, z, 5, at=at), later)
            change = apply_block(block(inv_ref, z, at=at), [a + b for a, b in zip(change, inner)])
            return [a - b for a, b in zip(sweep, change)]

        def turn_kernel(sweep_ref, change_ref, inv_ref, jac_ref, x_all, *rest):
            y_rows, (inner_ref, low_ref) = rest[:-2], rest[-2:]
            halo = halo_reader(x_all, y_rows, gx, gy)
            for tile, at in enumerate(spans):

                def step(i, later, tile=tile, at=at):
                    z = nz - 1 - i
                    inner = inplane(jac_ref, change_ref, z, tile, tiles, halo)
                    for var in range(VARS):
                        inner_ref[z, var, :, at] = inner[var]
                    sweep = planes_of(sweep_ref, z, at)
                    return tuple(backward_plane(sweep, inner, inv_ref, jac_ref, z, at, later))

                zero = tuple(jnp.zeros((ny, LANES), F32) for _ in range(VARS))
                low = lax.fori_loop(0, nz, step, zero)
                for var in range(VARS):
                    low_ref[var, :, at] = low[var]

        def backward_kernel(sweep_ref, inner_ref, inv_ref, jac_ref, *rest):
            came, low_ref = rest[:-1], rest[-1]
            for at in spans:

                def step(i, later, at=at):
                    z = nz - 1 - i
                    sweep, inner = planes_of(sweep_ref, z, at), planes_of(inner_ref, z, at)
                    return tuple(backward_plane(sweep, inner, inv_ref, jac_ref, z, at, later))

                low = lax.fori_loop(0, nz, step, incoming(came, at))
                for var in range(VARS):
                    low_ref[var, :, at] = low[var]

        def update_kernel(sweep_ref, inner_ref, inv_ref, jac_ref, *rest):
            came, (out_hbm, held, sems) = rest[:-3], rest[-3:]

            def out_copy(z):
                return pltpu.make_async_copy(held.at[z], out_hbm.at[z], sems.at[z])

            def step(i, later):
                z = nz - 1 - i
                results = []
                for tile, at in enumerate(spans):
                    sweep, inner = planes_of(sweep_ref, z, at), planes_of(inner_ref, z, at)
                    result = backward_plane(sweep, inner, inv_ref, jac_ref, z, at, later[tile])
                    for var in range(VARS):
                        held[z, var, :, at] = result[var]
                    results.append(tuple(result))
                out_copy(z).start()
                return tuple(results)

            lax.fori_loop(0, nz, step, tuple(incoming(came, at) for at in spans))
            for z in range(nz):
                out_copy(z).wait()

        prev, *faces = call(
            faces_kernel,
            [volume, x_face, y_face],
            prev,
            flops=cells,
            in_hbm=(0,),
            scratch=[pltpu.SemaphoreType.DMA],
        )
        halo = exchange(*faces)
        source, top, inv, jac = call(
            first_kernel,
            [volume, plane, (inv.shape, inv.dtype), (jac.shape, jac.dtype)],
            rhs,
            inv,
            jac,
            prev,
            *halo,
            flops=6 * block_flops,
            in_hbm=(0, 1, 2),
            scratch=[pltpu.VMEM(rhs.shape, F32), pltpu.SemaphoreType.DMA((3, nz))],
        )
        came = []
        for hop in range(gz - 1):
            if hop:
                (top,) = call(forward_kernel, [plane], source, inv, jac, *came, flops=2 * block_flops)
            came.append(lax.ppermute(top, "gz", [(hop, hop + 1)]))
        sweep, change, *faces = call(
            forward_last_kernel,
            [volume, volume, x_face, y_face],
            source,
            prev,
            inv,
            jac,
            *came,
            flops=2 * block_flops,
        )
        halo = exchange(*faces)
        inner, low = call(
            turn_kernel, [volume, plane], sweep, change, inv, jac, *halo, flops=6 * block_flops
        )
        came = []
        for hop in range(gz - 1, 0, -1):
            if came:
                (low,) = call(
                    backward_kernel, [plane], sweep, inner, inv, jac, *came, flops=2 * block_flops
                )
            came.append(lax.ppermute(low, "gz", [(hop, hop - 1)]))
        (update,) = call(
            update_kernel,
            [volume],
            sweep,
            inner,
            inv,
            jac,
            *came,
            flops=2 * block_flops,
            out_hbm=(0,),
            scratch=[pltpu.VMEM(volume[0], F32), pltpu.SemaphoreType.DMA((nz,))],
        )
        return jnp.transpose(update, (0, 2, 1, 3))

    placed = (
        P("gz", "gy", None, "gx"),
        P("gz", "gy", None, "gx"),
        P("gz", "gy", None, None, "gx"),
        P("gz", "gy", None, None, None, "gx"),
    )
    return jax.shard_map(
        body, mesh=mesh, in_specs=placed, out_specs=P("gz", "gy", None, "gx"), check_vma=False
    )
```

```python
import jax
import jax.numpy as jnp
from jax import lax
from jax.experimental import pallas as pl
from jax.experimental.pallas import tpu as pltpu
from jax.sharding import PartitionSpec as P

VARS = 6
LANES = 128
F32 = jnp.float32
WHOLE = pl.BlockSpec(memory_space=pltpu.VMEM)


def call(body, outs, *args, cost, limit=16 << 20, scratch=(), in_hbm=(), out_hbm=(), aliases={}):
    far = pl.BlockSpec(memory_space=pl.ANY)
    shapes = [
        jax.ShapeDtypeStruct(o[0], o[1]) if i in out_hbm else pltpu.VMEM(o[0], o[1])
        for i, o in enumerate(outs)
    ]
    return pl.pallas_call(
        body,
        out_shape=shapes,
        in_specs=[far if i in in_hbm else WHOLE for i in range(len(args))],
        out_specs=[far if i in out_hbm else WHOLE for i in range(len(outs))],
        scratch_shapes=scratch,
        input_output_aliases=aliases,
        cost_estimate=pl.CostEstimate(flops=0, bytes_accessed=cost, transcendentals=0),
        compiler_params=pltpu.CompilerParams(vmem_limit_bytes=limit),
    )(*[
        pltpu.with_memory_space_constraint(a, pltpu.HBM if i in in_hbm else pltpu.VMEM)
        for i, a in enumerate(args)
    ])


def lane_iota(rows):
    return lax.broadcasted_iota(jnp.int32, (rows, LANES), 1)


def row_iota(rows):
    return lax.broadcasted_iota(jnp.int32, (rows, LANES), 0)


def dot6(blocks, values):
    terms = [b.astype(F32) * v for b, v in zip(blocks, values)]
    return (terms[0] + terms[1]) + (terms[2] + terms[3]) + (terms[4] + terms[5])


def block(ref, *index, at):
    return lambda r, c: ref[(*index, r, c, slice(None), at)]


def apply_block(get, values):
    return [dot6([get(r, c) for c in range(VARS)], values) for r in range(VARS)]


def write_faces(value, x_face, y_face, z_count):
    y_count = value.shape[2]
    x_count = value.shape[3]
    lane = lane_iota(y_count)
    for side, start, source_lane in ((0, 0, 0), (1, x_count - LANES, LANES - 1)):
        for group in range(x_face.shape[1]):
            held = jnp.zeros((y_count, LANES), F32)
            for slot in range(min(LANES, z_count * VARS - group * LANES)):
                z, var = divmod(group * LANES + slot, VARS)
                tile = value[z, var, :, start : start + LANES]
                moved = pltpu.roll(tile, (slot - source_lane) % LANES, 1)
                held = jnp.where(lane == slot, moved, held)
            x_face[side, group] = held
    if y_face.shape[0] == 1:
        first = lax.axis_index("gy") == 0
        for z in range(z_count):
            for var in range(VARS):
                low = value[z, var, 0:1, :]
                high = value[z, var, y_count - 1 : y_count, :]
                y_face[0, z, var : var + 1, :] = jnp.where(first, high, low)
    else:
        for z in range(z_count):
            for var in range(VARS):
                y_face[0, z, var : var + 1, :] = value[z, var, 0:1, :]
                y_face[1, z, var : var + 1, :] = value[z, var, y_count - 1 : y_count, :]


def halo_reader(x_all, y_rows, gx, gy):
    me_x = lax.axis_index("gx")

    def column(there, side, to_lane):
        exists = (there >= 0) & (there < gx)
        device = jnp.clip(there, 0, gx - 1)

        def read(z, var):
            j = z * VARS + var
            face = x_all[device, side, j // LANES]
            moved = pltpu.roll(face, (to_lane + LANES - j % LANES) % LANES, 1)
            return jnp.where(exists, moved, jnp.zeros_like(moved))

        return read

    def row(which):
        def read(z, var, at):
            if len(y_rows) > 1:
                return y_rows[which][z, var : var + 1, at]
            here = y_rows[0][z, var : var + 1, at]
            return jnp.where(lax.axis_index("gy") == 1 - which, here, jnp.zeros_like(here))

        return read

    return column(me_x - 1, 1, 0), column(me_x + 1, 0, LANES - 1), row(0), row(1)


def neighbours(value, z, tile, tiles, halo):
    y_count = value.shape[2]
    lane = lane_iota(y_count)
    row = row_iota(y_count)
    at = slice(tile * LANES, (tile + 1) * LANES)
    result = ([], [], [], [])
    for var in range(VARS):
        here = value[z, var, :, at]
        if tile > 0:
            before = pltpu.roll(value[z, var, :, at.start - LANES : at.start], 1, 1)
        else:
            before = halo[0](z, var)
        if tile < tiles - 1:
            after = pltpu.roll(value[z, var, :, at.stop : at.stop + LANES], LANES - 1, 1)
        else:
            after = halo[1](z, var)
        result[0].append(jnp.where(lane == 0, before, pltpu.roll(here, 1, 1)))
        result[1].append(jnp.where(lane == LANES - 1, after, pltpu.roll(here, LANES - 1, 1)))
        result[2].append(jnp.where(row == 0, halo[2](z, var, at), pltpu.roll(here, 1, 0)))
        result[3].append(
            jnp.where(row == y_count - 1, halo[3](z, var, at), pltpu.roll(here, y_count - 1, 0))
        )
    return result


def inplane(jacobians, value, z, tile, tiles, halo):
    at = slice(tile * LANES, (tile + 1) * LANES)
    total = None
    for n, values in enumerate(neighbours(value, z, tile, tiles, halo)):
        part = apply_block(block(jacobians, z, n, at=at), values)
        total = part if total is None else [a + b for a, b in zip(total, part)]
    return total


def planes_of(ref, z, at):
    return [ref[z, var, :, at] for var in range(VARS)]


def solution(mesh):
    gz, gx, gy = (mesh.shape[a] for a in ("gz", "gx", "gy"))
    short = gz == 4

    def body(right_side, previous, diag_inverse, jacobians):
        rhs = jnp.transpose(right_side, (0, 2, 1, 3))
        prev = jnp.transpose(previous, (0, 2, 1, 3))
        inv = jnp.transpose(diag_inverse, (0, 2, 3, 1, 4))
        jac = jnp.transpose(jacobians, (0, 2, 3, 4, 1, 5))
        nz, _, ny, nx = rhs.shape
        tiles = nx // LANES
        assert nx % LANES == 0
        spans = [slice(t * LANES, (t + 1) * LANES) for t in range(tiles)]
        plane = (VARS, ny, nx)
        volume = (nz, VARS, ny, nx)
        x_face = ((2, -(-nz * VARS // LANES), ny, LANES), F32)
        y_face = ((1 if gy == 2 else 2, nz, VARS, nx), F32)
        plane, volume = (plane, F32), (volume, F32)
        cells = nz * ny * nx
        unit = 40 * cells

        def exchange(x_face, y_face):
            if gy == 2:
                rows = [lax.ppermute(y_face[0], "gy", [(0, 1), (1, 0)])]
            else:
                up = [(i, i + 1) for i in range(gy - 1)]
                rows = [
                    lax.ppermute(y_face[1], "gy", up),
                    lax.ppermute(y_face[0], "gy", [(j, i) for i, j in up]),
                ]
            return lax.all_gather(x_face, "gx"), *rows

        def faces_kernel(prev_hbm, *rest):
            prev_ref, x_face, y_face, sem = rest[-4:]
            copy = pltpu.make_async_copy(prev_hbm, prev_ref, sem)
            copy.start()
            copy.wait()
            write_faces(prev_ref, x_face, y_face, nz)

        def forward_plane(source, inv_ref, jac_ref, z, at, earlier):
            lagged = apply_block(block(jac_ref, z, 4, at=at), earlier)
            return apply_block(block(inv_ref, z, at=at), [a - b for a, b in zip(source, lagged)])

        def first_kernel(rhs_hbm, inv_hbm, jac_hbm, prev_ref, x_all, *rest):
            y_rows, (source_ref, top_ref, inv_ref, jac_ref, rhs_ref, sems) = rest[:-6], rest[-6:]
            halo = halo_reader(x_all, y_rows, gx, gy)

            def copies(z):
                pairs = ((jac_hbm, jac_ref), (rhs_hbm, rhs_ref), (inv_hbm, inv_ref))
                return [
                    pltpu.make_async_copy(far.at[z], near.at[z], sems.at[i, z])
                    for i, (far, near) in enumerate(pairs)
                ]

            for z in range(nz):
                for copy in copies(z):
                    copy.start()

            def step(z, earlier):
                for copy in copies(z):
                    copy.wait()
                results = []
                for tile, at in enumerate(spans):
                    lagged = inplane(jac_ref, prev_ref, z, tile, tiles, halo)
                    source = [a - b for a, b in zip(planes_of(rhs_ref, z, at), lagged)]
                    for var in range(VARS):
                        source_ref[z, var, :, at] = source[var]
                    result = forward_plane(source, inv_ref, jac_ref, z, at, earlier[tile])
                    results.append(tuple(result))
                return tuple(results)

            zero = tuple(jnp.zeros((ny, LANES), F32) for _ in range(VARS))
            top = lax.fori_loop(0, nz, step, (zero,) * tiles)
            for tile, at in enumerate(spans):
                for var in range(VARS):
                    top_ref[var, :, at] = top[tile][var]

        def incoming(refs, at):
            total = [refs[0][var, :, at] for var in range(VARS)]
            for ref in refs[1:]:
                total = [a + ref[var, :, at] for var, a in enumerate(total)]
            return tuple(total)

        def transfer(matrix_ref, inv_ref, jac_at, wait):
            half = VARS // 2

            def plane(z, at, group, vectors):
                couple, inverse = jac_at(z), block(inv_ref, z, at=at)
                middle = [[] for _ in group]
                for r in range(VARS):
                    row = [couple(r, c, at).astype(F32) for c in range(VARS)]
                    for i in range(len(group)):
                        middle[i].append(row[group[i]] if vectors is None else dot6(row, vectors[i]))
                for r in range(VARS):
                    row = [inverse(r, c).astype(F32) for c in range(VARS)]
                    for i, c in enumerate(group):
                        matrix_ref[r, c, :, at] = -dot6(row, middle[i])

            groups = [range(g * half, (g + 1) * half) for g in range(VARS // half)]

            def step(i, carry):
                z = wait(i)
                for at in spans:
                    for group in groups:
                        vectors = [[matrix_ref[r, c, :, at] for r in range(VARS)] for c in group]
                        plane(z, at, group, vectors)
                return carry

            z = wait(0)
            for at in spans:
                for group in groups:
                    plane(z, at, group, None)
            lax.fori_loop(1, nz, step, 0)

        def only_on(device, work, matrix_ref):
            here = lax.axis_index("gz") == device
            pl.when(here)(work)

            @pl.when(jnp.logical_not(here))
            def _():
                matrix_ref[...] = jnp.zeros(matrix_ref.shape, F32)

        def up_matrix_kernel(inv_hbm, jac_hbm, matrix_ref, inv_ref, jac_ref, sems):
            def copies(z):
                return [
                    pltpu.make_async_copy(inv_hbm.at[z], inv_ref.at[z], sems.at[0, z]),
                    pltpu.make_async_copy(jac_hbm.at[z, 4], jac_ref.at[z], sems.at[1, z]),
                ]

            def wait(z):
                for copy in copies(z):
                    copy.wait()
                return z

            def work():
                for z in range(nz):
                    for copy in copies(z):
                        copy.start()
                transfer(matrix_ref, inv_ref, lambda z: lambda r, c, at: jac_ref[z, r, c, :, at], wait)

            only_on(2, work, matrix_ref)

        def down_matrix_kernel(inv_ref, jac_ref, matrix_ref):
            def work():
                def couple(z):
                    return lambda r, c, at: jac_ref[z, 5, r, c, :, at]

                transfer(matrix_ref, inv_ref, couple, lambda i: nz - 1 - i)

            only_on(1, work, matrix_ref)

        def apply_matrix(matrix_ref, vector, at):
            return apply_block(block(matrix_ref, at=at), vector)

        def arrived(parts, at):
            *plain, matrix_ref, vector_ref = parts
            total = apply_matrix(matrix_ref, [vector_ref[var, :, at] for var in range(VARS)], at)
            for ref in plain:
                total = [a + ref[var, :, at] for var, a in enumerate(total)]
            return tuple(total)

        def forward_mid_kernel(low_ref, came_ref, after_ref, source_ref, inv_ref, jac_ref, _, top_ref):
            top_ref[...] = low_ref[...]

            @pl.when(lax.axis_index("gz") == 1)
            def _():
                def step(z, earlier):
                    return tuple(
                        tuple(
                            forward_plane(
                                planes_of(source_ref, z, at), inv_ref, jac_ref, z, at, earlier[tile]
                            )
                        )
                        for tile, at in enumerate(spans)
                    )

                start = tuple(incoming([came_ref], at) for at in spans)
                top = lax.fori_loop(0, nz, step, start)
                for tile, at in enumerate(spans):
                    for var in range(VARS):
                        top_ref[var, :, at] = top[tile][var]

        def backward_mid_kernel(high_ref, came_ref, sweep_ref, inner_ref, inv_ref, jac_ref, low_ref):
            low_ref[...] = high_ref[...]

            @pl.when(lax.axis_index("gz") == 2)
            def _():
                def step(i, later):
                    z = nz - 1 - i
                    return tuple(
                        tuple(
                            backward_plane(
                                planes_of(sweep_ref, z, at),
                                planes_of(inner_ref, z, at),
                                inv_ref,
                                jac_ref,
                                z,
                                at,
                                later[tile],
                            )
                        )
                        for tile, at in enumerate(spans)
                    )

                start = tuple(incoming([came_ref], at) for at in spans)
                low = lax.fori_loop(0, nz, step, start)
                for tile, at in enumerate(spans):
                    for var in range(VARS):
                        low_ref[var, :, at] = low[tile][var]

        def forward_kernel(source_ref, inv_ref, jac_ref, *rest):
            came, top_ref = rest[:-1], rest[-1]
            for at in spans:

                def step(z, earlier, at=at):
                    source = planes_of(source_ref, z, at)
                    return tuple(forward_plane(source, inv_ref, jac_ref, z, at, earlier))

                top = lax.fori_loop(0, nz, step, incoming(came, at))
                for var in range(VARS):
                    top_ref[var, :, at] = top[var]

        def forward_last_kernel(source_ref, prev_ref, inv_ref, jac_ref, *rest):
            if short:
                came, (sweep_ref, change_ref, x_face, y_face) = rest[:4], rest[5:9]
            else:
                came, (sweep_ref, change_ref, x_face, y_face) = rest[:-4], rest[-4:]
            for at in spans:

                def step(z, earlier, at=at):
                    source = planes_of(source_ref, z, at)
                    result = forward_plane(source, inv_ref, jac_ref, z, at, earlier)
                    before = planes_of(prev_ref, z, at)
                    for var in range(VARS):
                        sweep_ref[z, var, :, at] = result[var]
                        change_ref[z, var, :, at] = result[var] - before[var]
                    return tuple(result)

                start = arrived(came, at) if short else incoming(came, at)
                lax.fori_loop(0, nz, step, start)
            write_faces(change_ref, x_face, y_face, nz)

        def backward_plane(sweep, inner, inv_ref, jac_ref, z, at, later):
            change = apply_block(block(jac_ref, z, 5, at=at), later)
            change = apply_block(block(inv_ref, z, at=at), [a + b for a, b in zip(change, inner)])
            return [a - b for a, b in zip(sweep, change)]

        def turn_kernel(sweep_ref, change_ref, inv_ref, jac_ref, x_all, *rest):
            y_rows, (inner_ref, low_ref) = rest[:-2], rest[-2:]
            halo = halo_reader(x_all, y_rows, gx, gy)
            for tile, at in enumerate(spans):

                def step(i, later, tile=tile, at=at):
                    z = nz - 1 - i
                    inner = inplane(jac_ref, change_ref, z, tile, tiles, halo)
                    for var in range(VARS):
                        inner_ref[z, var, :, at] = inner[var]
                    sweep = planes_of(sweep_ref, z, at)
                    return tuple(backward_plane(sweep, inner, inv_ref, jac_ref, z, at, later))

                zero = tuple(jnp.zeros((ny, LANES), F32) for _ in range(VARS))
                low = lax.fori_loop(0, nz, step, zero)
                for var in range(VARS):
                    low_ref[var, :, at] = low[var]

        def backward_kernel(sweep_ref, inner_ref, inv_ref, jac_ref, *rest):
            came, low_ref = rest[:-1], rest[-1]
            for at in spans:

                def step(i, later, at=at):
                    z = nz - 1 - i
                    sweep, inner = planes_of(sweep_ref, z, at), planes_of(inner_ref, z, at)
                    return tuple(backward_plane(sweep, inner, inv_ref, jac_ref, z, at, later))

                low = lax.fori_loop(0, nz, step, incoming(came, at))
                for var in range(VARS):
                    low_ref[var, :, at] = low[var]

        def update_kernel(sweep_ref, inner_ref, inv_ref, jac_ref, *rest):
            came, (out_hbm, held, sems) = rest[:-3], rest[-3:]

            def out_copy(z):
                return pltpu.make_async_copy(held.at[z], out_hbm.at[z], sems.at[z])

            def step(i, later):
                z = nz - 1 - i
                results = []
                for tile, at in enumerate(spans):
                    sweep, inner = planes_of(sweep_ref, z, at), planes_of(inner_ref, z, at)
                    result = backward_plane(sweep, inner, inv_ref, jac_ref, z, at, later[tile])
                    for var in range(VARS):
                        held[z, var, :, at] = result[var]
                    results.append(tuple(result))
                out_copy(z).start()
                return tuple(results)

            entered = arrived if short else incoming
            lax.fori_loop(0, nz, step, tuple(entered(came, at) for at in spans))
            for z in range(nz):
                out_copy(z).wait()

        if short:
            matrix_shape = ((VARS, VARS, ny, nx), F32)
            (up_matrix,) = call(
                up_matrix_kernel,
                [matrix_shape],
                inv,
                jac,
                cost=12 * unit,
                in_hbm=(0, 1),
                scratch=[
                    pltpu.VMEM(inv.shape, inv.dtype),
                    pltpu.VMEM(inv.shape, jac.dtype),
                    pltpu.SemaphoreType.DMA((2, nz)),
                ],
            )
            up_there = lax.ppermute(up_matrix, "gz", [(gz - 2, gz - 1)])
        prev, *faces = call(
            faces_kernel,
            [volume, x_face, y_face],
            prev,
            *([up_matrix] if short else []),
            cost=3 * unit,
            in_hbm=(0,),
            scratch=[pltpu.SemaphoreType.DMA],
        )
        halo = exchange(*faces)
        source, top, inv, jac = call(
            first_kernel,
            [volume, plane, (inv.shape, inv.dtype), (jac.shape, jac.dtype)],
            rhs,
            inv,
            jac,
            prev,
            *halo,
            cost=18 * unit,
            in_hbm=(0, 1, 2),
            scratch=[pltpu.VMEM(rhs.shape, F32), pltpu.SemaphoreType.DMA((3, nz))],
        )
        if short:
            first = lax.ppermute(top, "gz", [(0, 1)])
            (down_matrix,) = call(down_matrix_kernel, [matrix_shape], inv, jac, cost=12 * unit)
            (top,) = call(
                forward_mid_kernel,
                [plane],
                top,
                first,
                up_there,
                source,
                inv,
                jac,
                down_matrix,
                cost=3 * unit,
            )
            far = lax.ppermute(top, "gz", [(1, 3)])
            near = lax.ppermute(top, "gz", [(1, 2), (2, 3)])
            came = [first, near, up_there, far]
            extra = [down_matrix]
        else:
            extra = []
            came = []
            for hop in range(gz - 1):
                if hop:
                    (top,) = call(
                        forward_kernel, [plane], source, inv, jac, *came, cost=3 * unit)
                came.append(lax.ppermute(top, "gz", [(hop, hop + 1)]))
        sweep, change, x_side, y_side, *extra = call(
            forward_last_kernel,
            [volume, volume, x_face, y_face] + [matrix_shape] * len(extra),
            source,
            prev,
            inv,
            jac,
            *came,
            *extra,
            cost=4 * unit,
            aliases={4 + len(came): 4} if short else {},
        )
        if short:
            down_there = lax.ppermute(extra[0], "gz", [(1, 0)])
        halo = exchange(x_side, y_side)
        inner, low = call(
            turn_kernel, [volume, plane], sweep, change, inv, jac, *halo, cost=11 * unit)
        if short:
            first = lax.ppermute(low, "gz", [(3, 2)])
            (low,) = call(
                backward_mid_kernel, [plane], low, first, sweep, inner, inv, jac, cost=3 * unit
            )
            far = lax.ppermute(low, "gz", [(2, 0)])
            near = lax.ppermute(low, "gz", [(2, 1), (1, 0)])
            came = [first, near, down_there, far]
        else:
            came = []
            for hop in range(gz - 1, 0, -1):
                if came:
                    (low,) = call(
                        backward_kernel,
                        [plane],
                        sweep,
                        inner,
                        inv,
                        jac,
                        *came,
                        cost=3 * unit,
                    )
                came.append(lax.ppermute(low, "gz", [(hop, hop - 1)]))
        (update,) = call(
            update_kernel,
            [volume],
            sweep,
            inner,
            inv,
            jac,
            *came,
            cost=5 * unit,
            out_hbm=(0,),
            scratch=[pltpu.VMEM(volume[0], F32), pltpu.SemaphoreType.DMA((nz,))],
        )
        return jnp.transpose(update, (0, 2, 1, 3))

    placed = (
        P("gz", "gy", None, "gx"),
        P("gz", "gy", None, "gx"),
        P("gz", "gy", None, None, "gx"),
        P("gz", "gy", None, None, None, "gx"),
    )
    return jax.shard_map(
        body, mesh=mesh, in_specs=placed, out_specs=P("gz", "gy", None, "gx"), check_vma=False
    )
```

```python
import functools

import jax
import jax.numpy as jnp
from jax import lax
from jax.experimental import pallas as pl
from jax.experimental.pallas import tpu as pltpu
from jax.sharding import PartitionSpec as P

VARS = 6
LANES = 128
F32 = jnp.float32
WHOLE = pl.BlockSpec(memory_space=pltpu.VMEM)


def call(body, outs, *args, cost, limit=16 << 20, scratch=(), in_hbm=(), out_hbm=(), aliases={}):
    far = pl.BlockSpec(memory_space=pl.ANY)
    shapes = [
        jax.ShapeDtypeStruct(o[0], o[1]) if i in out_hbm else pltpu.VMEM(o[0], o[1])
        for i, o in enumerate(outs)
    ]
    return pl.pallas_call(
        body,
        out_shape=shapes,
        in_specs=[far if i in in_hbm else WHOLE for i in range(len(args))],
        out_specs=[far if i in out_hbm else WHOLE for i in range(len(outs))],
        scratch_shapes=scratch,
        input_output_aliases=aliases,
        cost_estimate=pl.CostEstimate(flops=0, bytes_accessed=cost, transcendentals=0),
        compiler_params=pltpu.CompilerParams(vmem_limit_bytes=limit),
    )(*[
        pltpu.with_memory_space_constraint(a, pltpu.HBM if i in in_hbm else pltpu.VMEM)
        for i, a in enumerate(args)
    ])


def lane_iota(rows):
    return lax.broadcasted_iota(jnp.int32, (rows, LANES), 1)


def row_iota(rows):
    return lax.broadcasted_iota(jnp.int32, (rows, LANES), 0)


def dot6(blocks, values):
    terms = [b.astype(F32) * v for b, v in zip(blocks, values)]
    return (terms[0] + terms[1]) + (terms[2] + terms[3]) + (terms[4] + terms[5])


def block(ref, *index, at):
    return lambda r, c: ref[(*index, r, c, slice(None), at)]


def apply_block(get, values):
    return [dot6([get(r, c) for c in range(VARS)], values) for r in range(VARS)]


def write_faces(value, x_face, y_face, z_count):
    y_count = value.shape[2]
    x_count = value.shape[3]
    lane = lane_iota(y_count)
    for side, start, source_lane in ((0, 0, 0), (1, x_count - LANES, LANES - 1)):
        for group in range(x_face.shape[1]):
            held = jnp.zeros((y_count, LANES), F32)
            for slot in range(min(LANES, z_count * VARS - group * LANES)):
                z, var = divmod(group * LANES + slot, VARS)
                tile = value[z, var, :, start : start + LANES]
                moved = pltpu.roll(tile, (slot - source_lane) % LANES, 1)
                held = jnp.where(lane == slot, moved, held)
            x_face[side, group] = held
    if y_face.shape[0] == 1:
        first = lax.axis_index("gy") == 0
        for z in range(z_count):
            for var in range(VARS):
                low = value[z, var, 0:1, :]
                high = value[z, var, y_count - 1 : y_count, :]
                y_face[0, z, var : var + 1, :] = jnp.where(first, high, low)
    else:
        for z in range(z_count):
            for var in range(VARS):
                y_face[0, z, var : var + 1, :] = value[z, var, 0:1, :]
                y_face[1, z, var : var + 1, :] = value[z, var, y_count - 1 : y_count, :]


def halo_reader(x_all, y_rows, gx, gy):
    me_x = lax.axis_index("gx")

    def column(there, side, to_lane):
        exists = (there >= 0) & (there < gx)
        device = jnp.clip(there, 0, gx - 1)

        def read(z, var):
            j = z * VARS + var
            face = x_all[device, side, j // LANES]
            moved = pltpu.roll(face, (to_lane + LANES - j % LANES) % LANES, 1)
            return jnp.where(exists, moved, jnp.zeros_like(moved))

        return read

    def row(which):
        def read(z, var, at):
            if len(y_rows) > 1:
                return y_rows[which][z, var : var + 1, at]
            here = y_rows[0][z, var : var + 1, at]
            return jnp.where(lax.axis_index("gy") == 1 - which, here, jnp.zeros_like(here))

        return read

    return column(me_x - 1, 1, 0), column(me_x + 1, 0, LANES - 1), row(0), row(1)


def neighbours(value, z, tile, tiles, halo):
    y_count = value.shape[2]
    lane = lane_iota(y_count)
    row = row_iota(y_count)
    at = slice(tile * LANES, (tile + 1) * LANES)
    result = ([], [], [], [])
    for var in range(VARS):
        here = value[z, var, :, at]
        if tile > 0:
            before = pltpu.roll(value[z, var, :, at.start - LANES : at.start], 1, 1)
        else:
            before = halo[0](z, var)
        if tile < tiles - 1:
            after = pltpu.roll(value[z, var, :, at.stop : at.stop + LANES], LANES - 1, 1)
        else:
            after = halo[1](z, var)
        result[0].append(jnp.where(lane == 0, before, pltpu.roll(here, 1, 1)))
        result[1].append(jnp.where(lane == LANES - 1, after, pltpu.roll(here, LANES - 1, 1)))
        result[2].append(jnp.where(row == 0, halo[2](z, var, at), pltpu.roll(here, 1, 0)))
        result[3].append(
            jnp.where(row == y_count - 1, halo[3](z, var, at), pltpu.roll(here, y_count - 1, 0))
        )
    return result


def inplane(jacobians, value, z, tile, tiles, halo):
    at = slice(tile * LANES, (tile + 1) * LANES)
    total = None
    for n, values in enumerate(neighbours(value, z, tile, tiles, halo)):
        part = apply_block(block(jacobians, z, n, at=at), values)
        total = part if total is None else [a + b for a, b in zip(total, part)]
    return total


def planes_of(ref, z, at):
    return [ref[z, var, :, at] for var in range(VARS)]


def solution(mesh):
    gz, gx, gy = (mesh.shape[a] for a in ("gz", "gx", "gy"))
    short = gz == 4

    def body(right_side, previous, diag_inverse, jacobians):
        rhs = jnp.transpose(right_side, (0, 2, 1, 3))
        prev = jnp.transpose(previous, (0, 2, 1, 3))
        inv = jnp.transpose(diag_inverse, (0, 2, 3, 1, 4))
        jac = jnp.transpose(jacobians, (0, 2, 3, 4, 1, 5))
        nz, _, ny, nx = rhs.shape
        tiles = nx // LANES
        assert nx % LANES == 0
        spans = [slice(t * LANES, (t + 1) * LANES) for t in range(tiles)]
        plane = ((VARS, ny, nx), F32)
        volume = ((nz, VARS, ny, nx), F32)
        x_face = ((2, -(-nz * VARS // LANES), ny, LANES), F32)
        y_face = ((1 if gy == 2 else 2, nz, VARS, nx), F32)
        matrix = ((VARS, VARS, ny, nx), F32)
        blocks = ((nz, VARS, VARS, ny, nx), jac.dtype)
        side_blocks = ((nz, 4, VARS, VARS, ny, nx), jac.dtype)
        unit = 40 * nz * ny * nx

        def exchange(x_face, y_face):
            if gy == 2:
                rows = [lax.ppermute(y_face[0], "gy", [(0, 1), (1, 0)])]
            else:
                up = [(i, i + 1) for i in range(gy - 1)]
                rows = [
                    lax.ppermute(y_face[1], "gy", up),
                    lax.ppermute(y_face[0], "gy", [(j, i) for i, j in up]),
                ]
            return lax.all_gather(x_face, "gx"), *rows


        def forward_plane(source, inv_ref, low_jac, z, at, earlier):
            lagged = apply_block(block(low_jac, z, at=at), earlier)
            return apply_block(block(inv_ref, z, at=at), [a - b for a, b in zip(source, lagged)])

        def backward_plane(sweep, inner, inv_ref, high_jac, z, at, later):
            change = apply_block(block(high_jac, z, at=at), later)
            change = apply_block(block(inv_ref, z, at=at), [a + b for a, b in zip(change, inner)])
            return [a - b for a, b in zip(sweep, change)]

        def put(ref, values, at):
            for var in range(VARS):
                ref[var, :, at] = values[var]

        def incoming(refs, at):
            total = [refs[0][var, :, at] for var in range(VARS)]
            for ref in refs[1:]:
                total = [a + ref[var, :, at] for var, a in enumerate(total)]
            return tuple(total)

        def apply_matrix(matrix_ref, vector, at):
            return apply_block(block(matrix_ref, at=at), vector)

        def arrived(plain, matrix_ref, vector_ref, at):
            total = apply_matrix(matrix_ref, [vector_ref[var, :, at] for var in range(VARS)], at)
            for ref in plain:
                total = [a + ref[var, :, at] for var, a in enumerate(total)]
            return tuple(total)

        def forward_sweep(source_ref, inv_ref, low_jac, starts, keep=None):
            def step(z, earlier):
                results = []
                for tile, at in enumerate(spans):
                    source = planes_of(source_ref, z, at)
                    result = forward_plane(source, inv_ref, low_jac, z, at, earlier[tile])
                    if keep is not None:
                        keep(z, at, result)
                    results.append(tuple(result))
                return tuple(results)

            return lax.fori_loop(0, nz, step, starts)

        def backward_sweep(sweep_ref, inner_ref, inv_ref, high_jac, starts, keep=None):
            def step(i, later):
                z = nz - 1 - i
                results = []
                for tile, at in enumerate(spans):
                    sweep, inner = planes_of(sweep_ref, z, at), planes_of(inner_ref, z, at)
                    result = backward_plane(sweep, inner, inv_ref, high_jac, z, at, later[tile])
                    if keep is not None:
                        keep(z, tile, at, result)
                    results.append(tuple(result))
                return tuple(results)

            return lax.fori_loop(0, nz, step, starts)

        def transfer(matrix_ref, inv_ref, couple_ref, wait):
            half = VARS // 2
            groups = [range(g * half, (g + 1) * half) for g in range(VARS // half)]

            def plane_step(z, at, group, vectors):
                couple, inverse = block(couple_ref, z, at=at), block(inv_ref, z, at=at)
                middle = [[] for _ in group]
                for r in range(VARS):
                    row = [couple(r, c).astype(F32) for c in range(VARS)]
                    for i in range(len(group)):
                        middle[i].append(row[group[i]] if vectors is None else dot6(row, vectors[i]))
                for r in range(VARS):
                    row = [inverse(r, c).astype(F32) for c in range(VARS)]
                    for i, c in enumerate(group):
                        matrix_ref[r, c, :, at] = -dot6(row, middle[i])

            def step(i, carry):
                z = wait(i)
                for at in spans:
                    for group in groups:
                        vectors = [[matrix_ref[r, c, :, at] for r in range(VARS)] for c in group]
                        plane_step(z, at, group, vectors)
                return carry

            z = wait(0)
            for at in spans:
                for group in groups:
                    plane_step(z, at, group, None)
            lax.fori_loop(1, nz, step, 0)


        def open_kernel(prev_hbm, inv_hbm, jac_hbm, *rest):
            prev_ref, inv_ref, low_jac, x_side, y_side, *matrices, sem, sems = rest

            def copies(z):
                return [
                    pltpu.make_async_copy(inv_hbm.at[z], inv_ref.at[z], sems.at[0, z]),
                    pltpu.make_async_copy(jac_hbm.at[z, 4], low_jac.at[z], sems.at[1, z]),
                ]

            def wait(z):
                for copy in copies(z):
                    copy.wait()
                return z

            first_copy = pltpu.make_async_copy(prev_hbm, prev_ref, sem)
            first_copy.start()
            for z in range(nz):
                for copy in copies(z):
                    copy.start()
            first_copy.wait()
            write_faces(prev_ref, x_side, y_side, nz)
            if not matrices:
                for z in range(nz):
                    wait(z)
                return
            here = lax.axis_index("gz") == 2

            @pl.when(here)
            def _():
                transfer(matrices[0], inv_ref, low_jac, wait)

            @pl.when(jnp.logical_not(here))
            def _():
                matrices[0][...] = jnp.zeros(matrix[0], F32)
                for z in range(nz):
                    wait(z)

        def first_kernel(rhs_hbm, jac_hbm, prev_ref, inv_ref, low_jac, x_all, *rest):
            y_rows, (source_ref, top_ref, sides, high_jac, rhs_ref, sems) = rest[:-6], rest[-6:]
            halo = halo_reader(x_all, y_rows, gx, gy)

            def copies(z):
                return [
                    pltpu.make_async_copy(jac_hbm.at[z, 0:4], sides.at[z], sems.at[0, z]),
                    pltpu.make_async_copy(rhs_hbm.at[z], rhs_ref.at[z], sems.at[1, z]),
                ]

            def high_copy(z):
                return pltpu.make_async_copy(jac_hbm.at[z, 5], high_jac.at[z], sems.at[2, z])

            for z in range(nz):
                for copy in copies(z):
                    copy.start()
            for z in range(nz):
                high_copy(z).start()

            def step(z, earlier):
                for copy in copies(z):
                    copy.wait()
                results = []
                for tile, at in enumerate(spans):
                    lagged = inplane(sides, prev_ref, z, tile, tiles, halo)
                    source = [a - b for a, b in zip(planes_of(rhs_ref, z, at), lagged)]
                    for var in range(VARS):
                        source_ref[z, var, :, at] = source[var]
                    results.append(tuple(forward_plane(source, inv_ref, low_jac, z, at, earlier[tile])))
                return tuple(results)

            zero = tuple(jnp.zeros((ny, LANES), F32) for _ in range(VARS))
            top = lax.fori_loop(0, nz, step, (zero,) * tiles)
            for tile, at in enumerate(spans):
                put(top_ref, top[tile], at)
            for z in range(nz):
                high_copy(z).wait()

        def forward_kernel(source_ref, inv_ref, low_jac, *rest):
            came, top_ref = rest[:-1], rest[-1]
            starts = tuple(incoming(came, at) for at in spans)
            top = forward_sweep(source_ref, inv_ref, low_jac, starts)
            for tile, at in enumerate(spans):
                put(top_ref, top[tile], at)

        def forward_mid_kernel(low_ref, came_ref, _, source_ref, inv_ref, low_jac, __, top_ref):
            top_ref[...] = low_ref[...]

            @pl.when(lax.axis_index("gz") == 1)
            def _():
                forward_kernel(source_ref, inv_ref, low_jac, came_ref, top_ref)

        def forward_last_kernel(source_ref, prev_ref, inv_ref, low_jac, *rest):
            if short:
                (first, near, matrix_ref, far), outs = rest[:4], rest[5:9]
                starts = tuple(arrived((first, near), matrix_ref, far, at) for at in spans)
            else:
                came, outs = rest[:-4], rest[-4:]
                starts = tuple(incoming(came, at) for at in spans)
            sweep_ref, change_ref, x_side, y_side = outs

            def keep(z, at, result):
                before = planes_of(prev_ref, z, at)
                for var in range(VARS):
                    sweep_ref[z, var, :, at] = result[var]
                    change_ref[z, var, :, at] = result[var] - before[var]

            forward_sweep(source_ref, inv_ref, low_jac, starts, keep)
            write_faces(change_ref, x_side, y_side, nz)

        def turn_kernel(sweep_ref, change_ref, inv_ref, sides, high_jac, x_all, *rest):
            y_rows, (inner_ref, low_ref) = rest[:-2], rest[-2:]
            halo = halo_reader(x_all, y_rows, gx, gy)
            for tile, at in enumerate(spans):

                def step(i, later, tile=tile, at=at):
                    z = nz - 1 - i
                    inner = inplane(sides, change_ref, z, tile, tiles, halo)
                    for var in range(VARS):
                        inner_ref[z, var, :, at] = inner[var]
                    sweep = planes_of(sweep_ref, z, at)
                    return tuple(backward_plane(sweep, inner, inv_ref, high_jac, z, at, later))

                zero = tuple(jnp.zeros((ny, LANES), F32) for _ in range(VARS))
                put(low_ref, lax.fori_loop(0, nz, step, zero), at)

        def down_matrix_kernel(device, inv_ref, high_jac, matrix_ref):
            here = lax.axis_index("gz") == device

            @pl.when(here)
            def _():
                transfer(matrix_ref, inv_ref, high_jac, lambda i: nz - 1 - i)

            @pl.when(jnp.logical_not(here))
            def _():
                matrix_ref[...] = jnp.zeros(matrix[0], F32)

        def backward_kernel(sweep_ref, inner_ref, inv_ref, high_jac, *rest):
            came, low_ref = rest[:-1], rest[-1]
            starts = tuple(incoming(came, at) for at in spans)
            low = backward_sweep(sweep_ref, inner_ref, inv_ref, high_jac, starts)
            for tile, at in enumerate(spans):
                put(low_ref, low[tile], at)

        def backward_mid_kernel(own_ref, near, there_ref, far, matrix_ref, came_ref, low_ref):
            for at in spans:
                came = arrived((near,), there_ref, far, at)
                moved = apply_matrix(matrix_ref, came, at)
                put(came_ref, came, at)
                put(low_ref, [own_ref[var, :, at] + moved[var] for var in range(VARS)], at)

        def update_kernel(sweep_ref, inner_ref, inv_ref, high_jac, *rest):
            came, (out_hbm, held, sems) = rest[:-3], rest[-3:]

            def out_copy(z):
                return pltpu.make_async_copy(held.at[z], out_hbm.at[z], sems.at[z])

            def keep(z, tile, at, result):
                for var in range(VARS):
                    held[z, var, :, at] = result[var]
                if tile == tiles - 1:
                    out_copy(z).start()

            starts = tuple(incoming(came, at) for at in spans)
            backward_sweep(sweep_ref, inner_ref, inv_ref, high_jac, starts, keep)
            for z in range(nz):
                out_copy(z).wait()


        prev, inv, low_jac, x_side, y_side, *up_matrix = call(
            open_kernel,
            [volume, blocks, blocks, x_face, y_face] + [matrix] * (1 if short else 0),
            prev,
            inv,
            jac,
            cost=12 * unit,
            in_hbm=(0, 1, 2),
            scratch=[pltpu.SemaphoreType.DMA, pltpu.SemaphoreType.DMA((2, nz))],
        )
        if short:
            up_there = lax.ppermute(up_matrix[0], "gz", [(2, 3)])
        halo = exchange(x_side, y_side)
        source, top, sides, high_jac = call(
            first_kernel,
            [volume, plane, side_blocks, blocks],
            rhs,
            jac,
            prev,
            inv,
            low_jac,
            *halo,
            cost=14 * unit,
            in_hbm=(0, 1),
            scratch=[pltpu.VMEM(rhs.shape, F32), pltpu.SemaphoreType.DMA((3, nz))],
        )
        if short:
            first = lax.ppermute(top, "gz", [(0, 1)])
            (own_matrix,) = call(
                functools.partial(down_matrix_kernel, 1), [matrix], inv, high_jac, cost=12 * unit
            )
            (top,) = call(
                forward_mid_kernel,
                [plane],
                top,
                first,
                up_there,
                source,
                inv,
                low_jac,
                own_matrix,
                cost=3 * unit,
            )
            far = lax.ppermute(top, "gz", [(1, 3)])
            near = lax.ppermute(top, "gz", [(1, 2), (2, 3)])
            (down_matrix,) = call(
                functools.partial(down_matrix_kernel, 2), [matrix], inv, high_jac, cost=12 * unit
            )
            came = [first, near, up_there, far]
            extra = [down_matrix]
        else:
            came, extra = [], []
            for hop in range(gz - 1):
                if hop:
                    (top,) = call(
                        forward_kernel, [plane], source, inv, low_jac, *came, cost=3 * unit
                    )
                came.append(lax.ppermute(top, "gz", [(hop, hop + 1)]))
        sweep, change, x_side, y_side, *extra = call(
            forward_last_kernel,
            [volume, volume, x_face, y_face] + [matrix] * len(extra),
            source,
            prev,
            inv,
            low_jac,
            *came,
            *extra,
            cost=4 * unit,
            aliases={4 + len(came): 4} if short else {},
        )
        if short:
            down_there = lax.ppermute(extra[0], "gz", [(2, 1)])
        halo = exchange(x_side, y_side)
        inner, low = call(
            turn_kernel, [volume, plane], sweep, change, inv, sides, high_jac, *halo, cost=11 * unit
        )
        if short:
            far = lax.ppermute(low, "gz", [(3, 1)])
            near = lax.ppermute(low, "gz", [(3, 2), (2, 1)])
            entered, low = call(
                backward_mid_kernel,
                [plane, plane],
                low,
                near,
                down_there,
                far,
                own_matrix,
                cost=unit,
            )
            came = [entered, lax.ppermute(low, "gz", [(1, 0)])]
        else:
            came = []
            for hop in range(gz - 1, 0, -1):
                if came:
                    (low,) = call(
                        backward_kernel, [plane], sweep, inner, inv, high_jac, *came, cost=3 * unit
                    )
                came.append(lax.ppermute(low, "gz", [(hop, hop - 1)]))
        (update,) = call(
            update_kernel,
            [volume],
            sweep,
            inner,
            inv,
            high_jac,
            *came,
            cost=5 * unit,
            out_hbm=(0,),
            scratch=[pltpu.VMEM(volume[0], F32), pltpu.SemaphoreType.DMA((nz,))],
        )
        return jnp.transpose(update, (0, 2, 1, 3))

    placed = (
        P("gz", "gy", None, "gx"),
        P("gz", "gy", None, "gx"),
        P("gz", "gy", None, None, "gx"),
        P("gz", "gy", None, None, None, "gx"),
    )
    return jax.shard_map(
        body, mesh=mesh, in_specs=placed, out_specs=P("gz", "gy", None, "gx"), check_vma=False
    )
```

```python
import functools

import jax
import jax.numpy as jnp
from jax import lax
from jax.experimental import pallas as pl
from jax.experimental.pallas import tpu as pltpu
from jax.sharding import PartitionSpec as P

VARS = 6
LANES = 128
F32 = jnp.float32
WHOLE = pl.BlockSpec(memory_space=pltpu.VMEM)


def call(body, outs, *args, cost, limit=16 << 20, scratch=(), in_hbm=(), out_hbm=(), aliases={}):
    far = pl.BlockSpec(memory_space=pl.ANY)
    shapes = [
        jax.ShapeDtypeStruct(o[0], o[1]) if i in out_hbm else pltpu.VMEM(o[0], o[1])
        for i, o in enumerate(outs)
    ]
    return pl.pallas_call(
        body,
        out_shape=shapes,
        in_specs=[far if i in in_hbm else WHOLE for i in range(len(args))],
        out_specs=[far if i in out_hbm else WHOLE for i in range(len(outs))],
        scratch_shapes=scratch,
        input_output_aliases=aliases,
        cost_estimate=pl.CostEstimate(flops=0, bytes_accessed=cost, transcendentals=0),
        compiler_params=pltpu.CompilerParams(vmem_limit_bytes=limit),
    )(*[
        pltpu.with_memory_space_constraint(a, pltpu.HBM if i in in_hbm else pltpu.VMEM)
        for i, a in enumerate(args)
    ])


def lane_iota(rows):
    return lax.broadcasted_iota(jnp.int32, (rows, LANES), 1)


def row_iota(rows):
    return lax.broadcasted_iota(jnp.int32, (rows, LANES), 0)


def dot6(blocks, values):
    terms = [b.astype(F32) * v for b, v in zip(blocks, values)]
    return (terms[0] + terms[1]) + (terms[2] + terms[3]) + (terms[4] + terms[5])


def block(ref, *index, at):
    return lambda r, c: ref[(*index, r, c, slice(None), at)]


def apply_block(get, values):
    return [dot6([get(r, c) for c in range(VARS)], values) for r in range(VARS)]


def write_faces(value, x_face, y_face, z_count, slots):
    y_count = value.shape[2]
    x_count = value.shape[3]
    lane = lane_iota(y_count)
    for group in range(x_face.shape[1]):
        faces = []
        for start, source_lane in ((0, 0), (x_count - LANES, LANES - 1)):
            held = jnp.zeros((y_count, LANES), F32)
            for slot in range(min(LANES, z_count * VARS - group * LANES)):
                z, var = divmod(group * LANES + slot, VARS)
                tile = value[z, var, :, start : start + LANES]
                moved = pltpu.roll(tile, (slot - source_lane) % LANES, 1)
                held = jnp.where(lane == slot, moved, held)
            faces.append(held)
        if slots:
            for device in range(x_face.shape[0]):
                above = device > lax.axis_index("gx")
                x_face[device, group] = jnp.where(above, faces[1], faces[0])
        else:
            x_face[0, group], x_face[1, group] = faces
    if y_face.shape[0] == 1:
        first = lax.axis_index("gy") == 0
        for z in range(z_count):
            for var in range(VARS):
                low = value[z, var, 0:1, :]
                high = value[z, var, y_count - 1 : y_count, :]
                y_face[0, z, var : var + 1, :] = jnp.where(first, high, low)
    else:
        for z in range(z_count):
            for var in range(VARS):
                y_face[0, z, var : var + 1, :] = value[z, var, 0:1, :]
                y_face[1, z, var : var + 1, :] = value[z, var, y_count - 1 : y_count, :]


def halo_reader(x_all, y_rows, gx, gy, slots):
    me_x = lax.axis_index("gx")

    def column(there, side, to_lane):
        exists = (there >= 0) & (there < gx)
        device = jnp.clip(there, 0, gx - 1)

        def read(z, var):
            j = z * VARS + var
            face = x_all[(device, *side, j // LANES)]
            moved = pltpu.roll(face, (to_lane + LANES - j % LANES) % LANES, 1)
            return jnp.where(exists, moved, jnp.zeros_like(moved))

        return read

    def row(which):
        def read(z, var, at):
            if len(y_rows) > 1:
                return y_rows[which][z, var : var + 1, at]
            here = y_rows[0][z, var : var + 1, at]
            return jnp.where(lax.axis_index("gy") == 1 - which, here, jnp.zeros_like(here))

        return read

    sides = ((), ()) if slots else ((1,), (0,))
    before, after = column(me_x - 1, sides[0], 0), column(me_x + 1, sides[1], LANES - 1)
    return before, after, row(0), row(1)


def neighbours(value, z, tile, tiles, halo):
    y_count = value.shape[2]
    lane = lane_iota(y_count)
    row = row_iota(y_count)
    at = slice(tile * LANES, (tile + 1) * LANES)
    result = ([], [], [], [])
    for var in range(VARS):
        here = value[z, var, :, at]
        if tile > 0:
            before = pltpu.roll(value[z, var, :, at.start - LANES : at.start], 1, 1)
        else:
            before = halo[0](z, var)
        if tile < tiles - 1:
            after = pltpu.roll(value[z, var, :, at.stop : at.stop + LANES], LANES - 1, 1)
        else:
            after = halo[1](z, var)
        result[0].append(jnp.where(lane == 0, before, pltpu.roll(here, 1, 1)))
        result[1].append(jnp.where(lane == LANES - 1, after, pltpu.roll(here, LANES - 1, 1)))
        result[2].append(jnp.where(row == 0, halo[2](z, var, at), pltpu.roll(here, 1, 0)))
        result[3].append(
            jnp.where(row == y_count - 1, halo[3](z, var, at), pltpu.roll(here, y_count - 1, 0))
        )
    return result


def inplane(jacobians, value, z, tile, tiles, halo):
    at = slice(tile * LANES, (tile + 1) * LANES)
    total = None
    for n, values in enumerate(neighbours(value, z, tile, tiles, halo)):
        part = apply_block(block(jacobians, z, n, at=at), values)
        total = part if total is None else [a + b for a, b in zip(total, part)]
    return total


def planes_of(ref, z, at):
    return [ref[z, var, :, at] for var in range(VARS)]


def solution(mesh):
    gz, gx, gy = (mesh.shape[a] for a in ("gz", "gx", "gy"))
    short = gz == 4

    def body(right_side, previous, diag_inverse, jacobians):
        rhs = jnp.transpose(right_side, (0, 2, 1, 3))
        prev = jnp.transpose(previous, (0, 2, 1, 3))
        inv = jnp.transpose(diag_inverse, (0, 2, 3, 1, 4))
        jac = jnp.transpose(jacobians, (0, 2, 3, 4, 1, 5))
        nz, _, ny, nx = rhs.shape
        tiles = nx // LANES
        assert nx % LANES == 0
        spans = [slice(t * LANES, (t + 1) * LANES) for t in range(tiles)]
        plane = ((VARS, ny, nx), F32)
        volume = ((nz, VARS, ny, nx), F32)
        x_groups = -(-nz * VARS // LANES)
        x_face = ((2, x_groups, ny, LANES), F32)
        x_slots = ((gx, x_groups, ny, LANES), F32)
        y_face = ((1 if gy == 2 else 2, nz, VARS, nx), F32)
        matrix = ((VARS, VARS, ny, nx), F32)
        blocks = ((nz, VARS, VARS, ny, nx), jac.dtype)
        side_blocks = ((nz, 4, VARS, VARS, ny, nx), jac.dtype)
        unit = 40 * nz * ny * nx

        def exchange(x_side, y_side, slots):
            if gy == 2:
                rows = [lax.ppermute(y_side[0], "gy", [(0, 1), (1, 0)])]
            else:
                up = [(i, i + 1) for i in range(gy - 1)]
                rows = [
                    lax.ppermute(y_side[1], "gy", up),
                    lax.ppermute(y_side[0], "gy", [(j, i) for i, j in up]),
                ]
            if slots:
                return lax.all_to_all(x_side, "gx", 0, 0, tiled=True), *rows
            return lax.all_gather(x_side, "gx"), *rows


        def forward_plane(source, inv_ref, low_jac, z, at, earlier):
            lagged = apply_block(block(low_jac, z, at=at), earlier)
            return apply_block(block(inv_ref, z, at=at), [a - b for a, b in zip(source, lagged)])

        def backward_plane(sweep, inner, inv_ref, high_jac, z, at, later):
            change = apply_block(block(high_jac, z, at=at), later)
            change = apply_block(block(inv_ref, z, at=at), [a + b for a, b in zip(change, inner)])
            return [a - b for a, b in zip(sweep, change)]

        def put(ref, values, at):
            for var in range(VARS):
                ref[var, :, at] = values[var]

        def incoming(refs, at):
            total = [refs[0][var, :, at] for var in range(VARS)]
            for ref in refs[1:]:
                total = [a + ref[var, :, at] for var, a in enumerate(total)]
            return tuple(total)

        def apply_matrix(matrix_ref, vector, at):
            return apply_block(block(matrix_ref, at=at), vector)

        def arrived(plain, matrix_ref, vector_ref, at):
            total = apply_matrix(matrix_ref, [vector_ref[var, :, at] for var in range(VARS)], at)
            for ref in plain:
                total = [a + ref[var, :, at] for var, a in enumerate(total)]
            return tuple(total)

        def forward_sweep(source_ref, inv_ref, low_jac, starts, keep=None):
            def step(z, earlier):
                results = []
                for tile, at in enumerate(spans):
                    source = planes_of(source_ref, z, at)
                    result = forward_plane(source, inv_ref, low_jac, z, at, earlier[tile])
                    if keep is not None:
                        keep(z, at, result)
                    results.append(tuple(result))
                return tuple(results)

            return lax.fori_loop(0, nz, step, starts)

        def backward_sweep(sweep_ref, inner_ref, inv_ref, high_jac, starts, keep=None):
            def step(i, later):
                z = nz - 1 - i
                results = []
                for tile, at in enumerate(spans):
                    sweep, inner = planes_of(sweep_ref, z, at), planes_of(inner_ref, z, at)
                    result = backward_plane(sweep, inner, inv_ref, high_jac, z, at, later[tile])
                    if keep is not None:
                        keep(z, tile, at, result)
                    results.append(tuple(result))
                return tuple(results)

            return lax.fori_loop(0, nz, step, starts)

        def transfer(matrix_ref, inv_ref, couple_ref, wait):
            half = VARS // 2
            groups = [range(g * half, (g + 1) * half) for g in range(VARS // half)]

            def plane_step(z, at, group, vectors):
                couple, inverse = block(couple_ref, z, at=at), block(inv_ref, z, at=at)
                middle = [[] for _ in group]
                for r in range(VARS):
                    row = [couple(r, c).astype(F32) for c in range(VARS)]
                    for i in range(len(group)):
                        middle[i].append(row[group[i]] if vectors is None else dot6(row, vectors[i]))
                for r in range(VARS):
                    row = [inverse(r, c).astype(F32) for c in range(VARS)]
                    for i, c in enumerate(group):
                        matrix_ref[r, c, :, at] = -dot6(row, middle[i])

            def step(i, carry):
                z = wait(i)
                for at in spans:
                    for group in groups:
                        vectors = [[matrix_ref[r, c, :, at] for r in range(VARS)] for c in group]
                        plane_step(z, at, group, vectors)
                return carry

            z = wait(0)
            for at in spans:
                for group in groups:
                    plane_step(z, at, group, None)
            lax.fori_loop(1, nz, step, 0)


        def open_kernel(prev_hbm, inv_hbm, jac_hbm, *rest):
            prev_ref, inv_ref, low_jac, x_side, y_side, *matrices, sem, sems = rest

            def copies(z):
                return [
                    pltpu.make_async_copy(inv_hbm.at[z], inv_ref.at[z], sems.at[0, z]),
                    pltpu.make_async_copy(jac_hbm.at[z, 4], low_jac.at[z], sems.at[1, z]),
                ]

            def wait(z):
                for copy in copies(z):
                    copy.wait()
                return z

            first_copy = pltpu.make_async_copy(prev_hbm, prev_ref, sem)
            first_copy.start()
            for z in range(nz):
                for copy in copies(z):
                    copy.start()
            here = lax.axis_index("gz") == 2
            if matrices:

                @pl.when(here)
                def _():
                    transfer(matrices[0], inv_ref, low_jac, wait)

            first_copy.wait()
            write_faces(prev_ref, x_side, y_side, nz, True)

            def rest_of_copies():
                for z in range(nz):
                    wait(z)

            if matrices:

                @pl.when(jnp.logical_not(here))
                def _():
                    matrices[0][...] = jnp.zeros(matrix[0], F32)
                    rest_of_copies()

            else:
                rest_of_copies()

        def first_kernel(rhs_hbm, jac_hbm, prev_ref, inv_ref, low_jac, x_all, *rest):
            y_rows, (source_ref, top_ref, sides, high_jac, rhs_ref, sems) = rest[:-6], rest[-6:]
            halo = halo_reader(x_all, y_rows, gx, gy, True)

            def copies(z):
                return [
                    pltpu.make_async_copy(jac_hbm.at[z, 0:4], sides.at[z], sems.at[0, z]),
                    pltpu.make_async_copy(rhs_hbm.at[z], rhs_ref.at[z], sems.at[1, z]),
                ]

            def high_copy(z):
                return pltpu.make_async_copy(jac_hbm.at[z, 5], high_jac.at[z], sems.at[2, z])

            for z in range(nz):
                for copy in copies(z):
                    copy.start()
            for z in range(nz):
                high_copy(z).start()

            def step(z, earlier):
                for copy in copies(z):
                    copy.wait()
                results = []
                for tile, at in enumerate(spans):
                    lagged = inplane(sides, prev_ref, z, tile, tiles, halo)
                    source = [a - b for a, b in zip(planes_of(rhs_ref, z, at), lagged)]
                    for var in range(VARS):
                        source_ref[z, var, :, at] = source[var]
                    results.append(tuple(forward_plane(source, inv_ref, low_jac, z, at, earlier[tile])))
                return tuple(results)

            zero = tuple(jnp.zeros((ny, LANES), F32) for _ in range(VARS))
            top = lax.fori_loop(0, nz, step, (zero,) * tiles)
            for tile, at in enumerate(spans):
                put(top_ref, top[tile], at)
            for z in range(nz):
                high_copy(z).wait()

        def forward_kernel(source_ref, inv_ref, low_jac, *rest):
            came, top_ref = rest[:-1], rest[-1]
            starts = tuple(incoming(came, at) for at in spans)
            top = forward_sweep(source_ref, inv_ref, low_jac, starts)
            for tile, at in enumerate(spans):
                put(top_ref, top[tile], at)

        def forward_mid_kernel(low_ref, came_ref, source_ref, inv_ref, low_jac, _, top_ref):
            top_ref[...] = low_ref[...]

            @pl.when(lax.axis_index("gz") == 1)
            def _():
                forward_kernel(source_ref, inv_ref, low_jac, came_ref, top_ref)

        def forward_last_kernel(source_ref, prev_ref, inv_ref, low_jac, *rest):
            if short:
                (first, near, matrix_ref, far), outs = rest[:4], rest[5:9]
                starts = tuple(arrived((first, near), matrix_ref, far, at) for at in spans)
            else:
                came, outs = rest[:-4], rest[-4:]
                starts = tuple(incoming(came, at) for at in spans)
            sweep_ref, change_ref, x_side, y_side = outs

            def keep(z, at, result):
                before = planes_of(prev_ref, z, at)
                for var in range(VARS):
                    sweep_ref[z, var, :, at] = result[var]
                    change_ref[z, var, :, at] = result[var] - before[var]

            forward_sweep(source_ref, inv_ref, low_jac, starts, keep)
            write_faces(change_ref, x_side, y_side, nz, False)

        def turn_kernel(sweep_ref, change_ref, inv_ref, sides, high_jac, x_all, *rest):
            y_rows, (inner_ref, low_ref) = rest[:-2], rest[-2:]
            halo = halo_reader(x_all, y_rows, gx, gy, False)
            for tile, at in enumerate(spans):

                def step(i, later, tile=tile, at=at):
                    z = nz - 1 - i
                    inner = inplane(sides, change_ref, z, tile, tiles, halo)
                    for var in range(VARS):
                        inner_ref[z, var, :, at] = inner[var]
                    sweep = planes_of(sweep_ref, z, at)
                    return tuple(backward_plane(sweep, inner, inv_ref, high_jac, z, at, later))

                zero = tuple(jnp.zeros((ny, LANES), F32) for _ in range(VARS))
                put(low_ref, lax.fori_loop(0, nz, step, zero), at)

        def down_matrix_kernel(device, inv_ref, high_jac, *rest):
            matrix_ref = rest[-1]
            here = lax.axis_index("gz") == device

            @pl.when(here)
            def _():
                transfer(matrix_ref, inv_ref, high_jac, lambda i: nz - 1 - i)

            @pl.when(jnp.logical_not(here))
            def _():
                matrix_ref[...] = jnp.zeros(matrix[0], F32)

        def backward_kernel(sweep_ref, inner_ref, inv_ref, high_jac, *rest):
            came, low_ref = rest[:-1], rest[-1]
            starts = tuple(incoming(came, at) for at in spans)
            low = backward_sweep(sweep_ref, inner_ref, inv_ref, high_jac, starts)
            for tile, at in enumerate(spans):
                put(low_ref, low[tile], at)

        def backward_mid_kernel(own_ref, near, there_ref, far, matrix_ref, came_ref, low_ref):
            for at in spans:
                came = arrived((near,), there_ref, far, at)
                moved = apply_matrix(matrix_ref, came, at)
                put(came_ref, came, at)
                put(low_ref, [own_ref[var, :, at] + moved[var] for var in range(VARS)], at)

        def update_kernel(sweep_ref, inner_ref, inv_ref, high_jac, *rest):
            came, (out_hbm, held, sems) = rest[:-3], rest[-3:]

            def out_copy(z):
                return pltpu.make_async_copy(held.at[z], out_hbm.at[z], sems.at[z])

            def keep(z, tile, at, result):
                for var in range(VARS):
                    held[z, var, :, at] = result[var]
                if tile == tiles - 1:
                    out_copy(z).start()

            starts = tuple(incoming(came, at) for at in spans)
            backward_sweep(sweep_ref, inner_ref, inv_ref, high_jac, starts, keep)
            for z in range(nz):
                out_copy(z).wait()


        prev, inv, low_jac, x_side, y_side, *up_matrix = call(
            open_kernel,
            [volume, blocks, blocks, x_slots, y_face] + [matrix] * (1 if short else 0),
            prev,
            inv,
            jac,
            cost=12 * unit,
            in_hbm=(0, 1, 2),
            scratch=[pltpu.SemaphoreType.DMA, pltpu.SemaphoreType.DMA((2, nz))],
        )
        if short:
            up_there = lax.ppermute(up_matrix[0], "gz", [(2, 3)])
        halo = exchange(x_side, y_side, True)
        source, top, sides, high_jac = call(
            first_kernel,
            [volume, plane, side_blocks, blocks],
            rhs,
            jac,
            prev,
            inv,
            low_jac,
            *halo,
            cost=unit // 8,
            in_hbm=(0, 1),
            scratch=[pltpu.VMEM(rhs.shape, F32), pltpu.SemaphoreType.DMA((3, nz))],
        )
        if short:
            first = lax.ppermute(top, "gz", [(0, 1)])
            (own_matrix,) = call(
                functools.partial(down_matrix_kernel, 1), [matrix], inv, high_jac, cost=unit // 8
            )
            (top,) = call(
                forward_mid_kernel,
                [plane],
                top,
                first,
                source,
                inv,
                low_jac,
                own_matrix,
                cost=unit // 8,
            )
            far = lax.ppermute(top, "gz", [(1, 3)])
            near = lax.ppermute(top, "gz", [(1, 2), (2, 3)])
            (down_matrix,) = call(
                functools.partial(down_matrix_kernel, 2),
                [matrix],
                inv,
                high_jac,
                up_there,
                cost=unit // 8,
            )
            came = [first, near, up_there, far]
            extra = [down_matrix]
        else:
            came, extra = [], []
            for hop in range(gz - 1):
                if hop:
                    (top,) = call(
                        forward_kernel, [plane], source, inv, low_jac, *came, cost=3 * unit
                    )
                came.append(lax.ppermute(top, "gz", [(hop, hop + 1)]))
        sweep, change, x_side, y_side, *extra = call(
            forward_last_kernel,
            [volume, volume, x_face, y_face] + [matrix] * len(extra),
            source,
            prev,
            inv,
            low_jac,
            *came,
            *extra,
            cost=4 * unit,
            aliases={4 + len(came): 4} if short else {},
        )
        if short:
            down_there = lax.ppermute(extra[0], "gz", [(2, 1)])
        halo = exchange(x_side, y_side, False)
        inner, low = call(
            turn_kernel, [volume, plane], sweep, change, inv, sides, high_jac, *halo, cost=11 * unit
        )
        if short:
            far = lax.ppermute(low, "gz", [(3, 1)])
            near = lax.ppermute(low, "gz", [(3, 2), (2, 1)])
            entered, low = call(
                backward_mid_kernel,
                [plane, plane],
                low,
                near,
                down_there,
                far,
                own_matrix,
                cost=unit,
            )
            came = [entered, lax.ppermute(low, "gz", [(1, 0)])]
        else:
            came = []
            for hop in range(gz - 1, 0, -1):
                if came:
                    (low,) = call(
                        backward_kernel, [plane], sweep, inner, inv, high_jac, *came, cost=3 * unit
                    )
                came.append(lax.ppermute(low, "gz", [(hop, hop - 1)]))
        (update,) = call(
            update_kernel,
            [volume],
            sweep,
            inner,
            inv,
            high_jac,
            *came,
            cost=5 * unit,
            out_hbm=(0,),
            scratch=[pltpu.VMEM(volume[0], F32), pltpu.SemaphoreType.DMA((nz,))],
        )
        return jnp.transpose(update, (0, 2, 1, 3))

    placed = (
        P("gz", "gy", None, "gx"),
        P("gz", "gy", None, "gx"),
        P("gz", "gy", None, None, "gx"),
        P("gz", "gy", None, None, None, "gx"),
    )
    return jax.shard_map(
        body, mesh=mesh, in_specs=placed, out_specs=P("gz", "gy", None, "gx"), check_vma=False
    )
```

```python
import functools

import jax
import jax.numpy as jnp
from jax import lax
from jax.experimental import pallas as pl
from jax.experimental.pallas import tpu as pltpu
from jax.sharding import PartitionSpec as P

VARS = 6
LANES = 128
F32 = jnp.float32
WHOLE = pl.BlockSpec(memory_space=pltpu.VMEM)


def call(body, outs, *args, cost, limit=16 << 20, scratch=(), in_hbm=(), out_hbm=(), aliases={}):
    far = pl.BlockSpec(memory_space=pl.ANY)
    shapes = [
        jax.ShapeDtypeStruct(o[0], o[1]) if i in out_hbm else pltpu.VMEM(o[0], o[1])
        for i, o in enumerate(outs)
    ]
    return pl.pallas_call(
        body,
        out_shape=shapes,
        in_specs=[far if i in in_hbm else WHOLE for i in range(len(args))],
        out_specs=[far if i in out_hbm else WHOLE for i in range(len(outs))],
        scratch_shapes=scratch,
        input_output_aliases=aliases,
        cost_estimate=pl.CostEstimate(flops=0, bytes_accessed=cost, transcendentals=0),
        compiler_params=pltpu.CompilerParams(vmem_limit_bytes=limit),
    )(*[
        pltpu.with_memory_space_constraint(a, pltpu.HBM if i in in_hbm else pltpu.VMEM)
        for i, a in enumerate(args)
    ])


def lane_iota(rows):
    return lax.broadcasted_iota(jnp.int32, (rows, LANES), 1)


def row_iota(rows):
    return lax.broadcasted_iota(jnp.int32, (rows, LANES), 0)


def dot6(blocks, values):
    terms = [b.astype(F32) * v for b, v in zip(blocks, values)]
    return (terms[0] + terms[1]) + (terms[2] + terms[3]) + (terms[4] + terms[5])


def block(ref, *index, at):
    return lambda r, c: ref[(*index, r, c, slice(None), at)]


def apply_block(get, values):
    return [dot6([get(r, c) for c in range(VARS)], values) for r in range(VARS)]


def write_faces(value, x_face, y_face, z_count):
    y_count = value.shape[2]
    x_count = value.shape[3]
    lane = lane_iota(y_count)
    for group in range(x_face.shape[1]):
        faces = []
        for start, source_lane in ((0, 0), (x_count - LANES, LANES - 1)):
            held = jnp.zeros((y_count, LANES), F32)
            for slot in range(min(LANES, z_count * VARS - group * LANES)):
                z, var = divmod(group * LANES + slot, VARS)
                tile = value[z, var, :, start : start + LANES]
                moved = pltpu.roll(tile, (slot - source_lane) % LANES, 1)
                held = jnp.where(lane == slot, moved, held)
            faces.append(held)
        x_face[0, group], x_face[1, group] = faces
    if y_face.shape[0] == 1:
        first = lax.axis_index("gy") == 0
        for z in range(z_count):
            for var in range(VARS):
                low = value[z, var, 0:1, :]
                high = value[z, var, y_count - 1 : y_count, :]
                y_face[0, z, var : var + 1, :] = jnp.where(first, high, low)
    else:
        for z in range(z_count):
            for var in range(VARS):
                y_face[0, z, var : var + 1, :] = value[z, var, 0:1, :]
                y_face[1, z, var : var + 1, :] = value[z, var, y_count - 1 : y_count, :]


def halo_reader(x_all, y_rows, gx, gy):
    me_x = lax.axis_index("gx")

    def column(there, side, to_lane):
        exists = (there >= 0) & (there < gx)
        device = jnp.clip(there, 0, gx - 1)

        def read(z, var):
            j = z * VARS + var
            face = x_all[device, side, j // LANES]
            moved = pltpu.roll(face, (to_lane + LANES - j % LANES) % LANES, 1)
            return jnp.where(exists, moved, jnp.zeros_like(moved))

        return read

    def row(which):
        def read(z, var, at):
            if len(y_rows) > 1:
                return y_rows[which][z, var : var + 1, at]
            here = y_rows[0][z, var : var + 1, at]
            return jnp.where(lax.axis_index("gy") == 1 - which, here, jnp.zeros_like(here))

        return read

    return column(me_x - 1, 1, 0), column(me_x + 1, 0, LANES - 1), row(0), row(1)


def neighbours(value, z, tile, tiles, halo):
    y_count = value.shape[2]
    lane = lane_iota(y_count)
    row = row_iota(y_count)
    at = slice(tile * LANES, (tile + 1) * LANES)
    result = ([], [], [], [])
    for var in range(VARS):
        here = value[z, var, :, at]
        if tile > 0:
            before = pltpu.roll(value[z, var, :, at.start - LANES : at.start], 1, 1)
        else:
            before = halo[0](z, var)
        if tile < tiles - 1:
            after = pltpu.roll(value[z, var, :, at.stop : at.stop + LANES], LANES - 1, 1)
        else:
            after = halo[1](z, var)
        result[0].append(jnp.where(lane == 0, before, pltpu.roll(here, 1, 1)))
        result[1].append(jnp.where(lane == LANES - 1, after, pltpu.roll(here, LANES - 1, 1)))
        result[2].append(jnp.where(row == 0, halo[2](z, var, at), pltpu.roll(here, 1, 0)))
        result[3].append(
            jnp.where(row == y_count - 1, halo[3](z, var, at), pltpu.roll(here, y_count - 1, 0))
        )
    return result


def inplane(jacobians, value, z, tile, tiles, halo):
    at = slice(tile * LANES, (tile + 1) * LANES)
    total = None
    for n, values in enumerate(neighbours(value, z, tile, tiles, halo)):
        part = apply_block(block(jacobians, z, n, at=at), values)
        total = part if total is None else [a + b for a, b in zip(total, part)]
    return total


def planes_of(ref, z, at):
    return [ref[z, var, :, at] for var in range(VARS)]


def solution(mesh):
    gz, gx, gy = (mesh.shape[a] for a in ("gz", "gx", "gy"))
    short = gz == 4

    def body(right_side, previous, diag_inverse, jacobians):
        rhs = jnp.transpose(right_side, (0, 2, 1, 3))
        prev = jnp.transpose(previous, (0, 2, 1, 3))
        inv = jnp.transpose(diag_inverse, (0, 2, 3, 1, 4))
        jac = jnp.transpose(jacobians, (0, 2, 3, 4, 1, 5))
        nz, _, ny, nx = rhs.shape
        tiles = nx // LANES
        assert nx % LANES == 0
        spans = [slice(t * LANES, (t + 1) * LANES) for t in range(tiles)]
        plane = ((VARS, ny, nx), F32)
        volume = ((nz, VARS, ny, nx), F32)
        x_groups = -(-nz * VARS // LANES)
        x_face = ((2, x_groups, ny, LANES), F32)
        y_face = ((1 if gy == 2 else 2, nz, VARS, nx), F32)
        matrix = ((VARS, VARS, ny, nx), F32)
        blocks = ((nz, VARS, VARS, ny, nx), jac.dtype)
        side_blocks = ((nz, 4, VARS, VARS, ny, nx), jac.dtype)
        unit = 40 * nz * ny * nx

        def exchange(x_side, y_side):
            if gy == 2:
                rows = [lax.ppermute(y_side[0], "gy", [(0, 1), (1, 0)])]
            else:
                up = [(i, i + 1) for i in range(gy - 1)]
                rows = [
                    lax.ppermute(y_side[1], "gy", up),
                    lax.ppermute(y_side[0], "gy", [(j, i) for i, j in up]),
                ]
            return lax.all_gather(x_side, "gx"), *rows


        def forward_plane(source, inv_ref, low_jac, z, at, earlier):
            lagged = apply_block(block(low_jac, z, at=at), earlier)
            return apply_block(block(inv_ref, z, at=at), [a - b for a, b in zip(source, lagged)])

        def backward_plane(sweep, inner, inv_ref, high_jac, z, at, later):
            change = apply_block(block(high_jac, z, at=at), later)
            change = apply_block(block(inv_ref, z, at=at), [a + b for a, b in zip(change, inner)])
            return [a - b for a, b in zip(sweep, change)]

        def put(ref, values, at):
            for var in range(VARS):
                ref[var, :, at] = values[var]

        def incoming(refs, at):
            total = [refs[0][var, :, at] for var in range(VARS)]
            for ref in refs[1:]:
                total = [a + ref[var, :, at] for var, a in enumerate(total)]
            return tuple(total)

        def planes_in(ref, at):
            return [ref[var, :, at] for var in range(VARS)]

        def apply_matrix(matrix_ref, vector, at):
            return apply_block(block(matrix_ref, at=at), vector)

        def arrived(plain, matrix_ref, vector_ref, at):
            total = apply_matrix(matrix_ref, [vector_ref[var, :, at] for var in range(VARS)], at)
            for ref in plain:
                total = [a + ref[var, :, at] for var, a in enumerate(total)]
            return tuple(total)

        def forward_sweep(source_ref, inv_ref, low_jac, starts, keep=None):
            def step(z, earlier):
                results = []
                for tile, at in enumerate(spans):
                    source = planes_of(source_ref, z, at)
                    result = forward_plane(source, inv_ref, low_jac, z, at, earlier[tile])
                    if keep is not None:
                        keep(z, at, result)
                    results.append(tuple(result))
                return tuple(results)

            return lax.fori_loop(0, nz, step, starts)

        def backward_sweep(sweep_ref, inner_ref, inv_ref, high_jac, starts, keep=None):
            def step(i, later):
                z = nz - 1 - i
                results = []
                for tile, at in enumerate(spans):
                    sweep, inner = planes_of(sweep_ref, z, at), planes_of(inner_ref, z, at)
                    result = backward_plane(sweep, inner, inv_ref, high_jac, z, at, later[tile])
                    if keep is not None:
                        keep(z, tile, at, result)
                    results.append(tuple(result))
                return tuple(results)

            return lax.fori_loop(0, nz, step, starts)

        def transfer(matrix_ref, inv_ref, couple_ref, wait):
            half = VARS // 2
            groups = [range(g * half, (g + 1) * half) for g in range(VARS // half)]

            def plane_step(z, at, group, vectors):
                couple, inverse = block(couple_ref, z, at=at), block(inv_ref, z, at=at)
                middle = [[] for _ in group]
                for r in range(VARS):
                    row = [couple(r, c).astype(F32) for c in range(VARS)]
                    for i in range(len(group)):
                        middle[i].append(row[group[i]] if vectors is None else dot6(row, vectors[i]))
                for r in range(VARS):
                    row = [inverse(r, c).astype(F32) for c in range(VARS)]
                    for i, c in enumerate(group):
                        matrix_ref[r, c, :, at] = -dot6(row, middle[i])

            def step(i, carry):
                z = wait(i)
                for at in spans:
                    for group in groups:
                        vectors = [[matrix_ref[r, c, :, at] for r in range(VARS)] for c in group]
                        plane_step(z, at, group, vectors)
                return carry

            z = wait(0)
            for at in spans:
                for group in groups:
                    plane_step(z, at, group, None)
            lax.fori_loop(1, nz, step, 0)


        def open_kernel(prev_hbm, inv_hbm, jac_hbm, *rest):
            prev_ref, inv_ref, low_jac, x_side, y_side, *matrices, sem, sems = rest

            def copies(z):
                return [
                    pltpu.make_async_copy(inv_hbm.at[z], inv_ref.at[z], sems.at[0, z]),
                    pltpu.make_async_copy(jac_hbm.at[z, 4], low_jac.at[z], sems.at[1, z]),
                ]

            def wait(z):
                for copy in copies(z):
                    copy.wait()
                return z

            first_copy = pltpu.make_async_copy(prev_hbm, prev_ref, sem)
            first_copy.start()
            for z in range(nz):
                for copy in copies(z):
                    copy.start()
            here = lax.axis_index("gz") == 2
            if matrices:

                @pl.when(here)
                def _():
                    transfer(matrices[0], inv_ref, low_jac, wait)

            first_copy.wait()
            write_faces(prev_ref, x_side, y_side, nz)

            def rest_of_copies():
                for z in range(nz):
                    wait(z)

            if matrices:

                @pl.when(jnp.logical_not(here))
                def _():
                    matrices[0][...] = jnp.zeros(matrix[0], F32)
                    rest_of_copies()

            else:
                rest_of_copies()

        def on(wanted, work):
            if wanted is None:
                work()
            else:
                pl.when(wanted(lax.axis_index("gz")))(work)

        def first_kernel(wanted, rhs_hbm, jac_hbm, prev_ref, inv_ref, low_jac, x_all, *rest):
            y_rows, outs = rest[: 1 if gy == 2 else 2], rest[-6:]
            on(
                wanted,
                lambda: first_work(
                    rhs_hbm, jac_hbm, prev_ref, inv_ref, low_jac, x_all, y_rows, *outs
                ),
            )

        def first_again_kernel(wanted, *refs):
            refs[-5][...] = refs[-9][...]
            first_kernel(wanted, *refs)

        def first_work(
            rhs_hbm, jac_hbm, prev_ref, inv_ref, low_jac, x_all, y_rows,
            source_ref, top_ref, sides, high_jac, rhs_ref, sems,
        ):
            halo = halo_reader(x_all, y_rows, gx, gy)

            def copies(z):
                return [
                    pltpu.make_async_copy(jac_hbm.at[z, 0:4], sides.at[z], sems.at[0, z]),
                    pltpu.make_async_copy(rhs_hbm.at[z], rhs_ref.at[z], sems.at[1, z]),
                ]

            def high_copy(z):
                return pltpu.make_async_copy(jac_hbm.at[z, 5], high_jac.at[z], sems.at[2, z])

            for z in range(nz):
                for copy in copies(z):
                    copy.start()
            for z in range(nz):
                high_copy(z).start()

            def step(z, earlier):
                for copy in copies(z):
                    copy.wait()
                results = []
                for tile, at in enumerate(spans):
                    lagged = inplane(sides, prev_ref, z, tile, tiles, halo)
                    source = [a - b for a, b in zip(planes_of(rhs_ref, z, at), lagged)]
                    for var in range(VARS):
                        source_ref[z, var, :, at] = source[var]
                    results.append(tuple(forward_plane(source, inv_ref, low_jac, z, at, earlier[tile])))
                return tuple(results)

            zero = tuple(jnp.zeros((ny, LANES), F32) for _ in range(VARS))
            top = lax.fori_loop(0, nz, step, (zero,) * tiles)
            for tile, at in enumerate(spans):
                put(top_ref, top[tile], at)
            for z in range(nz):
                high_copy(z).wait()

        def forward_kernel(source_ref, inv_ref, low_jac, *rest):
            came, top_ref = rest[:-1], rest[-1]
            starts = tuple(incoming(came, at) for at in spans)
            top = forward_sweep(source_ref, inv_ref, low_jac, starts)
            for tile, at in enumerate(spans):
                put(top_ref, top[tile], at)

        def forward_mid_kernel(low_ref, came_ref, source_ref, inv_ref, low_jac, _, top_ref):
            top_ref[...] = low_ref[...]

            @pl.when(lax.axis_index("gz") == 1)
            def _():
                forward_kernel(source_ref, inv_ref, low_jac, came_ref, top_ref)

        def forward_last_kernel(source_ref, prev_ref, inv_ref, low_jac, *rest):
            if short:
                (first, near, matrix_ref, far), outs = rest[:4], rest[5:9]
                starts = tuple(arrived((first, near), matrix_ref, far, at) for at in spans)
            else:
                came, outs = rest[:-4], rest[-4:]
                starts = tuple(incoming(came, at) for at in spans)
            sweep_ref, change_ref, x_side, y_side = outs

            def keep(z, at, result):
                before = planes_of(prev_ref, z, at)
                for var in range(VARS):
                    sweep_ref[z, var, :, at] = result[var]
                    change_ref[z, var, :, at] = result[var] - before[var]

            forward_sweep(source_ref, inv_ref, low_jac, starts, keep)
            write_faces(change_ref, x_side, y_side, nz)

        def turn_kernel(wanted, sweep_ref, change_ref, inv_ref, sides, high_jac, x_all, *rest):
            y_rows, outs = rest[: 1 if gy == 2 else 2], rest[-2:]
            on(
                wanted,
                lambda: turn_work(
                    sweep_ref, change_ref, inv_ref, sides, high_jac, x_all, y_rows, *outs
                ),
            )

        def turn_again_kernel(wanted, *refs):
            refs[-1][...] = refs[-3][...]
            turn_kernel(wanted, *refs)

        def turn_work(
            sweep_ref, change_ref, inv_ref, sides, high_jac, x_all, y_rows, inner_ref, low_ref
        ):
            halo = halo_reader(x_all, y_rows, gx, gy)
            for tile, at in enumerate(spans):

                def step(i, later, tile=tile, at=at):
                    z = nz - 1 - i
                    inner = inplane(sides, change_ref, z, tile, tiles, halo)
                    for var in range(VARS):
                        inner_ref[z, var, :, at] = inner[var]
                    sweep = planes_of(sweep_ref, z, at)
                    return tuple(backward_plane(sweep, inner, inv_ref, high_jac, z, at, later))

                zero = tuple(jnp.zeros((ny, LANES), F32) for _ in range(VARS))
                put(low_ref, lax.fori_loop(0, nz, step, zero), at)

        def down_matrix_kernel(device, inv_ref, high_jac, *rest):
            matrix_ref = rest[-1]
            here = lax.axis_index("gz") == device

            @pl.when(here)
            def _():
                transfer(matrix_ref, inv_ref, high_jac, lambda i: nz - 1 - i)

            @pl.when(jnp.logical_not(here))
            def _():
                matrix_ref[...] = jnp.zeros(matrix[0], F32)

        def backward_kernel(sweep_ref, inner_ref, inv_ref, high_jac, *rest):
            came, low_ref = rest[:-1], rest[-1]
            starts = tuple(incoming(came, at) for at in spans)
            low = backward_sweep(sweep_ref, inner_ref, inv_ref, high_jac, starts)
            for tile, at in enumerate(spans):
                put(low_ref, low[tile], at)

        def far_kernel(far_ref, matrix_ref, moved_ref):
            for at in spans:
                put(moved_ref, apply_matrix(matrix_ref, planes_in(far_ref, at), at), at)

        def backward_mid_kernel(own_ref, near_ref, moved_ref, matrix_ref, came_ref, low_ref):
            for at in spans:
                came = incoming((near_ref, moved_ref), at)
                moved = apply_matrix(matrix_ref, came, at)
                put(came_ref, came, at)
                put(low_ref, [a + b for a, b in zip(planes_in(own_ref, at), moved)], at)

        def update_kernel(sweep_ref, inner_ref, inv_ref, high_jac, *rest):
            came, (out_hbm, held, sems) = rest[:-3], rest[-3:]

            def out_copy(z):
                return pltpu.make_async_copy(held.at[z], out_hbm.at[z], sems.at[z])

            def keep(z, tile, at, result):
                for var in range(VARS):
                    held[z, var, :, at] = result[var]
                if tile == tiles - 1:
                    out_copy(z).start()

            starts = tuple(incoming(came, at) for at in spans)
            backward_sweep(sweep_ref, inner_ref, inv_ref, high_jac, starts, keep)
            for z in range(nz):
                out_copy(z).wait()


        prev, inv, low_jac, x_side, y_side, *up_matrix = call(
            open_kernel,
            [volume, blocks, blocks, x_face, y_face] + [matrix] * (1 if short else 0),
            prev,
            inv,
            jac,
            cost=12 * unit,
            in_hbm=(0, 1, 2),
            scratch=[pltpu.SemaphoreType.DMA, pltpu.SemaphoreType.DMA((2, nz))],
        )
        if short:
            up_there = lax.ppermute(up_matrix[0], "gz", [(2, 3)])
        halo = exchange(x_side, y_side)
        ahead, behind = None, None
        if short:
            ahead, behind = (lambda device: device == 0), (lambda device: device != 0)
        first_args = [rhs, jac, prev, inv, low_jac, *halo]
        first_options = dict(
            cost=unit // 8,
            in_hbm=(0, 1),
            scratch=[pltpu.VMEM(rhs.shape, F32), pltpu.SemaphoreType.DMA((3, nz))],
        )
        first_outs = [volume, plane, side_blocks, blocks]
        source, top, sides, high_jac = call(
            functools.partial(first_kernel, ahead), first_outs, *first_args, **first_options
        )
        if short:
            first = lax.ppermute(top, "gz", [(0, 1)])
            n = len(first_args)
            source, top, sides, high_jac = call(
                functools.partial(first_again_kernel, behind),
                first_outs,
                *first_args,
                source,
                top,
                sides,
                high_jac,
                aliases={n: 0, n + 2: 2, n + 3: 3},
                **first_options,
            )
            (own_matrix,) = call(
                functools.partial(down_matrix_kernel, 1), [matrix], inv, high_jac, cost=unit // 8
            )
            (top,) = call(
                forward_mid_kernel,
                [plane],
                top,
                first,
                source,
                inv,
                low_jac,
                own_matrix,
                cost=unit // 8,
            )
            far = lax.ppermute(top, "gz", [(1, 3)])
            near = lax.ppermute(top, "gz", [(1, 2), (2, 3)])
            (down_matrix,) = call(
                functools.partial(down_matrix_kernel, 2),
                [matrix],
                inv,
                high_jac,
                up_there,
                cost=unit // 8,
            )
            came = [first, near, up_there, far]
            extra = [down_matrix]
        else:
            came, extra = [], []
            for hop in range(gz - 1):
                if hop:
                    (top,) = call(
                        forward_kernel, [plane], source, inv, low_jac, *came, cost=3 * unit
                    )
                came.append(lax.ppermute(top, "gz", [(hop, hop + 1)]))
        sweep, change, x_side, y_side, *extra = call(
            forward_last_kernel,
            [volume, volume, x_face, y_face] + [matrix] * len(extra),
            source,
            prev,
            inv,
            low_jac,
            *came,
            *extra,
            cost=4 * unit,
            aliases={4 + len(came): 4} if short else {},
        )
        if short:
            down_there = lax.ppermute(extra[0], "gz", [(2, 1)])
        halo = exchange(x_side, y_side)
        if short:
            ahead, behind = (lambda device: device == 3), (lambda device: device != 3)
        turn_args = [sweep, change, inv, sides, high_jac, *halo]
        inner, low = call(
            functools.partial(turn_kernel, ahead), [volume, plane], *turn_args, cost=11 * unit
        )
        if short:
            ahead_low = low
            inner, low = call(
                functools.partial(turn_again_kernel, behind),
                [volume, plane],
                *turn_args,
                inner,
                low,
                aliases={len(turn_args): 0},
                cost=unit // 8,
            )
            near = lax.ppermute(low, "gz", [(3, 2), (2, 1)])
            far = lax.ppermute(ahead_low, "gz", [(3, 1)])
            (moved,) = call(far_kernel, [plane], far, down_there, cost=unit // 8)
            entered, low = call(
                backward_mid_kernel, [plane, plane], low, near, moved, own_matrix, cost=unit // 8
            )
            came = [entered, lax.ppermute(low, "gz", [(1, 0)])]
        else:
            came = []
            for hop in range(gz - 1, 0, -1):
                if came:
                    (low,) = call(
                        backward_kernel, [plane], sweep, inner, inv, high_jac, *came, cost=3 * unit
                    )
                came.append(lax.ppermute(low, "gz", [(hop, hop - 1)]))
        (update,) = call(
            update_kernel,
            [volume],
            sweep,
            inner,
            inv,
            high_jac,
            *came,
            cost=5 * unit,
            out_hbm=(0,),
            scratch=[pltpu.VMEM(volume[0], F32), pltpu.SemaphoreType.DMA((nz,))],
        )
        return jnp.transpose(update, (0, 2, 1, 3))

    placed = (
        P("gz", "gy", None, "gx"),
        P("gz", "gy", None, "gx"),
        P("gz", "gy", None, None, "gx"),
        P("gz", "gy", None, None, None, "gx"),
    )
    return jax.shard_map(
        body, mesh=mesh, in_specs=placed, out_specs=P("gz", "gy", None, "gx"), check_vma=False
    )
```

```python
import functools

import jax
import jax.numpy as jnp
from jax import lax
from jax.experimental import pallas as pl
from jax.experimental.pallas import tpu as pltpu
from jax.sharding import PartitionSpec as P

VARS = 6
LANES = 128
F32 = jnp.float32
WHOLE = pl.BlockSpec(memory_space=pltpu.VMEM)


def call(body, outs, *args, cost, limit=16 << 20, scratch=(), in_hbm=(), out_hbm=(), aliases={}):
    far = pl.BlockSpec(memory_space=pl.ANY)
    shapes = [
        jax.ShapeDtypeStruct(o[0], o[1]) if i in out_hbm else pltpu.VMEM(o[0], o[1])
        for i, o in enumerate(outs)
    ]
    return pl.pallas_call(
        body,
        out_shape=shapes,
        in_specs=[far if i in in_hbm else WHOLE for i in range(len(args))],
        out_specs=[far if i in out_hbm else WHOLE for i in range(len(outs))],
        scratch_shapes=scratch,
        input_output_aliases=aliases,
        cost_estimate=pl.CostEstimate(flops=0, bytes_accessed=cost, transcendentals=0),
        compiler_params=pltpu.CompilerParams(vmem_limit_bytes=limit),
    )(*[
        pltpu.with_memory_space_constraint(a, pltpu.HBM if i in in_hbm else pltpu.VMEM)
        for i, a in enumerate(args)
    ])


def lane_iota(rows):
    return lax.broadcasted_iota(jnp.int32, (rows, LANES), 1)


def row_iota(rows):
    return lax.broadcasted_iota(jnp.int32, (rows, LANES), 0)


def dot6(blocks, values):
    terms = [b.astype(F32) * v for b, v in zip(blocks, values)]
    return (terms[0] + terms[1]) + (terms[2] + terms[3]) + (terms[4] + terms[5])


def block(ref, *index, at):
    return lambda r, c: ref[(*index, r, c, slice(None), at)]


def apply_block(get, values):
    return [dot6([get(r, c) for c in range(VARS)], values) for r in range(VARS)]


def write_faces(value, x_face, y_face, z_count):
    y_count = value.shape[2]
    x_count = value.shape[3]
    lane = lane_iota(y_count)
    for group in range(x_face.shape[1]):
        faces = []
        for start, source_lane in ((0, 0), (x_count - LANES, LANES - 1)):
            held = jnp.zeros((y_count, LANES), F32)
            for slot in range(min(LANES, z_count * VARS - group * LANES)):
                z, var = divmod(group * LANES + slot, VARS)
                tile = value[z, var, :, start : start + LANES]
                moved = pltpu.roll(tile, (slot - source_lane) % LANES, 1)
                held = jnp.where(lane == slot, moved, held)
            faces.append(held)
        x_face[0, group], x_face[1, group] = faces
    if y_face.shape[0] == 1:
        first = lax.axis_index("gy") == 0
        for z in range(z_count):
            for var in range(VARS):
                low = value[z, var, 0:1, :]
                high = value[z, var, y_count - 1 : y_count, :]
                y_face[0, z, var : var + 1, :] = jnp.where(first, high, low)
    else:
        for z in range(z_count):
            for var in range(VARS):
                y_face[0, z, var : var + 1, :] = value[z, var, 0:1, :]
                y_face[1, z, var : var + 1, :] = value[z, var, y_count - 1 : y_count, :]


def halo_reader(x_all, y_rows, gx, gy):
    me_x = lax.axis_index("gx")

    def column(there, side, to_lane):
        exists = (there >= 0) & (there < gx)
        device = jnp.clip(there, 0, gx - 1)

        def read(z, var):
            j = z * VARS + var
            face = x_all[device, side, j // LANES]
            moved = pltpu.roll(face, (to_lane + LANES - j % LANES) % LANES, 1)
            return jnp.where(exists, moved, jnp.zeros_like(moved))

        return read

    def row(which):
        def read(z, var, at):
            if len(y_rows) > 1:
                return y_rows[which][z, var : var + 1, at]
            here = y_rows[0][z, var : var + 1, at]
            return jnp.where(lax.axis_index("gy") == 1 - which, here, jnp.zeros_like(here))

        return read

    return column(me_x - 1, 1, 0), column(me_x + 1, 0, LANES - 1), row(0), row(1)


def neighbours(value, z, tile, tiles, halo):
    y_count = value.shape[2]
    lane = lane_iota(y_count)
    row = row_iota(y_count)
    at = slice(tile * LANES, (tile + 1) * LANES)
    result = ([], [], [], [])
    for var in range(VARS):
        here = value[z, var, :, at]
        if tile > 0:
            before = pltpu.roll(value[z, var, :, at.start - LANES : at.start], 1, 1)
        else:
            before = halo[0](z, var)
        if tile < tiles - 1:
            after = pltpu.roll(value[z, var, :, at.stop : at.stop + LANES], LANES - 1, 1)
        else:
            after = halo[1](z, var)
        result[0].append(jnp.where(lane == 0, before, pltpu.roll(here, 1, 1)))
        result[1].append(jnp.where(lane == LANES - 1, after, pltpu.roll(here, LANES - 1, 1)))
        result[2].append(jnp.where(row == 0, halo[2](z, var, at), pltpu.roll(here, 1, 0)))
        result[3].append(
            jnp.where(row == y_count - 1, halo[3](z, var, at), pltpu.roll(here, y_count - 1, 0))
        )
    return result


def inplane(jacobians, value, z, tile, tiles, halo):
    at = slice(tile * LANES, (tile + 1) * LANES)
    total = None
    for n, values in enumerate(neighbours(value, z, tile, tiles, halo)):
        part = apply_block(block(jacobians, z, n, at=at), values)
        total = part if total is None else [a + b for a, b in zip(total, part)]
    return total


def planes_of(ref, z, at):
    return [ref[z, var, :, at] for var in range(VARS)]


def solution(mesh):
    gz, gx, gy = (mesh.shape[a] for a in ("gz", "gx", "gy"))
    short = gz == 4

    def body(right_side, previous, diag_inverse, jacobians):
        rhs = jnp.transpose(right_side, (0, 2, 1, 3))
        prev = jnp.transpose(previous, (0, 2, 1, 3))
        inv = jnp.transpose(diag_inverse, (0, 2, 3, 1, 4))
        jac = jnp.transpose(jacobians, (0, 2, 3, 4, 1, 5))
        nz, _, ny, nx = rhs.shape
        tiles = nx // LANES
        assert nx % LANES == 0
        spans = [slice(t * LANES, (t + 1) * LANES) for t in range(tiles)]
        plane = ((VARS, ny, nx), F32)
        volume = ((nz, VARS, ny, nx), F32)
        x_groups = -(-nz * VARS // LANES)
        x_face = ((2, x_groups, ny, LANES), F32)
        y_face = ((1 if gy == 2 else 2, nz, VARS, nx), F32)
        matrix = ((VARS, VARS, ny, nx), F32)
        steps = ((nz, VARS, VARS, ny, nx), F32)
        blocks = ((nz, VARS, VARS, ny, nx), jac.dtype)
        side_blocks = ((nz, 4, VARS, VARS, ny, nx), jac.dtype)
        unit = 40 * nz * ny * nx

        def exchange(x_side, y_side):
            if gy == 2:
                rows = [lax.ppermute(y_side[0], "gy", [(0, 1), (1, 0)])]
            else:
                up = [(i, i + 1) for i in range(gy - 1)]
                rows = [
                    lax.ppermute(y_side[1], "gy", up),
                    lax.ppermute(y_side[0], "gy", [(j, i) for i, j in up]),
                ]
            return lax.all_gather(x_side, "gx"), *rows


        def forward_plane(source, inv_ref, low_jac, z, at, earlier):
            lagged = apply_block(block(low_jac, z, at=at), earlier)
            return apply_block(block(inv_ref, z, at=at), [a - b for a, b in zip(source, lagged)])

        def backward_plane(sweep, inner, inv_ref, high_jac, z, at, later):
            change = apply_block(block(high_jac, z, at=at), later)
            change = apply_block(block(inv_ref, z, at=at), [a + b for a, b in zip(change, inner)])
            return [a - b for a, b in zip(sweep, change)]

        def fast_plane(step_ref, plain_ref, z, at, before):
            moved = apply_block(block(step_ref, z, at=at), before)
            return [a + b for a, b in zip(planes_of(plain_ref, z, at), moved)]

        def make_fast(step_ref, plain_ref, inv_ref, couple_ref, plain_of):
            half = VARS // 2

            def step(z, carry):
                for at in spans:
                    couple, inverse = block(couple_ref, z, at=at), block(inv_ref, z, at=at)
                    for g in range(VARS // half):
                        columns = range(g * half, (g + 1) * half)
                        held = [[couple(k, c).astype(F32) for k in range(VARS)] for c in columns]
                        for r in range(VARS):
                            row = [inverse(r, k).astype(F32) for k in range(VARS)]
                            for i, c in enumerate(columns):
                                step_ref[z, r, c, :, at] = -dot6(row, held[i])
                    plain = plain_of(z, at, lambda values: apply_block(inverse, values))
                    for var in range(VARS):
                        plain_ref[z, var, :, at] = plain[var]
                return carry

            lax.fori_loop(0, nz, step, 0)

        def put(ref, values, at):
            for var in range(VARS):
                ref[var, :, at] = values[var]

        def incoming(refs, at):
            total = [refs[0][var, :, at] for var in range(VARS)]
            for ref in refs[1:]:
                total = [a + ref[var, :, at] for var, a in enumerate(total)]
            return tuple(total)

        def planes_in(ref, at):
            return [ref[var, :, at] for var in range(VARS)]

        def apply_matrix(matrix_ref, vector, at):
            return apply_block(block(matrix_ref, at=at), vector)

        def arrived(plain, matrix_ref, vector_ref, at):
            total = apply_matrix(matrix_ref, [vector_ref[var, :, at] for var in range(VARS)], at)
            for ref in plain:
                total = [a + ref[var, :, at] for var, a in enumerate(total)]
            return tuple(total)

        def forward_sweep(source_ref, inv_ref, low_jac, starts, keep=None, fast=None):
            def step(z, earlier):
                results = []
                for tile, at in enumerate(spans):
                    if fast is not None:
                        result = fast_plane(*fast, z, at, earlier[tile])
                    else:
                        source = planes_of(source_ref, z, at)
                        result = forward_plane(source, inv_ref, low_jac, z, at, earlier[tile])
                    if keep is not None:
                        keep(z, at, result)
                    results.append(tuple(result))
                return tuple(results)

            return lax.fori_loop(0, nz, step, starts)

        def backward_sweep(sweep_ref, inner_ref, inv_ref, high_jac, starts, keep=None, fast=None):
            def step(i, later):
                z = nz - 1 - i
                results = []
                for tile, at in enumerate(spans):
                    if fast is not None:
                        result = fast_plane(*fast, z, at, later[tile])
                    else:
                        sweep, inner = planes_of(sweep_ref, z, at), planes_of(inner_ref, z, at)
                        result = backward_plane(sweep, inner, inv_ref, high_jac, z, at, later[tile])
                    if keep is not None:
                        keep(z, tile, at, result)
                    results.append(tuple(result))
                return tuple(results)

            return lax.fori_loop(0, nz, step, starts)

        def transfer(matrix_ref, inv_ref, couple_ref, wait):
            half = VARS // 2
            groups = [range(g * half, (g + 1) * half) for g in range(VARS // half)]

            def plane_step(z, at, group, vectors):
                couple, inverse = block(couple_ref, z, at=at), block(inv_ref, z, at=at)
                middle = [[] for _ in group]
                for r in range(VARS):
                    row = [couple(r, c).astype(F32) for c in range(VARS)]
                    for i in range(len(group)):
                        middle[i].append(row[group[i]] if vectors is None else dot6(row, vectors[i]))
                for r in range(VARS):
                    row = [inverse(r, c).astype(F32) for c in range(VARS)]
                    for i, c in enumerate(group):
                        matrix_ref[r, c, :, at] = -dot6(row, middle[i])

            def step(i, carry):
                z = wait(i)
                for at in spans:
                    for group in groups:
                        vectors = [[matrix_ref[r, c, :, at] for r in range(VARS)] for c in group]
                        plane_step(z, at, group, vectors)
                return carry

            z = wait(0)
            for at in spans:
                for group in groups:
                    plane_step(z, at, group, None)
            lax.fori_loop(1, nz, step, 0)


        def open_kernel(prev_hbm, inv_hbm, jac_hbm, *rest):
            prev_ref, inv_ref, low_jac, x_side, y_side, *matrices, sem, sems = rest

            def copies(z):
                return [
                    pltpu.make_async_copy(inv_hbm.at[z], inv_ref.at[z], sems.at[0, z]),
                    pltpu.make_async_copy(jac_hbm.at[z, 4], low_jac.at[z], sems.at[1, z]),
                ]

            def wait(z):
                for copy in copies(z):
                    copy.wait()
                return z

            first_copy = pltpu.make_async_copy(prev_hbm, prev_ref, sem)
            first_copy.start()
            for z in range(nz):
                for copy in copies(z):
                    copy.start()
            here = lax.axis_index("gz") == 2
            if matrices:

                @pl.when(here)
                def _():
                    transfer(matrices[0], inv_ref, low_jac, wait)

            first_copy.wait()
            write_faces(prev_ref, x_side, y_side, nz)

            def rest_of_copies():
                for z in range(nz):
                    wait(z)

            if matrices:

                @pl.when(jnp.logical_not(here))
                def _():
                    matrices[0][...] = jnp.zeros(matrix[0], F32)
                    rest_of_copies()

            else:
                rest_of_copies()

        def on(wanted, work):
            if wanted is None:
                work()
            else:
                pl.when(wanted(lax.axis_index("gz")))(work)

        def first_kernel(wanted, rhs_hbm, jac_hbm, prev_ref, inv_ref, low_jac, x_all, *rest):
            y_rows, outs = rest[: 1 if gy == 2 else 2], rest[-6:]
            on(
                wanted,
                lambda: first_work(
                    rhs_hbm, jac_hbm, prev_ref, inv_ref, low_jac, x_all, y_rows, *outs
                ),
            )

        def first_again_kernel(wanted, *refs):
            refs[-5][...] = refs[-9][...]
            first_kernel(wanted, *refs)

        def first_work(
            rhs_hbm, jac_hbm, prev_ref, inv_ref, low_jac, x_all, y_rows,
            source_ref, top_ref, sides, high_jac, rhs_ref, sems,
        ):
            halo = halo_reader(x_all, y_rows, gx, gy)

            def copies(z):
                return [
                    pltpu.make_async_copy(jac_hbm.at[z, 0:4], sides.at[z], sems.at[0, z]),
                    pltpu.make_async_copy(rhs_hbm.at[z], rhs_ref.at[z], sems.at[1, z]),
                ]

            def high_copy(z):
                return pltpu.make_async_copy(jac_hbm.at[z, 5], high_jac.at[z], sems.at[2, z])

            for z in range(nz):
                for copy in copies(z):
                    copy.start()
            for z in range(nz):
                high_copy(z).start()

            def step(z, earlier):
                for copy in copies(z):
                    copy.wait()
                results = []
                for tile, at in enumerate(spans):
                    lagged = inplane(sides, prev_ref, z, tile, tiles, halo)
                    source = [a - b for a, b in zip(planes_of(rhs_ref, z, at), lagged)]
                    for var in range(VARS):
                        source_ref[z, var, :, at] = source[var]
                    results.append(tuple(forward_plane(source, inv_ref, low_jac, z, at, earlier[tile])))
                return tuple(results)

            zero = tuple(jnp.zeros((ny, LANES), F32) for _ in range(VARS))
            top = lax.fori_loop(0, nz, step, (zero,) * tiles)
            for tile, at in enumerate(spans):
                put(top_ref, top[tile], at)
            for z in range(nz):
                high_copy(z).wait()

        def forward_kernel(source_ref, inv_ref, low_jac, *rest):
            came, top_ref = rest[:-1], rest[-1]
            starts = tuple(incoming(came, at) for at in spans)
            top = forward_sweep(source_ref, inv_ref, low_jac, starts)
            for tile, at in enumerate(spans):
                put(top_ref, top[tile], at)

        def forward_mid_kernel(low_ref, came_ref, source_ref, inv_ref, low_jac, top_ref):
            top_ref[...] = low_ref[...]

            @pl.when(lax.axis_index("gz") == 1)
            def _():
                forward_kernel(source_ref, inv_ref, low_jac, came_ref, top_ref)

        def either(device, work, fast):
            if fast is None:
                work(None)
                return
            here = lax.axis_index("gz") == device
            pl.when(here)(lambda: work(fast))
            pl.when(jnp.logical_not(here))(lambda: work(None))

        def forward_last_kernel(source_ref, prev_ref, inv_ref, low_jac, *rest):
            came, (sweep_ref, change_ref, x_side, y_side) = rest[:-4], rest[-4:]
            fast = None
            if short:
                first, near, matrix_ref, far, *fast = came

            def keep(z, at, result):
                before = planes_of(prev_ref, z, at)
                for var in range(VARS):
                    sweep_ref[z, var, :, at] = result[var]
                    change_ref[z, var, :, at] = result[var] - before[var]

            def work(fast):
                if short:
                    starts = tuple(arrived((first, near), matrix_ref, far, at) for at in spans)
                else:
                    starts = tuple(incoming(came, at) for at in spans)
                forward_sweep(source_ref, inv_ref, low_jac, starts, keep, fast)

            either(3, work, fast)
            write_faces(change_ref, x_side, y_side, nz)

        def turn_kernel(wanted, sweep_ref, change_ref, inv_ref, sides, high_jac, x_all, *rest):
            y_rows, outs = rest[: 1 if gy == 2 else 2], rest[-2:]
            on(
                wanted,
                lambda: turn_work(
                    sweep_ref, change_ref, inv_ref, sides, high_jac, x_all, y_rows, *outs
                ),
            )

        def turn_again_kernel(wanted, *refs):
            refs[-1][...] = refs[-3][...]
            turn_kernel(wanted, *refs)

        def turn_work(
            sweep_ref, change_ref, inv_ref, sides, high_jac, x_all, y_rows, inner_ref, low_ref
        ):
            halo = halo_reader(x_all, y_rows, gx, gy)
            for tile, at in enumerate(spans):

                def step(i, later, tile=tile, at=at):
                    z = nz - 1 - i
                    inner = inplane(sides, change_ref, z, tile, tiles, halo)
                    for var in range(VARS):
                        inner_ref[z, var, :, at] = inner[var]
                    sweep = planes_of(sweep_ref, z, at)
                    return tuple(backward_plane(sweep, inner, inv_ref, high_jac, z, at, later))

                zero = tuple(jnp.zeros((ny, LANES), F32) for _ in range(VARS))
                put(low_ref, lax.fori_loop(0, nz, step, zero), at)

        def only(device, work, ref, shape):
            here = lax.axis_index("gz") == device
            pl.when(here)(work)

            @pl.when(jnp.logical_not(here))
            def _():
                ref[...] = jnp.zeros(shape, F32)

        def down_matrix(inv_ref, high_jac, matrix_ref):
            transfer(matrix_ref, inv_ref, high_jac, lambda i: nz - 1 - i)

        def forward_idle_kernel(inv_ref, high_jac, low_jac, source_ref, _, matrix_ref, step_ref, plain_ref):
            only(2, lambda: down_matrix(inv_ref, high_jac, matrix_ref), matrix_ref, matrix[0])

            @pl.when(lax.axis_index("gz") == 3)
            def _():
                def plain_of(z, at, times):
                    return times(planes_of(source_ref, z, at))

                make_fast(step_ref, plain_ref, inv_ref, low_jac, plain_of)

        def backward_idle_kernel(inv_ref, high_jac, sweep_ref, inner_ref, _, matrix_ref, step_ref, plain_ref):
            only(1, lambda: down_matrix(inv_ref, high_jac, matrix_ref), matrix_ref, matrix[0])

            @pl.when(lax.axis_index("gz") == 0)
            def _():
                def plain_of(z, at, times):
                    moved = times(planes_of(inner_ref, z, at))
                    return [a - b for a, b in zip(planes_of(sweep_ref, z, at), moved)]

                make_fast(step_ref, plain_ref, inv_ref, high_jac, plain_of)

        def backward_kernel(sweep_ref, inner_ref, inv_ref, high_jac, *rest):
            came, low_ref = rest[:-1], rest[-1]
            starts = tuple(incoming(came, at) for at in spans)
            low = backward_sweep(sweep_ref, inner_ref, inv_ref, high_jac, starts)
            for tile, at in enumerate(spans):
                put(low_ref, low[tile], at)

        def pass_kernel(*refs):
            pass

        def far_kernel(far_ref, matrix_ref, _, moved_ref):
            for at in spans:
                put(moved_ref, apply_matrix(matrix_ref, planes_in(far_ref, at), at), at)

        def backward_mid_kernel(own_ref, near_ref, moved_ref, matrix_ref, came_ref, low_ref):
            for at in spans:
                came = incoming((near_ref, moved_ref), at)
                moved = apply_matrix(matrix_ref, came, at)
                put(came_ref, came, at)
                put(low_ref, [a + b for a, b in zip(planes_in(own_ref, at), moved)], at)

        def update_kernel(sweep_ref, inner_ref, inv_ref, high_jac, *rest):
            came, (out_hbm, held, sems) = rest[:-3], rest[-3:]
            fast = None
            if short:
                came, fast = came[:2], came[2:]

            def out_copy(z):
                return pltpu.make_async_copy(held.at[z], out_hbm.at[z], sems.at[z])

            def keep(z, tile, at, result):
                for var in range(VARS):
                    held[z, var, :, at] = result[var]
                if tile == tiles - 1:
                    out_copy(z).start()

            def work(fast):
                starts = tuple(incoming(came, at) for at in spans)
                backward_sweep(sweep_ref, inner_ref, inv_ref, high_jac, starts, keep, fast)

            either(0, work, fast)
            for z in range(nz):
                out_copy(z).wait()


        prev, inv, low_jac, x_side, y_side, *up_matrix = call(
            open_kernel,
            [volume, blocks, blocks, x_face, y_face] + [matrix] * (1 if short else 0),
            prev,
            inv,
            jac,
            cost=12 * unit,
            in_hbm=(0, 1, 2),
            scratch=[pltpu.SemaphoreType.DMA, pltpu.SemaphoreType.DMA((2, nz))],
        )
        if short:
            up_there = lax.ppermute(up_matrix[0], "gz", [(2, 3)])
        halo = exchange(x_side, y_side)
        ahead, behind = None, None
        if short:
            ahead, behind = (lambda device: device == 0), (lambda device: device != 0)
        first_args = [rhs, jac, prev, inv, low_jac, *halo]
        first_options = dict(
            cost=unit // 8,
            in_hbm=(0, 1),
            scratch=[pltpu.VMEM(rhs.shape, F32), pltpu.SemaphoreType.DMA((3, nz))],
        )
        first_outs = [volume, plane, side_blocks, blocks]
        source, top, sides, high_jac = call(
            functools.partial(first_kernel, ahead), first_outs, *first_args, **first_options
        )
        if short:
            first = lax.ppermute(top, "gz", [(0, 1)])
            n = len(first_args)
            source, top, sides, high_jac = call(
                functools.partial(first_again_kernel, behind),
                first_outs,
                *first_args,
                source,
                top,
                sides,
                high_jac,
                aliases={n: 0, n + 2: 2, n + 3: 3},
                **first_options,
            )
            (top,) = call(
                forward_mid_kernel,
                [plane],
                top,
                first,
                source,
                inv,
                low_jac,
                cost=unit // 8,
            )
            far = lax.ppermute(top, "gz", [(1, 3)])
            near = lax.ppermute(top, "gz", [(1, 2), (2, 3)])
            down_one, *fast = call(
                forward_idle_kernel,
                [matrix, steps, volume],
                inv,
                high_jac,
                low_jac,
                source,
                up_there,
                cost=unit // 8,
            )
            (down_one,) = call(
                pass_kernel, [matrix], down_one, near, far, cost=unit // 8, aliases={0: 0}
            )
            down_there = lax.ppermute(down_one, "gz", [(2, 1)])
            came = [first, near, up_there, far, *fast]
        else:
            came = []
            for hop in range(gz - 1):
                if hop:
                    (top,) = call(
                        forward_kernel, [plane], source, inv, low_jac, *came, cost=3 * unit
                    )
                came.append(lax.ppermute(top, "gz", [(hop, hop + 1)]))
        sweep, change, x_side, y_side = call(
            forward_last_kernel,
            [volume, volume, x_face, y_face],
            source,
            prev,
            inv,
            low_jac,
            *came,
            cost=4 * unit,
        )
        halo = exchange(x_side, y_side)
        if short:
            ahead, behind = (lambda device: device == 3), (lambda device: device != 3)
        turn_args = [sweep, change, inv, sides, high_jac, *halo]
        inner, low = call(
            functools.partial(turn_kernel, ahead), [volume, plane], *turn_args, cost=11 * unit
        )
        if short:
            ahead_low = low
            inner, low = call(
                functools.partial(turn_again_kernel, behind),
                [volume, plane],
                *turn_args,
                inner,
                low,
                aliases={len(turn_args): 0},
                cost=unit // 8,
            )
            near = lax.ppermute(low, "gz", [(3, 2), (2, 1)])
            far = lax.ppermute(ahead_low, "gz", [(3, 1)])
            own_matrix, *fast = call(
                backward_idle_kernel,
                [matrix, steps, volume],
                inv,
                high_jac,
                sweep,
                inner,
                low,
                cost=unit // 8,
            )
            (moved,) = call(far_kernel, [plane], far, down_there, own_matrix, cost=unit // 8)
            entered, low = call(
                backward_mid_kernel, [plane, plane], low, near, moved, own_matrix, cost=unit // 8
            )
            came = [entered, lax.ppermute(low, "gz", [(1, 0)]), *fast]
        else:
            came = []
            for hop in range(gz - 1, 0, -1):
                if came:
                    (low,) = call(
                        backward_kernel, [plane], sweep, inner, inv, high_jac, *came, cost=3 * unit
                    )
                came.append(lax.ppermute(low, "gz", [(hop, hop - 1)]))
        (update,) = call(
            update_kernel,
            [volume],
            sweep,
            inner,
            inv,
            high_jac,
            *came,
            cost=5 * unit,
            out_hbm=(0,),
            scratch=[pltpu.VMEM(volume[0], F32), pltpu.SemaphoreType.DMA((nz,))],
        )
        return jnp.transpose(update, (0, 2, 1, 3))

    placed = (
        P("gz", "gy", None, "gx"),
        P("gz", "gy", None, "gx"),
        P("gz", "gy", None, None, "gx"),
        P("gz", "gy", None, None, None, "gx"),
    )
    return jax.shard_map(
        body, mesh=mesh, in_specs=placed, out_specs=P("gz", "gy", None, "gx"), check_vma=False
    )
```

```python
import functools

import jax
import jax.numpy as jnp
from jax import lax
from jax.experimental import pallas as pl
from jax.experimental.pallas import tpu as pltpu
from jax.sharding import PartitionSpec as P

VARS = 6
LANES = 128
F32 = jnp.float32
WHOLE = pl.BlockSpec(memory_space=pltpu.VMEM)


def call(body, outs, *args, cost, limit=16 << 20, scratch=(), in_hbm=(), out_hbm=(), aliases={}):
    far = pl.BlockSpec(memory_space=pl.ANY)
    shapes = [
        jax.ShapeDtypeStruct(o[0], o[1]) if i in out_hbm else pltpu.VMEM(o[0], o[1])
        for i, o in enumerate(outs)
    ]
    return pl.pallas_call(
        body,
        out_shape=shapes,
        in_specs=[far if i in in_hbm else WHOLE for i in range(len(args))],
        out_specs=[far if i in out_hbm else WHOLE for i in range(len(outs))],
        scratch_shapes=scratch,
        input_output_aliases=aliases,
        cost_estimate=pl.CostEstimate(flops=0, bytes_accessed=cost, transcendentals=0),
        compiler_params=pltpu.CompilerParams(vmem_limit_bytes=limit),
    )(*[
        pltpu.with_memory_space_constraint(a, pltpu.HBM if i in in_hbm else pltpu.VMEM)
        for i, a in enumerate(args)
    ])


def lane_iota(rows):
    return lax.broadcasted_iota(jnp.int32, (rows, LANES), 1)


def row_iota(rows):
    return lax.broadcasted_iota(jnp.int32, (rows, LANES), 0)


def dot6(blocks, values):
    terms = [b.astype(F32) * v for b, v in zip(blocks, values)]
    return (terms[0] + terms[1]) + (terms[2] + terms[3]) + (terms[4] + terms[5])


def block(ref, *index, at):
    return lambda r, c: ref[(*index, r, c, slice(None), at)]


def apply_block(get, values):
    return [dot6([get(r, c) for c in range(VARS)], values) for r in range(VARS)]


def write_faces(value, x_face, y_face, z_count):
    y_count = value.shape[2]
    x_count = value.shape[3]
    lane = lane_iota(y_count)
    for group in range(x_face.shape[1]):
        faces = []
        for start, source_lane in ((0, 0), (x_count - LANES, LANES - 1)):
            held = jnp.zeros((y_count, LANES), F32)
            for slot in range(min(LANES, z_count * VARS - group * LANES)):
                z, var = divmod(group * LANES + slot, VARS)
                tile = value[z, var, :, start : start + LANES]
                moved = pltpu.roll(tile, (slot - source_lane) % LANES, 1)
                held = jnp.where(lane == slot, moved, held)
            faces.append(held)
        x_face[0, group], x_face[1, group] = faces
    if y_face.shape[0] == 1:
        first = lax.axis_index("gy") == 0
        for z in range(z_count):
            for var in range(VARS):
                low = value[z, var, 0:1, :]
                high = value[z, var, y_count - 1 : y_count, :]
                y_face[0, z, var : var + 1, :] = jnp.where(first, high, low)
    else:
        for z in range(z_count):
            for var in range(VARS):
                y_face[0, z, var : var + 1, :] = value[z, var, 0:1, :]
                y_face[1, z, var : var + 1, :] = value[z, var, y_count - 1 : y_count, :]


def halo_reader(x_all, y_rows, gx, gy):
    me_x = lax.axis_index("gx")

    def column(there, side, to_lane):
        exists = (there >= 0) & (there < gx)
        device = jnp.clip(there, 0, gx - 1)

        def read(z, var):
            j = z * VARS + var
            face = x_all[device, side, j // LANES]
            moved = pltpu.roll(face, (to_lane + LANES - j % LANES) % LANES, 1)
            return jnp.where(exists, moved, jnp.zeros_like(moved))

        return read

    def row(which):
        def read(z, var, at):
            if len(y_rows) > 1:
                return y_rows[which][z, var : var + 1, at]
            here = y_rows[0][z, var : var + 1, at]
            return jnp.where(lax.axis_index("gy") == 1 - which, here, jnp.zeros_like(here))

        return read

    return column(me_x - 1, 1, 0), column(me_x + 1, 0, LANES - 1), row(0), row(1)


def neighbours(value, z, tile, tiles, halo):
    y_count = value.shape[2]
    lane = lane_iota(y_count)
    row = row_iota(y_count)
    at = slice(tile * LANES, (tile + 1) * LANES)
    result = ([], [], [], [])
    for var in range(VARS):
        here = value[z, var, :, at]
        if tile > 0:
            before = pltpu.roll(value[z, var, :, at.start - LANES : at.start], 1, 1)
        else:
            before = halo[0](z, var)
        if tile < tiles - 1:
            after = pltpu.roll(value[z, var, :, at.stop : at.stop + LANES], LANES - 1, 1)
        else:
            after = halo[1](z, var)
        result[0].append(jnp.where(lane == 0, before, pltpu.roll(here, 1, 1)))
        result[1].append(jnp.where(lane == LANES - 1, after, pltpu.roll(here, LANES - 1, 1)))
        result[2].append(jnp.where(row == 0, halo[2](z, var, at), pltpu.roll(here, 1, 0)))
        result[3].append(
            jnp.where(row == y_count - 1, halo[3](z, var, at), pltpu.roll(here, y_count - 1, 0))
        )
    return result


def inplane(jacobians, value, z, tile, tiles, halo):
    at = slice(tile * LANES, (tile + 1) * LANES)
    total = None
    for n, values in enumerate(neighbours(value, z, tile, tiles, halo)):
        part = apply_block(block(jacobians, z, n, at=at), values)
        total = part if total is None else [a + b for a, b in zip(total, part)]
    return total


def planes_of(ref, z, at):
    return [ref[z, var, :, at] for var in range(VARS)]


def solution(mesh):
    gz, gx, gy = (mesh.shape[a] for a in ("gz", "gx", "gy"))
    short = gz == 4

    def body(right_side, previous, diag_inverse, jacobians):
        rhs = jnp.transpose(right_side, (0, 2, 1, 3))
        prev = jnp.transpose(previous, (0, 2, 1, 3))
        inv = jnp.transpose(diag_inverse, (0, 2, 3, 1, 4))
        jac = jnp.transpose(jacobians, (0, 2, 3, 4, 1, 5))
        nz, _, ny, nx = rhs.shape
        tiles = nx // LANES
        assert nx % LANES == 0
        spans = [slice(t * LANES, (t + 1) * LANES) for t in range(tiles)]
        plane = ((VARS, ny, nx), F32)
        volume = ((nz, VARS, ny, nx), F32)
        x_groups = -(-nz * VARS // LANES)
        x_face = ((2, x_groups, ny, LANES), F32)
        y_face = ((1 if gy == 2 else 2, nz, VARS, nx), F32)
        matrix = ((VARS, VARS, ny, nx), F32)
        steps = ((nz, VARS, VARS, ny, nx), F32)
        blocks = ((nz, VARS, VARS, ny, nx), jac.dtype)
        side_blocks = ((nz, 4, VARS, VARS, ny, nx), jac.dtype)
        unit = 40 * nz * ny * nx

        def exchange(x_side, y_side):
            if gy == 2:
                rows = [lax.ppermute(y_side[0], "gy", [(0, 1), (1, 0)])]
            else:
                up = [(i, i + 1) for i in range(gy - 1)]
                rows = [
                    lax.ppermute(y_side[1], "gy", up),
                    lax.ppermute(y_side[0], "gy", [(j, i) for i, j in up]),
                ]
            return lax.all_gather(x_side, "gx"), *rows


        def forward_plane(source, inv_ref, low_jac, z, at, earlier):
            lagged = apply_block(block(low_jac, z, at=at), earlier)
            return apply_block(block(inv_ref, z, at=at), [a - b for a, b in zip(source, lagged)])

        def backward_plane(sweep, inner, inv_ref, high_jac, z, at, later):
            change = apply_block(block(high_jac, z, at=at), later)
            change = apply_block(block(inv_ref, z, at=at), [a + b for a, b in zip(change, inner)])
            return [a - b for a, b in zip(sweep, change)]

        def fast_plane(step_ref, plain_ref, z, at, before):
            moved = apply_block(block(step_ref, z, at=at), before)
            return [a + b for a, b in zip(planes_of(plain_ref, z, at), moved)]

        def make_fast(step_ref, plain_ref, inv_ref, couple_ref, plain_of):
            half = VARS // 2

            def step(z, carry):
                for at in spans:
                    couple, inverse = block(couple_ref, z, at=at), block(inv_ref, z, at=at)
                    for g in range(VARS // half):
                        columns = range(g * half, (g + 1) * half)
                        held = [[couple(k, c).astype(F32) for k in range(VARS)] for c in columns]
                        for r in range(VARS):
                            row = [inverse(r, k).astype(F32) for k in range(VARS)]
                            for i, c in enumerate(columns):
                                step_ref[z, r, c, :, at] = -dot6(row, held[i])
                    plain = plain_of(z, at, lambda values: apply_block(inverse, values))
                    for var in range(VARS):
                        plain_ref[z, var, :, at] = plain[var]
                return carry

            lax.fori_loop(0, nz, step, 0)

        def put(ref, values, at):
            for var in range(VARS):
                ref[var, :, at] = values[var]

        def incoming(refs, at):
            total = [refs[0][var, :, at] for var in range(VARS)]
            for ref in refs[1:]:
                total = [a + ref[var, :, at] for var, a in enumerate(total)]
            return tuple(total)

        def planes_in(ref, at):
            return [ref[var, :, at] for var in range(VARS)]

        def apply_matrix(matrix_ref, vector, at):
            return apply_block(block(matrix_ref, at=at), vector)

        def arrived(plain, matrix_ref, vector_ref, at):
            total = apply_matrix(matrix_ref, [vector_ref[var, :, at] for var in range(VARS)], at)
            for ref in plain:
                total = [a + ref[var, :, at] for var, a in enumerate(total)]
            return tuple(total)

        def forward_sweep(source_ref, inv_ref, low_jac, starts, keep=None, fast=None):
            def step(z, earlier):
                results = []
                for tile, at in enumerate(spans):
                    if fast is not None:
                        result = fast_plane(*fast, z, at, earlier[tile])
                    else:
                        source = planes_of(source_ref, z, at)
                        result = forward_plane(source, inv_ref, low_jac, z, at, earlier[tile])
                    if keep is not None:
                        keep(z, at, result)
                    results.append(tuple(result))
                return tuple(results)

            return lax.fori_loop(0, nz, step, starts)

        def backward_sweep(sweep_ref, inner_ref, inv_ref, high_jac, starts, keep=None, fast=None):
            def step(i, later):
                z = nz - 1 - i
                results = []
                for tile, at in enumerate(spans):
                    if fast is not None:
                        result = fast_plane(*fast, z, at, later[tile])
                    else:
                        sweep, inner = planes_of(sweep_ref, z, at), planes_of(inner_ref, z, at)
                        result = backward_plane(sweep, inner, inv_ref, high_jac, z, at, later[tile])
                    if keep is not None:
                        keep(z, tile, at, result)
                    results.append(tuple(result))
                return tuple(results)

            return lax.fori_loop(0, nz, step, starts)

        def transfer(matrix_ref, inv_ref, couple_ref, wait):
            half = VARS // 2
            groups = [range(g * half, (g + 1) * half) for g in range(VARS // half)]

            def plane_step(z, at, group, vectors):
                couple, inverse = block(couple_ref, z, at=at), block(inv_ref, z, at=at)
                middle = [[] for _ in group]
                for r in range(VARS):
                    row = [couple(r, c).astype(F32) for c in range(VARS)]
                    for i in range(len(group)):
                        middle[i].append(row[group[i]] if vectors is None else dot6(row, vectors[i]))
                for r in range(VARS):
                    row = [inverse(r, c).astype(F32) for c in range(VARS)]
                    for i, c in enumerate(group):
                        matrix_ref[r, c, :, at] = -dot6(row, middle[i])

            def step(i, carry):
                z = wait(i)
                for at in spans:
                    for group in groups:
                        vectors = [[matrix_ref[r, c, :, at] for r in range(VARS)] for c in group]
                        plane_step(z, at, group, vectors)
                return carry

            z = wait(0)
            for at in spans:
                for group in groups:
                    plane_step(z, at, group, None)
            lax.fori_loop(1, nz, step, 0)


        def open_kernel(prev_hbm, inv_hbm, jac_hbm, *rest):
            prev_ref, inv_ref, low_jac, x_side, y_side, *matrices, sem, sems = rest

            def copies(z):
                return [
                    pltpu.make_async_copy(inv_hbm.at[z], inv_ref.at[z], sems.at[0, z]),
                    pltpu.make_async_copy(jac_hbm.at[z, 4], low_jac.at[z], sems.at[1, z]),
                ]

            def wait(z):
                for copy in copies(z):
                    copy.wait()
                return z

            first_copy = pltpu.make_async_copy(prev_hbm, prev_ref, sem)
            first_copy.start()
            for z in range(nz):
                for copy in copies(z):
                    copy.start()
            here = lax.axis_index("gz") == 2
            if matrices:

                @pl.when(here)
                def _():
                    transfer(matrices[0], inv_ref, low_jac, wait)

            first_copy.wait()
            write_faces(prev_ref, x_side, y_side, nz)

            def rest_of_copies():
                for z in range(nz):
                    wait(z)

            if matrices:

                @pl.when(jnp.logical_not(here))
                def _():
                    matrices[0][...] = jnp.zeros(matrix[0], F32)
                    rest_of_copies()

            else:
                rest_of_copies()

        def on(wanted, work):
            if wanted is None:
                work()
            else:
                pl.when(wanted(lax.axis_index("gz")))(work)

        def load_high(jac_hbm, high_jac, sem):
            return pltpu.make_async_copy(jac_hbm.at[:, 5], high_jac, sem)

        def first_kernel(rhs_hbm, jac_hbm, prev_ref, inv_ref, low_jac, x_all, *rest):
            *y_rows, source_ref, top_ref, sides, high_jac, rhs_ref, sems, high_sem = rest
            high_copy = load_high(jac_hbm, high_jac, high_sem)
            first_work(
                rhs_hbm, jac_hbm, prev_ref, inv_ref, low_jac, x_all, y_rows,
                source_ref, top_ref, sides, rhs_ref, sems, high_copy,
            )
            high_copy.wait()

        def first_ahead_kernel(rhs_hbm, jac_hbm, prev_ref, inv_ref, low_jac, x_all, *rest):
            *y_rows, source_ref, top_ref, sides, rhs_ref, sems = rest

            @pl.when(lax.axis_index("gz") == 0)
            def _():
                first_work(
                    rhs_hbm, jac_hbm, prev_ref, inv_ref, low_jac, x_all, y_rows,
                    source_ref, top_ref, sides, rhs_ref, sems, None,
                )

        def first_behind_kernel(*refs):
            jac_hbm, high_jac, high_sem = refs[1], refs[-4], refs[-1]
            inputs, top_before = refs[: len(first_args)], refs[len(first_args) + 1]
            source_ref, top_ref, sides, _, rhs_ref, sems, _ = refs[-7:]
            high_copy = load_high(jac_hbm, high_jac, high_sem)
            here = lax.axis_index("gz") == 0

            @pl.when(here)
            def _():
                high_copy.start()
                top_ref[...] = top_before[...]

            @pl.when(jnp.logical_not(here))
            def _():
                first_work(
                    *inputs[:6], inputs[6:], source_ref, top_ref, sides, rhs_ref, sems, high_copy
                )

            high_copy.wait()

        def first_work(
            rhs_hbm, jac_hbm, prev_ref, inv_ref, low_jac, x_all, y_rows,
            source_ref, top_ref, sides, rhs_ref, sems, also,
        ):
            halo = halo_reader(x_all, y_rows, gx, gy)

            def copies(z):
                return [
                    pltpu.make_async_copy(jac_hbm.at[z, 0:4], sides.at[z], sems.at[0, z]),
                    pltpu.make_async_copy(rhs_hbm.at[z], rhs_ref.at[z], sems.at[1, z]),
                ]

            for z in range(nz):
                for copy in copies(z):
                    copy.start()
            if also is not None:
                also.start()

            def step(z, earlier):
                for copy in copies(z):
                    copy.wait()
                results = []
                for tile, at in enumerate(spans):
                    lagged = inplane(sides, prev_ref, z, tile, tiles, halo)
                    source = [a - b for a, b in zip(planes_of(rhs_ref, z, at), lagged)]
                    for var in range(VARS):
                        source_ref[z, var, :, at] = source[var]
                    results.append(tuple(forward_plane(source, inv_ref, low_jac, z, at, earlier[tile])))
                return tuple(results)

            zero = tuple(jnp.zeros((ny, LANES), F32) for _ in range(VARS))
            top = lax.fori_loop(0, nz, step, (zero,) * tiles)
            for tile, at in enumerate(spans):
                put(top_ref, top[tile], at)

        def forward_kernel(source_ref, inv_ref, low_jac, *rest):
            came, top_ref = rest[:-1], rest[-1]
            starts = tuple(incoming(came, at) for at in spans)
            top = forward_sweep(source_ref, inv_ref, low_jac, starts)
            for tile, at in enumerate(spans):
                put(top_ref, top[tile], at)

        def forward_mid_kernel(low_ref, came_ref, source_ref, inv_ref, low_jac, top_ref):
            here = lax.axis_index("gz") == 1
            pl.when(here)(lambda: forward_kernel(source_ref, inv_ref, low_jac, came_ref, top_ref))

            @pl.when(jnp.logical_not(here))
            def _():
                top_ref[...] = low_ref[...]

        def either(device, work, fast):
            if fast is None:
                work(None)
                return
            here = lax.axis_index("gz") == device
            pl.when(here)(lambda: work(fast))
            pl.when(jnp.logical_not(here))(lambda: work(None))

        def forward_last_kernel(source_ref, prev_ref, inv_ref, low_jac, *rest):
            came, (sweep_ref, change_ref, x_side, y_side) = rest[:-4], rest[-4:]
            fast = None
            if short:
                first, far, third, matrix_ref, near, *fast = came

            def keep(z, at, result):
                before = planes_of(prev_ref, z, at)
                for var in range(VARS):
                    sweep_ref[z, var, :, at] = result[var]
                    change_ref[z, var, :, at] = result[var] - before[var]

            def work(fast):
                if short:
                    starts = tuple(
                        arrived((first, near, third), matrix_ref, far, at) for at in spans
                    )
                else:
                    starts = tuple(incoming(came, at) for at in spans)
                forward_sweep(source_ref, inv_ref, low_jac, starts, keep, fast)

            either(3, work, fast)
            write_faces(change_ref, x_side, y_side, nz)

        def turn_kernel(wanted, sweep_ref, change_ref, inv_ref, sides, high_jac, x_all, *rest):
            y_rows, outs = rest[: 1 if gy == 2 else 2], rest[-2:]
            on(
                wanted,
                lambda: turn_work(
                    sweep_ref, change_ref, inv_ref, sides, high_jac, x_all, y_rows, *outs
                ),
            )

        def turn_again_kernel(wanted, *refs):
            refs[-1][...] = refs[-3][...]
            turn_kernel(wanted, *refs)

        def turn_work(
            sweep_ref, change_ref, inv_ref, sides, high_jac, x_all, y_rows, inner_ref, low_ref
        ):
            halo = halo_reader(x_all, y_rows, gx, gy)
            for tile, at in enumerate(spans):

                def step(i, later, tile=tile, at=at):
                    z = nz - 1 - i
                    inner = inplane(sides, change_ref, z, tile, tiles, halo)
                    for var in range(VARS):
                        inner_ref[z, var, :, at] = inner[var]
                    sweep = planes_of(sweep_ref, z, at)
                    return tuple(backward_plane(sweep, inner, inv_ref, high_jac, z, at, later))

                zero = tuple(jnp.zeros((ny, LANES), F32) for _ in range(VARS))
                put(low_ref, lax.fori_loop(0, nz, step, zero), at)

        def only(device, work, ref, shape):
            here = lax.axis_index("gz") == device
            pl.when(here)(work)

            @pl.when(jnp.logical_not(here))
            def _():
                ref[...] = jnp.zeros(shape, F32)

        def down_matrix(inv_ref, high_jac, matrix_ref):
            transfer(matrix_ref, inv_ref, high_jac, lambda i: nz - 1 - i)

        def forward_idle_kernel(inv_ref, high_jac, low_jac, source_ref, _, matrix_ref, step_ref, plain_ref):
            only(2, lambda: down_matrix(inv_ref, high_jac, matrix_ref), matrix_ref, matrix[0])

            @pl.when(lax.axis_index("gz") == 3)
            def _():
                def plain_of(z, at, times):
                    return times(planes_of(source_ref, z, at))

                make_fast(step_ref, plain_ref, inv_ref, low_jac, plain_of)

        def backward_idle_kernel(inv_ref, high_jac, sweep_ref, inner_ref, _, matrix_ref, step_ref, plain_ref):
            only(1, lambda: down_matrix(inv_ref, high_jac, matrix_ref), matrix_ref, matrix[0])

            @pl.when(lax.axis_index("gz") == 0)
            def _():
                def plain_of(z, at, times):
                    moved = times(planes_of(inner_ref, z, at))
                    return [a - b for a, b in zip(planes_of(sweep_ref, z, at), moved)]

                make_fast(step_ref, plain_ref, inv_ref, high_jac, plain_of)

        def backward_kernel(sweep_ref, inner_ref, inv_ref, high_jac, *rest):
            came, low_ref = rest[:-1], rest[-1]
            starts = tuple(incoming(came, at) for at in spans)
            low = backward_sweep(sweep_ref, inner_ref, inv_ref, high_jac, starts)
            for tile, at in enumerate(spans):
                put(low_ref, low[tile], at)

        def pass_kernel(*refs):
            pass

        def far_kernel(far_ref, matrix_ref, _, moved_ref):
            for at in spans:
                put(moved_ref, apply_matrix(matrix_ref, planes_in(far_ref, at), at), at)

        def backward_mid_kernel(own_ref, near_ref, moved_ref, matrix_ref, came_ref, low_ref):
            for at in spans:
                came = incoming((near_ref, moved_ref), at)
                moved = apply_matrix(matrix_ref, came, at)
                put(came_ref, came, at)
                put(low_ref, [a + b for a, b in zip(planes_in(own_ref, at), moved)], at)

        def update_kernel(sweep_ref, inner_ref, inv_ref, high_jac, *rest):
            came, (out_hbm, held, sems) = rest[:-3], rest[-3:]
            fast = None
            if short:
                came, fast = came[:2], came[2:]

            def out_copy(z):
                return pltpu.make_async_copy(held.at[z], out_hbm.at[z], sems.at[z])

            def keep(z, tile, at, result):
                for var in range(VARS):
                    held[z, var, :, at] = result[var]
                if tile == tiles - 1:
                    out_copy(z).start()

            def work(fast):
                starts = tuple(incoming(came, at) for at in spans)
                backward_sweep(sweep_ref, inner_ref, inv_ref, high_jac, starts, keep, fast)

            either(0, work, fast)
            for z in range(nz):
                out_copy(z).wait()


        prev, inv, low_jac, x_side, y_side, *up_matrix = call(
            open_kernel,
            [volume, blocks, blocks, x_face, y_face] + [matrix] * (1 if short else 0),
            prev,
            inv,
            jac,
            cost=12 * unit,
            in_hbm=(0, 1, 2),
            scratch=[pltpu.SemaphoreType.DMA, pltpu.SemaphoreType.DMA((2, nz))],
        )
        if short:
            up_there = lax.ppermute(up_matrix[0], "gz", [(2, 3)])
        halo = exchange(x_side, y_side)
        first_args = [rhs, jac, prev, inv, low_jac, *halo]
        first_scratch = [pltpu.VMEM(rhs.shape, F32), pltpu.SemaphoreType.DMA((2, nz))]
        if short:
            source, top, sides = call(
                first_ahead_kernel,
                [volume, plane, side_blocks],
                *first_args,
                cost=unit // 8,
                in_hbm=(0, 1),
                scratch=first_scratch,
            )
            first = lax.ppermute(top, "gz", [(0, 1)])
            n = len(first_args)
            source, top, sides, high_jac = call(
                first_behind_kernel,
                [volume, plane, side_blocks, blocks],
                *first_args,
                source,
                top,
                sides,
                cost=unit // 8,
                in_hbm=(0, 1),
                aliases={n: 0, n + 2: 2},
                scratch=first_scratch + [pltpu.SemaphoreType.DMA],
            )
            third = lax.ppermute(top, "gz", [(2, 3)])
            (top,) = call(
                forward_mid_kernel, [plane], top, first, source, inv, low_jac, cost=unit // 8
            )
            near = lax.ppermute(top, "gz", [(1, 2)])
            far = lax.ppermute(top, "gz", [(1, 3)])
            down_one, *fast = call(
                forward_idle_kernel,
                [matrix, steps, volume],
                inv,
                high_jac,
                low_jac,
                source,
                up_there,
                cost=unit // 8,
            )
            (down_one,) = call(
                pass_kernel, [matrix], down_one, far, near, third, cost=unit // 8, aliases={0: 0}
            )
            down_there = lax.ppermute(down_one, "gz", [(2, 1)])
            came = [first, far, third, up_there, near, *fast]
        else:
            source, top, sides, high_jac = call(
                first_kernel,
                [volume, plane, side_blocks, blocks],
                *first_args,
                cost=14 * unit,
                in_hbm=(0, 1),
                scratch=first_scratch + [pltpu.SemaphoreType.DMA],
            )
            came = []
            for hop in range(gz - 1):
                if hop:
                    (top,) = call(
                        forward_kernel, [plane], source, inv, low_jac, *came, cost=3 * unit
                    )
                came.append(lax.ppermute(top, "gz", [(hop, hop + 1)]))
        sweep, change, x_side, y_side = call(
            forward_last_kernel,
            [volume, volume, x_face, y_face],
            source,
            prev,
            inv,
            low_jac,
            *came,
            cost=4 * unit,
        )
        halo = exchange(x_side, y_side)
        if short:
            ahead, behind = (lambda device: device == 3), (lambda device: device != 3)
        turn_args = [sweep, change, inv, sides, high_jac, *halo]
        inner, low = call(
            functools.partial(turn_kernel, ahead), [volume, plane], *turn_args, cost=11 * unit
        )
        if short:
            ahead_low = low
            inner, low = call(
                functools.partial(turn_again_kernel, behind),
                [volume, plane],
                *turn_args,
                inner,
                low,
                aliases={len(turn_args): 0},
                cost=unit // 8,
            )
            near = lax.ppermute(low, "gz", [(3, 2), (2, 1)])
            far = lax.ppermute(ahead_low, "gz", [(3, 1)])
            own_matrix, *fast = call(
                backward_idle_kernel,
                [matrix, steps, volume],
                inv,
                high_jac,
                sweep,
                inner,
                low,
                cost=unit // 8,
            )
            (moved,) = call(far_kernel, [plane], far, down_there, own_matrix, cost=unit // 8)
            entered, low = call(
                backward_mid_kernel, [plane, plane], low, near, moved, own_matrix, cost=unit // 8
            )
            came = [entered, lax.ppermute(low, "gz", [(1, 0)]), *fast]
        else:
            came = []
            for hop in range(gz - 1, 0, -1):
                if came:
                    (low,) = call(
                        backward_kernel, [plane], sweep, inner, inv, high_jac, *came, cost=3 * unit
                    )
                came.append(lax.ppermute(low, "gz", [(hop, hop - 1)]))
        (update,) = call(
            update_kernel,
            [volume],
            sweep,
            inner,
            inv,
            high_jac,
            *came,
            cost=5 * unit,
            out_hbm=(0,),
            scratch=[pltpu.VMEM(volume[0], F32), pltpu.SemaphoreType.DMA((nz,))],
        )
        return jnp.transpose(update, (0, 2, 1, 3))

    placed = (
        P("gz", "gy", None, "gx"),
        P("gz", "gy", None, "gx"),
        P("gz", "gy", None, None, "gx"),
        P("gz", "gy", None, None, None, "gx"),
    )
    return jax.shard_map(
        body, mesh=mesh, in_specs=placed, out_specs=P("gz", "gy", None, "gx"), check_vma=False
    )
```

```python
import functools

import jax
import jax.numpy as jnp
from jax import lax
from jax.experimental import pallas as pl
from jax.experimental.pallas import tpu as pltpu
from jax.sharding import PartitionSpec as P

VARS = 6
LANES = 128
F32 = jnp.float32
WHOLE = pl.BlockSpec(memory_space=pltpu.VMEM)


def call(body, outs, *args, cost, limit=16 << 20, scratch=(), in_hbm=(), out_hbm=(), aliases={}):
    far = pl.BlockSpec(memory_space=pl.ANY)
    shapes = [
        jax.ShapeDtypeStruct(o[0], o[1]) if i in out_hbm else pltpu.VMEM(o[0], o[1])
        for i, o in enumerate(outs)
    ]
    return pl.pallas_call(
        body,
        out_shape=shapes,
        in_specs=[far if i in in_hbm else WHOLE for i in range(len(args))],
        out_specs=[far if i in out_hbm else WHOLE for i in range(len(outs))],
        scratch_shapes=scratch,
        input_output_aliases=aliases,
        cost_estimate=pl.CostEstimate(flops=0, bytes_accessed=cost, transcendentals=0),
        compiler_params=pltpu.CompilerParams(vmem_limit_bytes=limit),
    )(*[
        pltpu.with_memory_space_constraint(a, pltpu.HBM if i in in_hbm else pltpu.VMEM)
        for i, a in enumerate(args)
    ])


def lane_iota(rows):
    return lax.broadcasted_iota(jnp.int32, (rows, LANES), 1)


def row_iota(rows):
    return lax.broadcasted_iota(jnp.int32, (rows, LANES), 0)


def dot6(blocks, values):
    terms = [b.astype(F32) * v for b, v in zip(blocks, values)]
    return (terms[0] + terms[1]) + (terms[2] + terms[3]) + (terms[4] + terms[5])


def block(ref, *index, at):
    return lambda r, c: ref[(*index, r, c, slice(None), at)]


def apply_block(get, values):
    return [dot6([get(r, c) for c in range(VARS)], values) for r in range(VARS)]


def write_faces(value, x_face, y_face, z_count):
    y_count = value.shape[2]
    x_count = value.shape[3]
    lane = lane_iota(y_count)
    for group in range(x_face.shape[1]):
        faces = []
        for start, source_lane in ((0, 0), (x_count - LANES, LANES - 1)):
            held = jnp.zeros((y_count, LANES), F32)
            for slot in range(min(LANES, z_count * VARS - group * LANES)):
                z, var = divmod(group * LANES + slot, VARS)
                tile = value[z, var, :, start : start + LANES]
                moved = pltpu.roll(tile, (slot - source_lane) % LANES, 1)
                held = jnp.where(lane == slot, moved, held)
            faces.append(held)
        x_face[0, group], x_face[1, group] = faces
    if y_face.shape[0] == 1:
        first = lax.axis_index("gy") == 0
        for z in range(z_count):
            for var in range(VARS):
                low = value[z, var, 0:1, :]
                high = value[z, var, y_count - 1 : y_count, :]
                y_face[0, z, var : var + 1, :] = jnp.where(first, high, low)
    else:
        for z in range(z_count):
            for var in range(VARS):
                y_face[0, z, var : var + 1, :] = value[z, var, 0:1, :]
                y_face[1, z, var : var + 1, :] = value[z, var, y_count - 1 : y_count, :]


def halo_reader(x_all, y_rows, gx, gy):
    me_x = lax.axis_index("gx")

    def column(there, side, to_lane):
        exists = (there >= 0) & (there < gx)
        device = jnp.clip(there, 0, gx - 1)

        def read(z, var):
            j = z * VARS + var
            face = x_all[device, side, j // LANES]
            moved = pltpu.roll(face, (to_lane + LANES - j % LANES) % LANES, 1)
            return jnp.where(exists, moved, jnp.zeros_like(moved))

        return read

    def row(which):
        def read(z, var, at):
            if len(y_rows) > 1:
                return y_rows[which][z, var : var + 1, at]
            here = y_rows[0][z, var : var + 1, at]
            return jnp.where(lax.axis_index("gy") == 1 - which, here, jnp.zeros_like(here))

        return read

    return column(me_x - 1, 1, 0), column(me_x + 1, 0, LANES - 1), row(0), row(1)


def neighbours(value, z, tile, tiles, halo):
    y_count = value.shape[2]
    lane = lane_iota(y_count)
    row = row_iota(y_count)
    at = slice(tile * LANES, (tile + 1) * LANES)
    result = ([], [], [], [])
    for var in range(VARS):
        here = value[z, var, :, at]
        if tile > 0:
            before = pltpu.roll(value[z, var, :, at.start - LANES : at.start], 1, 1)
        else:
            before = halo[0](z, var)
        if tile < tiles - 1:
            after = pltpu.roll(value[z, var, :, at.stop : at.stop + LANES], LANES - 1, 1)
        else:
            after = halo[1](z, var)
        result[0].append(jnp.where(lane == 0, before, pltpu.roll(here, 1, 1)))
        result[1].append(jnp.where(lane == LANES - 1, after, pltpu.roll(here, LANES - 1, 1)))
        result[2].append(jnp.where(row == 0, halo[2](z, var, at), pltpu.roll(here, 1, 0)))
        result[3].append(
            jnp.where(row == y_count - 1, halo[3](z, var, at), pltpu.roll(here, y_count - 1, 0))
        )
    return result


def inplane(jacobians, value, z, tile, tiles, halo):
    at = slice(tile * LANES, (tile + 1) * LANES)
    total = None
    for n, values in enumerate(neighbours(value, z, tile, tiles, halo)):
        part = apply_block(block(jacobians, z, n, at=at), values)
        total = part if total is None else [a + b for a, b in zip(total, part)]
    return total


def planes_of(ref, z, at):
    return [ref[z, var, :, at] for var in range(VARS)]


def solution(mesh):
    gz, gx, gy = (mesh.shape[a] for a in ("gz", "gx", "gy"))
    short = gz == 4

    def body(right_side, previous, diag_inverse, jacobians):
        rhs = jnp.transpose(right_side, (0, 2, 1, 3))
        prev = jnp.transpose(previous, (0, 2, 1, 3))
        inv = jnp.transpose(diag_inverse, (0, 2, 3, 1, 4))
        jac = jnp.transpose(jacobians, (0, 2, 3, 4, 1, 5))
        nz, _, ny, nx = rhs.shape
        tiles = nx // LANES
        assert nx % LANES == 0
        spans = [slice(t * LANES, (t + 1) * LANES) for t in range(tiles)]
        plane = ((VARS, ny, nx), F32)
        volume = ((nz, VARS, ny, nx), F32)
        x_groups = -(-nz * VARS // LANES)
        x_face = ((2, x_groups, ny, LANES), F32)
        y_face = ((1 if gy == 2 else 2, nz, VARS, nx), F32)
        matrix = ((VARS, VARS, ny, nx), F32)
        steps = ((nz, VARS, VARS, ny, nx), F32)
        blocks = ((nz, VARS, VARS, ny, nx), jac.dtype)
        side_blocks = ((nz, 4, VARS, VARS, ny, nx), jac.dtype)
        unit = 40 * nz * ny * nx

        def exchange(x_side, y_side):
            if gy == 2:
                rows = [lax.ppermute(y_side[0], "gy", [(0, 1), (1, 0)])]
            else:
                up = [(i, i + 1) for i in range(gy - 1)]
                rows = [
                    lax.ppermute(y_side[1], "gy", up),
                    lax.ppermute(y_side[0], "gy", [(j, i) for i, j in up]),
                ]
            return lax.all_gather(x_side, "gx"), *rows


        def forward_plane(source, inv_ref, low_jac, z, at, earlier):
            lagged = apply_block(block(low_jac, z, at=at), earlier)
            return apply_block(block(inv_ref, z, at=at), [a - b for a, b in zip(source, lagged)])

        def backward_plane(sweep, inner, inv_ref, high_jac, z, at, later):
            change = apply_block(block(high_jac, z, at=at), later)
            change = apply_block(block(inv_ref, z, at=at), [a + b for a, b in zip(change, inner)])
            return [a - b for a, b in zip(sweep, change)]

        def fast_plane(step_ref, plain_ref, z, at, before):
            moved = apply_block(block(step_ref, z, at=at), before)
            return [a + b for a, b in zip(planes_of(plain_ref, z, at), moved)]

        def make_fast(step_ref, plain_ref, inv_ref, couple_ref, plain_of):
            half = VARS // 2

            def step(z, carry):
                for at in spans:
                    couple, inverse = block(couple_ref, z, at=at), block(inv_ref, z, at=at)
                    for g in range(VARS // half):
                        columns = range(g * half, (g + 1) * half)
                        held = [[couple(k, c).astype(F32) for k in range(VARS)] for c in columns]
                        for r in range(VARS):
                            row = [inverse(r, k).astype(F32) for k in range(VARS)]
                            for i, c in enumerate(columns):
                                step_ref[z, r, c, :, at] = -dot6(row, held[i])
                    plain = plain_of(z, at, lambda values: apply_block(inverse, values))
                    for var in range(VARS):
                        plain_ref[z, var, :, at] = plain[var]
                return carry

            lax.fori_loop(0, nz, step, 0)

        def put(ref, values, at):
            for var in range(VARS):
                ref[var, :, at] = values[var]

        def incoming(refs, at):
            total = [refs[0][var, :, at] for var in range(VARS)]
            for ref in refs[1:]:
                total = [a + ref[var, :, at] for var, a in enumerate(total)]
            return tuple(total)

        def planes_in(ref, at):
            return [ref[var, :, at] for var in range(VARS)]

        def apply_matrix(matrix_ref, vector, at):
            return apply_block(block(matrix_ref, at=at), vector)

        def arrived(plain, matrix_ref, vector_ref, at):
            total = apply_matrix(matrix_ref, [vector_ref[var, :, at] for var in range(VARS)], at)
            for ref in plain:
                total = [a + ref[var, :, at] for var, a in enumerate(total)]
            return tuple(total)

        def forward_sweep(source_ref, inv_ref, low_jac, starts, keep=None, fast=None):
            def step(z, earlier):
                results = []
                for tile, at in enumerate(spans):
                    if fast is not None:
                        result = fast_plane(*fast, z, at, earlier[tile])
                    else:
                        source = planes_of(source_ref, z, at)
                        result = forward_plane(source, inv_ref, low_jac, z, at, earlier[tile])
                    if keep is not None:
                        keep(z, at, result)
                    results.append(tuple(result))
                return tuple(results)

            return lax.fori_loop(0, nz, step, starts)

        def backward_sweep(sweep_ref, inner_ref, inv_ref, high_jac, starts, keep=None, fast=None):
            def step(i, later):
                z = nz - 1 - i
                results = []
                for tile, at in enumerate(spans):
                    if fast is not None:
                        result = fast_plane(*fast, z, at, later[tile])
                    else:
                        sweep, inner = planes_of(sweep_ref, z, at), planes_of(inner_ref, z, at)
                        result = backward_plane(sweep, inner, inv_ref, high_jac, z, at, later[tile])
                    if keep is not None:
                        keep(z, tile, at, result)
                    results.append(tuple(result))
                return tuple(results)

            return lax.fori_loop(0, nz, step, starts)

        def transfer(matrix_ref, inv_ref, couple_ref, wait):
            half = VARS // 2
            groups = [range(g * half, (g + 1) * half) for g in range(VARS // half)]

            def plane_step(z, at, group, vectors):
                couple, inverse = block(couple_ref, z, at=at), block(inv_ref, z, at=at)
                middle = [[] for _ in group]
                for r in range(VARS):
                    row = [couple(r, c).astype(F32) for c in range(VARS)]
                    for i in range(len(group)):
                        middle[i].append(row[group[i]] if vectors is None else dot6(row, vectors[i]))
                for r in range(VARS):
                    row = [inverse(r, c).astype(F32) for c in range(VARS)]
                    for i, c in enumerate(group):
                        matrix_ref[r, c, :, at] = -dot6(row, middle[i])

            def step(i, carry):
                z = wait(i)
                for at in spans:
                    for group in groups:
                        vectors = [[matrix_ref[r, c, :, at] for r in range(VARS)] for c in group]
                        plane_step(z, at, group, vectors)
                return carry

            z = wait(0)
            for at in spans:
                for group in groups:
                    plane_step(z, at, group, None)
            lax.fori_loop(1, nz, step, 0)


        def open_kernel(prev_hbm, inv_hbm, jac_hbm, *rest):
            prev_ref, inv_ref, low_jac, x_side, y_side, *matrices, sem, sems = rest

            def copies(z):
                return [
                    pltpu.make_async_copy(inv_hbm.at[z], inv_ref.at[z], sems.at[0, z]),
                    pltpu.make_async_copy(jac_hbm.at[z, 4], low_jac.at[z], sems.at[1, z]),
                ]

            def wait(z):
                for copy in copies(z):
                    copy.wait()
                return z

            first_copy = pltpu.make_async_copy(prev_hbm, prev_ref, sem)
            first_copy.start()
            for z in range(nz):
                for copy in copies(z):
                    copy.start()
            here = lax.axis_index("gz") == 2
            if matrices:

                @pl.when(here)
                def _():
                    transfer(matrices[0], inv_ref, low_jac, wait)

            first_copy.wait()
            write_faces(prev_ref, x_side, y_side, nz)

            def rest_of_copies():
                for z in range(nz):
                    wait(z)

            if matrices:

                @pl.when(jnp.logical_not(here))
                def _():
                    matrices[0][...] = jnp.zeros(matrix[0], F32)
                    rest_of_copies()

            else:
                rest_of_copies()

        def on(wanted, work):
            if wanted is None:
                work()
            else:
                pl.when(wanted(lax.axis_index("gz")))(work)

        def first_kernel(wanted, rhs_hbm, jac_hbm, prev_ref, inv_ref, low_jac, x_all, *rest):
            y_rows, outs = rest[: 1 if gy == 2 else 2], rest[-6:]
            on(
                wanted,
                lambda: first_work(
                    rhs_hbm, jac_hbm, prev_ref, inv_ref, low_jac, x_all, y_rows, *outs
                ),
            )

        def first_again_kernel(wanted, *refs):
            refs[-5][...] = refs[-9][...]
            first_kernel(wanted, *refs)

        def first_work(
            rhs_hbm, jac_hbm, prev_ref, inv_ref, low_jac, x_all, y_rows,
            source_ref, top_ref, sides, high_jac, rhs_ref, sems,
        ):
            halo = halo_reader(x_all, y_rows, gx, gy)

            def copies(z):
                return [
                    pltpu.make_async_copy(jac_hbm.at[z, 0:4], sides.at[z], sems.at[0, z]),
                    pltpu.make_async_copy(rhs_hbm.at[z], rhs_ref.at[z], sems.at[1, z]),
                ]

            def high_copy(z):
                return pltpu.make_async_copy(jac_hbm.at[z, 5], high_jac.at[z], sems.at[2, z])

            for z in range(nz):
                for copy in copies(z):
                    copy.start()
            for z in range(nz):
                high_copy(z).start()

            def step(z, earlier):
                for copy in copies(z):
                    copy.wait()
                results = []
                for tile, at in enumerate(spans):
                    lagged = inplane(sides, prev_ref, z, tile, tiles, halo)
                    source = [a - b for a, b in zip(planes_of(rhs_ref, z, at), lagged)]
                    for var in range(VARS):
                        source_ref[z, var, :, at] = source[var]
                    results.append(tuple(forward_plane(source, inv_ref, low_jac, z, at, earlier[tile])))
                return tuple(results)

            zero = tuple(jnp.zeros((ny, LANES), F32) for _ in range(VARS))
            top = lax.fori_loop(0, nz, step, (zero,) * tiles)
            for tile, at in enumerate(spans):
                put(top_ref, top[tile], at)
            for z in range(nz):
                high_copy(z).wait()

        def forward_kernel(source_ref, inv_ref, low_jac, *rest):
            came, top_ref = rest[:-1], rest[-1]
            starts = tuple(incoming(came, at) for at in spans)
            top = forward_sweep(source_ref, inv_ref, low_jac, starts)
            for tile, at in enumerate(spans):
                put(top_ref, top[tile], at)

        def forward_mid_kernel(low_ref, came_ref, source_ref, inv_ref, low_jac, top_ref):
            top_ref[...] = low_ref[...]

            @pl.when(lax.axis_index("gz") == 1)
            def _():
                forward_kernel(source_ref, inv_ref, low_jac, came_ref, top_ref)

        def either(device, work, fast):
            if fast is None:
                work(None)
                return
            here = lax.axis_index("gz") == device
            pl.when(here)(lambda: work(fast))
            pl.when(jnp.logical_not(here))(lambda: work(None))

        def forward_last_kernel(source_ref, prev_ref, inv_ref, low_jac, *rest):
            came, (sweep_ref, change_ref, x_side, y_side) = rest[:-4], rest[-4:]
            fast = None
            if short:
                first, near, matrix_ref, far, *fast = came

            def keep(z, at, result):
                before = planes_of(prev_ref, z, at)
                for var in range(VARS):
                    sweep_ref[z, var, :, at] = result[var]
                    change_ref[z, var, :, at] = result[var] - before[var]

            def work(fast):
                if short:
                    starts = tuple(arrived((first, near), matrix_ref, far, at) for at in spans)
                else:
                    starts = tuple(incoming(came, at) for at in spans)
                forward_sweep(source_ref, inv_ref, low_jac, starts, keep, fast)

            either(3, work, fast)
            write_faces(change_ref, x_side, y_side, nz)

        def turn_kernel(wanted, sweep_ref, change_ref, inv_ref, sides, high_jac, x_all, *rest):
            y_rows, outs = rest[: 1 if gy == 2 else 2], rest[-2:]
            on(
                wanted,
                lambda: turn_work(
                    sweep_ref, change_ref, inv_ref, sides, high_jac, x_all, y_rows, *outs
                ),
            )

        def turn_again_kernel(wanted, *refs):
            refs[-1][...] = refs[-3][...]
            turn_kernel(wanted, *refs)

        def turn_work(
            sweep_ref, change_ref, inv_ref, sides, high_jac, x_all, y_rows, inner_ref, low_ref
        ):
            halo = halo_reader(x_all, y_rows, gx, gy)
            for tile, at in enumerate(spans):

                def step(i, later, tile=tile, at=at):
                    z = nz - 1 - i
                    inner = inplane(sides, change_ref, z, tile, tiles, halo)
                    for var in range(VARS):
                        inner_ref[z, var, :, at] = inner[var]
                    sweep = planes_of(sweep_ref, z, at)
                    return tuple(backward_plane(sweep, inner, inv_ref, high_jac, z, at, later))

                zero = tuple(jnp.zeros((ny, LANES), F32) for _ in range(VARS))
                put(low_ref, lax.fori_loop(0, nz, step, zero), at)

        def only(device, work, ref, shape):
            here = lax.axis_index("gz") == device
            pl.when(here)(work)

            @pl.when(jnp.logical_not(here))
            def _():
                ref[...] = jnp.zeros(shape, F32)

        def down_matrix(inv_ref, high_jac, matrix_ref):
            transfer(matrix_ref, inv_ref, high_jac, lambda i: nz - 1 - i)

        def forward_idle_kernel(inv_ref, high_jac, low_jac, source_ref, _, matrix_ref, step_ref, plain_ref):
            only(1, lambda: down_matrix(inv_ref, high_jac, matrix_ref), matrix_ref, matrix[0])

            @pl.when(lax.axis_index("gz") == 3)
            def _():
                def plain_of(z, at, times):
                    return times(planes_of(source_ref, z, at))

                make_fast(step_ref, plain_ref, inv_ref, low_jac, plain_of)

        def backward_idle_kernel(inv_ref, high_jac, sweep_ref, inner_ref, step_ref, plain_ref):
            me = lax.axis_index("gz")

            @pl.when((me == 0) | (me == 2))
            def _():
                def plain_of(z, at, times):
                    moved = times(planes_of(inner_ref, z, at))
                    return [a - b for a, b in zip(planes_of(sweep_ref, z, at), moved)]

                make_fast(step_ref, plain_ref, inv_ref, high_jac, plain_of)

        def backward_kernel(sweep_ref, inner_ref, inv_ref, high_jac, *rest):
            came, low_ref = rest[:-1], rest[-1]
            starts = tuple(incoming(came, at) for at in spans)
            low = backward_sweep(sweep_ref, inner_ref, inv_ref, high_jac, starts)
            for tile, at in enumerate(spans):
                put(low_ref, low[tile], at)

        def pass_kernel(*refs):
            pass

        def backward_mid_kernel(own_ref, came_ref, step_ref, plain_ref, low_ref):
            here = lax.axis_index("gz") == 2

            @pl.when(here)
            def _():
                starts = tuple(incoming((came_ref,), at) for at in spans)
                low = backward_sweep(None, None, None, None, starts, fast=(step_ref, plain_ref))
                for tile, at in enumerate(spans):
                    put(low_ref, low[tile], at)

            @pl.when(jnp.logical_not(here))
            def _():
                low_ref[...] = own_ref[...]

        def update_kernel(sweep_ref, inner_ref, inv_ref, high_jac, *rest):
            came, (out_hbm, held, sems) = rest[:-3], rest[-3:]
            fast = None
            if short:
                first, near, matrix_ref, far, *fast = came

            def out_copy(z):
                return pltpu.make_async_copy(held.at[z], out_hbm.at[z], sems.at[z])

            def keep(z, tile, at, result):
                for var in range(VARS):
                    held[z, var, :, at] = result[var]
                if tile == tiles - 1:
                    out_copy(z).start()

            def work(fast):
                if short:
                    starts = tuple(arrived((first, near), matrix_ref, far, at) for at in spans)
                else:
                    starts = tuple(incoming(came, at) for at in spans)
                backward_sweep(sweep_ref, inner_ref, inv_ref, high_jac, starts, keep, fast)

            either(0, work, fast)
            for z in range(nz):
                out_copy(z).wait()


        prev, inv, low_jac, x_side, y_side, *up_matrix = call(
            open_kernel,
            [volume, blocks, blocks, x_face, y_face] + [matrix] * (1 if short else 0),
            prev,
            inv,
            jac,
            cost=12 * unit,
            in_hbm=(0, 1, 2),
            scratch=[pltpu.SemaphoreType.DMA, pltpu.SemaphoreType.DMA((2, nz))],
        )
        if short:
            up_there = lax.ppermute(up_matrix[0], "gz", [(2, 3)])
        halo = exchange(x_side, y_side)
        ahead, behind = None, None
        if short:
            ahead, behind = (lambda device: device == 0), (lambda device: device != 0)
        first_args = [rhs, jac, prev, inv, low_jac, *halo]
        first_options = dict(
            cost=unit // 8,
            in_hbm=(0, 1),
            scratch=[pltpu.VMEM(rhs.shape, F32), pltpu.SemaphoreType.DMA((3, nz))],
        )
        first_outs = [volume, plane, side_blocks, blocks]
        source, top, sides, high_jac = call(
            functools.partial(first_kernel, ahead), first_outs, *first_args, **first_options
        )
        if short:
            first = lax.ppermute(top, "gz", [(0, 1)])
            n = len(first_args)
            source, top, sides, high_jac = call(
                functools.partial(first_again_kernel, behind),
                first_outs,
                *first_args,
                source,
                top,
                sides,
                high_jac,
                aliases={n: 0, n + 2: 2, n + 3: 3},
                **first_options,
            )
            (top,) = call(
                forward_mid_kernel,
                [plane],
                top,
                first,
                source,
                inv,
                low_jac,
                cost=unit // 8,
            )
            far = lax.ppermute(top, "gz", [(1, 3)])
            near = lax.ppermute(top, "gz", [(1, 2), (2, 3)])
            down_one, *fast = call(
                forward_idle_kernel,
                [matrix, steps, volume],
                inv,
                high_jac,
                low_jac,
                source,
                up_there,
                cost=unit // 8,
            )
            (down_one,) = call(
                pass_kernel, [matrix], down_one, near, far, cost=unit // 8, aliases={0: 0}
            )
            down_there = lax.ppermute(down_one, "gz", [(1, 0)])
            came = [first, near, up_there, far, *fast]
        else:
            came = []
            for hop in range(gz - 1):
                if hop:
                    (top,) = call(
                        forward_kernel, [plane], source, inv, low_jac, *came, cost=3 * unit
                    )
                came.append(lax.ppermute(top, "gz", [(hop, hop + 1)]))
        sweep, change, x_side, y_side = call(
            forward_last_kernel,
            [volume, volume, x_face, y_face],
            source,
            prev,
            inv,
            low_jac,
            *came,
            cost=4 * unit,
        )
        halo = exchange(x_side, y_side)
        if short:
            ahead, behind = (lambda device: device == 3), (lambda device: device != 3)
        turn_args = [sweep, change, inv, sides, high_jac, *halo]
        inner, low = call(
            functools.partial(turn_kernel, ahead), [volume, plane], *turn_args, cost=11 * unit
        )
        if short:
            ahead_low = low
            inner, low = call(
                functools.partial(turn_again_kernel, behind),
                [volume, plane],
                *turn_args,
                inner,
                low,
                aliases={len(turn_args): 0},
                cost=unit // 8,
            )
            first = lax.ppermute(ahead_low, "gz", [(3, 2)])
            fast = call(
                backward_idle_kernel,
                [steps, volume],
                inv,
                high_jac,
                sweep,
                inner,
                cost=unit // 8,
            )
            (low,) = call(backward_mid_kernel, [plane], low, first, *fast, cost=unit // 8)
            far = lax.ppermute(low, "gz", [(2, 0)])
            near = lax.ppermute(low, "gz", [(2, 1), (1, 0)])
            came = [first, near, down_there, far, *fast]
        else:
            came = []
            for hop in range(gz - 1, 0, -1):
                if came:
                    (low,) = call(
                        backward_kernel, [plane], sweep, inner, inv, high_jac, *came, cost=3 * unit
                    )
                came.append(lax.ppermute(low, "gz", [(hop, hop - 1)]))
        (update,) = call(
            update_kernel,
            [volume],
            sweep,
            inner,
            inv,
            high_jac,
            *came,
            cost=5 * unit,
            out_hbm=(0,),
            scratch=[pltpu.VMEM(volume[0], F32), pltpu.SemaphoreType.DMA((nz,))],
        )
        return jnp.transpose(update, (0, 2, 1, 3))

    placed = (
        P("gz", "gy", None, "gx"),
        P("gz", "gy", None, "gx"),
        P("gz", "gy", None, None, "gx"),
        P("gz", "gy", None, None, None, "gx"),
    )
    return jax.shard_map(
        body, mesh=mesh, in_specs=placed, out_specs=P("gz", "gy", None, "gx"), check_vma=False
    )
```

```python
import functools

import jax
import jax.numpy as jnp
from jax import lax
from jax.experimental import pallas as pl
from jax.experimental.pallas import tpu as pltpu
from jax.sharding import PartitionSpec as P

VARS = 6
LANES = 128
F32 = jnp.float32
WHOLE = pl.BlockSpec(memory_space=pltpu.VMEM)


def call(body, outs, *args, cost, limit=16 << 20, scratch=(), in_hbm=(), out_hbm=(), aliases={}):
    far = pl.BlockSpec(memory_space=pl.ANY)
    shapes = [
        jax.ShapeDtypeStruct(o[0], o[1]) if i in out_hbm else pltpu.VMEM(o[0], o[1])
        for i, o in enumerate(outs)
    ]
    return pl.pallas_call(
        body,
        out_shape=shapes,
        in_specs=[far if i in in_hbm else WHOLE for i in range(len(args))],
        out_specs=[far if i in out_hbm else WHOLE for i in range(len(outs))],
        scratch_shapes=scratch,
        input_output_aliases=aliases,
        cost_estimate=pl.CostEstimate(flops=0, bytes_accessed=cost, transcendentals=0),
        compiler_params=pltpu.CompilerParams(vmem_limit_bytes=limit),
    )(*[
        pltpu.with_memory_space_constraint(a, pltpu.HBM if i in in_hbm else pltpu.VMEM)
        for i, a in enumerate(args)
    ])


def lane_iota(rows):
    return lax.broadcasted_iota(jnp.int32, (rows, LANES), 1)


def row_iota(rows):
    return lax.broadcasted_iota(jnp.int32, (rows, LANES), 0)


def dot6(blocks, values):
    terms = [b.astype(F32) * v for b, v in zip(blocks, values)]
    return (terms[0] + terms[1]) + (terms[2] + terms[3]) + (terms[4] + terms[5])


def block(ref, *index, at):
    return lambda r, c: ref[(*index, r, c, slice(None), at)]


def apply_block(get, values):
    return [dot6([get(r, c) for c in range(VARS)], values) for r in range(VARS)]


def write_faces(value, x_face, y_face, z_count):
    y_count = value.shape[2]
    x_count = value.shape[3]
    lane = lane_iota(y_count)
    for group in range(x_face.shape[1]):
        faces = []
        for start, source_lane in ((0, 0), (x_count - LANES, LANES - 1)):
            held = jnp.zeros((y_count, LANES), F32)
            for slot in range(min(LANES, z_count * VARS - group * LANES)):
                z, var = divmod(group * LANES + slot, VARS)
                tile = value[z, var, :, start : start + LANES]
                moved = pltpu.roll(tile, (slot - source_lane) % LANES, 1)
                held = jnp.where(lane == slot, moved, held)
            faces.append(held)
        x_face[0, group], x_face[1, group] = faces
    if y_face.shape[0] == 1:
        first = lax.axis_index("gy") == 0
        for z in range(z_count):
            for var in range(VARS):
                low = value[z, var, 0:1, :]
                high = value[z, var, y_count - 1 : y_count, :]
                y_face[0, z, var : var + 1, :] = jnp.where(first, high, low)
    else:
        for z in range(z_count):
            for var in range(VARS):
                y_face[0, z, var : var + 1, :] = value[z, var, 0:1, :]
                y_face[1, z, var : var + 1, :] = value[z, var, y_count - 1 : y_count, :]


def halo_reader(x_all, y_rows, gx, gy):
    me_x = lax.axis_index("gx")

    def column(there, side, to_lane):
        exists = (there >= 0) & (there < gx)
        device = jnp.clip(there, 0, gx - 1)

        def read(z, var):
            j = z * VARS + var
            face = x_all[device, side, j // LANES]
            moved = pltpu.roll(face, (to_lane + LANES - j % LANES) % LANES, 1)
            return jnp.where(exists, moved, jnp.zeros_like(moved))

        return read

    def row(which):
        def read(z, var, at):
            if len(y_rows) > 1:
                return y_rows[which][z, var : var + 1, at]
            here = y_rows[0][z, var : var + 1, at]
            return jnp.where(lax.axis_index("gy") == 1 - which, here, jnp.zeros_like(here))

        return read

    return column(me_x - 1, 1, 0), column(me_x + 1, 0, LANES - 1), row(0), row(1)


def neighbours(value, z, tile, tiles, halo):
    y_count = value.shape[2]
    lane = lane_iota(y_count)
    row = row_iota(y_count)
    at = slice(tile * LANES, (tile + 1) * LANES)
    result = ([], [], [], [])
    for var in range(VARS):
        here = value[z, var, :, at]
        if tile > 0:
            before = pltpu.roll(value[z, var, :, at.start - LANES : at.start], 1, 1)
        else:
            before = halo[0](z, var)
        if tile < tiles - 1:
            after = pltpu.roll(value[z, var, :, at.stop : at.stop + LANES], LANES - 1, 1)
        else:
            after = halo[1](z, var)
        result[0].append(jnp.where(lane == 0, before, pltpu.roll(here, 1, 1)))
        result[1].append(jnp.where(lane == LANES - 1, after, pltpu.roll(here, LANES - 1, 1)))
        result[2].append(jnp.where(row == 0, halo[2](z, var, at), pltpu.roll(here, 1, 0)))
        result[3].append(
            jnp.where(row == y_count - 1, halo[3](z, var, at), pltpu.roll(here, y_count - 1, 0))
        )
    return result


def inplane(jacobians, value, z, tile, tiles, halo):
    at = slice(tile * LANES, (tile + 1) * LANES)
    total = None
    for n, values in enumerate(neighbours(value, z, tile, tiles, halo)):
        part = apply_block(block(jacobians, z, n, at=at), values)
        total = part if total is None else [a + b for a, b in zip(total, part)]
    return total


def planes_of(ref, z, at):
    return [ref[z, var, :, at] for var in range(VARS)]


def solution(mesh):
    gz, gx, gy = (mesh.shape[a] for a in ("gz", "gx", "gy"))
    short = gz == 4

    def body(right_side, previous, diag_inverse, jacobians):
        rhs = jnp.transpose(right_side, (0, 2, 1, 3))
        prev = jnp.transpose(previous, (0, 2, 1, 3))
        inv = jnp.transpose(diag_inverse, (0, 2, 3, 1, 4))
        jac = jnp.transpose(jacobians, (0, 2, 3, 4, 1, 5))
        nz, _, ny, nx = rhs.shape
        tiles = nx // LANES
        assert nx % LANES == 0
        spans = [slice(t * LANES, (t + 1) * LANES) for t in range(tiles)]
        plane = ((VARS, ny, nx), F32)
        volume = ((nz, VARS, ny, nx), F32)
        x_groups = -(-nz * VARS // LANES)
        x_face = ((2, x_groups, ny, LANES), F32)
        y_face = ((1 if gy == 2 else 2, nz, VARS, nx), F32)
        matrix = ((VARS, VARS, ny, nx), F32)
        steps = ((nz, VARS, VARS, ny, nx), F32)
        blocks = ((nz, VARS, VARS, ny, nx), jac.dtype)
        side_blocks = ((nz, 4, VARS, VARS, ny, nx), jac.dtype)
        unit = 40 * nz * ny * nx

        def exchange(x_side, y_side):
            if gy == 2:
                rows = [lax.ppermute(y_side[0], "gy", [(0, 1), (1, 0)])]
            else:
                up = [(i, i + 1) for i in range(gy - 1)]
                rows = [
                    lax.ppermute(y_side[1], "gy", up),
                    lax.ppermute(y_side[0], "gy", [(j, i) for i, j in up]),
                ]
            return lax.all_gather(x_side, "gx"), *rows


        def forward_plane(source, inv_ref, low_jac, z, at, earlier):
            lagged = apply_block(block(low_jac, z, at=at), earlier)
            return apply_block(block(inv_ref, z, at=at), [a - b for a, b in zip(source, lagged)])

        def backward_plane(sweep, inner, inv_ref, high_jac, z, at, later):
            change = apply_block(block(high_jac, z, at=at), later)
            change = apply_block(block(inv_ref, z, at=at), [a + b for a, b in zip(change, inner)])
            return [a - b for a, b in zip(sweep, change)]

        def fast_plane(step_ref, plain_ref, z, at, before):
            moved = apply_block(block(step_ref, z, at=at), before)
            return [a + b for a, b in zip(planes_of(plain_ref, z, at), moved)]

        def make_fast(step_ref, plain_ref, inv_ref, couple_ref, plain_of):
            half = VARS // 2

            def step(z, carry):
                for at in spans:
                    couple, inverse = block(couple_ref, z, at=at), block(inv_ref, z, at=at)
                    for g in range(VARS // half):
                        columns = range(g * half, (g + 1) * half)
                        held = [[couple(k, c).astype(F32) for k in range(VARS)] for c in columns]
                        for r in range(VARS):
                            row = [inverse(r, k).astype(F32) for k in range(VARS)]
                            for i, c in enumerate(columns):
                                step_ref[z, r, c, :, at] = -dot6(row, held[i])
                    plain = plain_of(z, at, lambda values: apply_block(inverse, values))
                    for var in range(VARS):
                        plain_ref[z, var, :, at] = plain[var]
                return carry

            lax.fori_loop(0, nz, step, 0)

        def put(ref, values, at):
            for var in range(VARS):
                ref[var, :, at] = values[var]

        def incoming(refs, at):
            total = [refs[0][var, :, at] for var in range(VARS)]
            for ref in refs[1:]:
                total = [a + ref[var, :, at] for var, a in enumerate(total)]
            return tuple(total)

        def planes_in(ref, at):
            return [ref[var, :, at] for var in range(VARS)]

        def apply_matrix(matrix_ref, vector, at):
            return apply_block(block(matrix_ref, at=at), vector)

        def arrived(plain, matrix_ref, vector_ref, at):
            total = apply_matrix(matrix_ref, [vector_ref[var, :, at] for var in range(VARS)], at)
            for ref in plain:
                total = [a + ref[var, :, at] for var, a in enumerate(total)]
            return tuple(total)

        def forward_sweep(source_ref, inv_ref, low_jac, starts, keep=None, fast=None):
            def step(z, earlier):
                results = []
                for tile, at in enumerate(spans):
                    if fast is not None:
                        result = fast_plane(*fast, z, at, earlier[tile])
                    else:
                        source = planes_of(source_ref, z, at)
                        result = forward_plane(source, inv_ref, low_jac, z, at, earlier[tile])
                    if keep is not None:
                        keep(z, at, result)
                    results.append(tuple(result))
                return tuple(results)

            return lax.fori_loop(0, nz, step, starts)

        def backward_sweep(sweep_ref, inner_ref, inv_ref, high_jac, starts, keep=None, fast=None):
            def step(i, later):
                z = nz - 1 - i
                results = []
                for tile, at in enumerate(spans):
                    if fast is not None:
                        result = fast_plane(*fast, z, at, later[tile])
                    else:
                        sweep, inner = planes_of(sweep_ref, z, at), planes_of(inner_ref, z, at)
                        result = backward_plane(sweep, inner, inv_ref, high_jac, z, at, later[tile])
                    if keep is not None:
                        keep(z, tile, at, result)
                    results.append(tuple(result))
                return tuple(results)

            return lax.fori_loop(0, nz, step, starts)

        def transfer(matrix_ref, inv_ref, couple_ref, wait):
            half = VARS // 2
            groups = [range(g * half, (g + 1) * half) for g in range(VARS // half)]

            def plane_step(z, at, group, vectors):
                couple, inverse = block(couple_ref, z, at=at), block(inv_ref, z, at=at)
                middle = [[] for _ in group]
                for r in range(VARS):
                    row = [couple(r, c).astype(F32) for c in range(VARS)]
                    for i in range(len(group)):
                        middle[i].append(row[group[i]] if vectors is None else dot6(row, vectors[i]))
                for r in range(VARS):
                    row = [inverse(r, c).astype(F32) for c in range(VARS)]
                    for i, c in enumerate(group):
                        matrix_ref[r, c, :, at] = -dot6(row, middle[i])

            def step(i, carry):
                z = wait(i)
                for at in spans:
                    for group in groups:
                        vectors = [[matrix_ref[r, c, :, at] for r in range(VARS)] for c in group]
                        plane_step(z, at, group, vectors)
                return carry

            z = wait(0)
            for at in spans:
                for group in groups:
                    plane_step(z, at, group, None)
            lax.fori_loop(1, nz, step, 0)


        def open_kernel(prev_hbm, inv_hbm, jac_hbm, *rest):
            prev_ref, inv_ref, low_jac, x_side, y_side, *matrices, sem, sems = rest

            def copies(z):
                return [
                    pltpu.make_async_copy(inv_hbm.at[z], inv_ref.at[z], sems.at[0, z]),
                    pltpu.make_async_copy(jac_hbm.at[z, 4], low_jac.at[z], sems.at[1, z]),
                ]

            def wait(z):
                for copy in copies(z):
                    copy.wait()
                return z

            first_copy = pltpu.make_async_copy(prev_hbm, prev_ref, sem)
            first_copy.start()
            me = lax.axis_index("gz")
            here = me == 2

            def start_copies():
                for z in range(nz):
                    for copy in copies(z):
                        copy.start()

            if matrices:
                pl.when(me != 0)(start_copies)
            else:
                start_copies()
            if matrices:

                @pl.when(here)
                def _():
                    transfer(matrices[0], inv_ref, low_jac, wait)

            first_copy.wait()
            write_faces(prev_ref, x_side, y_side, nz)

            def rest_of_copies():
                for z in range(nz):
                    wait(z)

            if matrices:

                @pl.when(jnp.logical_not(here))
                def _():
                    matrices[0][...] = jnp.zeros(matrix[0], F32)
                    pl.when(me != 0)(rest_of_copies)

            else:
                rest_of_copies()

        def on(wanted, work):
            if wanted is None:
                work()
            else:
                pl.when(wanted(lax.axis_index("gz")))(work)

        def load_high(jac_hbm, high_jac, sem):
            return pltpu.make_async_copy(jac_hbm.at[:, 5], high_jac, sem)

        def first_kernel(rhs_hbm, jac_hbm, prev_ref, inv_ref, low_jac, x_all, *rest):
            *y_rows, source_ref, top_ref, sides, high_jac, rhs_ref, sems, high_sem = rest
            high_copy = load_high(jac_hbm, high_jac, high_sem)
            first_work(
                rhs_hbm, jac_hbm, prev_ref, inv_ref, low_jac, x_all, y_rows,
                source_ref, top_ref, sides, rhs_ref, sems, high_copy,
            )
            high_copy.wait()

        def first_ahead_kernel(rhs_hbm, jac_hbm, prev_ref, _, __, x_all, *rest):
            *y_rows, inv_hbm, source_ref, top_ref, sides, inv_ref, low_jac, rhs_ref, sems = rest

            @pl.when(lax.axis_index("gz") == 0)
            def _():
                first_work(
                    rhs_hbm, jac_hbm, prev_ref, inv_ref, low_jac, x_all, y_rows,
                    source_ref, top_ref, sides, rhs_ref, sems, None, inv_hbm,
                )

        def first_behind_kernel(*refs):
            jac_hbm, high_jac, high_sem = refs[1], refs[-4], refs[-1]
            inputs, top_before = refs[: len(first_args)], refs[len(first_args) + 1]
            source_ref, top_ref, sides, _, rhs_ref, sems, _ = refs[-7:]
            high_copy = load_high(jac_hbm, high_jac, high_sem)
            here = lax.axis_index("gz") == 0

            @pl.when(here)
            def _():
                high_copy.start()
                top_ref[...] = top_before[...]

            @pl.when(jnp.logical_not(here))
            def _():
                first_work(
                    *inputs[:6], inputs[6:], source_ref, top_ref, sides, rhs_ref, sems, high_copy
                )

            high_copy.wait()

        def first_work(
            rhs_hbm, jac_hbm, prev_ref, inv_ref, low_jac, x_all, y_rows,
            source_ref, top_ref, sides, rhs_ref, sems, also, inv_hbm=None,
        ):
            halo = halo_reader(x_all, y_rows, gx, gy)

            def copies(z):
                pairs = [(jac_hbm.at[z, 0:4], sides), (rhs_hbm.at[z], rhs_ref)]
                if inv_hbm is not None:
                    pairs += [(inv_hbm.at[z], inv_ref), (jac_hbm.at[z, 4], low_jac)]
                return [
                    pltpu.make_async_copy(far, near.at[z], sems.at[i, z])
                    for i, (far, near) in enumerate(pairs)
                ]

            for z in range(nz):
                for copy in copies(z):
                    copy.start()
            if also is not None:
                also.start()

            def step(z, earlier):
                for copy in copies(z):
                    copy.wait()
                results = []
                for tile, at in enumerate(spans):
                    lagged = inplane(sides, prev_ref, z, tile, tiles, halo)
                    source = [a - b for a, b in zip(planes_of(rhs_ref, z, at), lagged)]
                    for var in range(VARS):
                        source_ref[z, var, :, at] = source[var]
                    results.append(tuple(forward_plane(source, inv_ref, low_jac, z, at, earlier[tile])))
                return tuple(results)

            zero = tuple(jnp.zeros((ny, LANES), F32) for _ in range(VARS))
            top = lax.fori_loop(0, nz, step, (zero,) * tiles)
            for tile, at in enumerate(spans):
                put(top_ref, top[tile], at)

        def forward_kernel(source_ref, inv_ref, low_jac, *rest):
            came, top_ref = rest[:-1], rest[-1]
            starts = tuple(incoming(came, at) for at in spans)
            top = forward_sweep(source_ref, inv_ref, low_jac, starts)
            for tile, at in enumerate(spans):
                put(top_ref, top[tile], at)

        def forward_mid_kernel(low_ref, came_ref, source_ref, inv_ref, low_jac, top_ref):
            top_ref[...] = low_ref[...]

            @pl.when(lax.axis_index("gz") == 1)
            def _():
                forward_kernel(source_ref, inv_ref, low_jac, came_ref, top_ref)

        def either(wanted, work, fast):
            if fast is None:
                work(None)
                return
            here = wanted(lax.axis_index("gz"))
            pl.when(here)(lambda: work(fast))
            pl.when(jnp.logical_not(here))(lambda: work(None))

        def forward_last_kernel(source_ref, prev_ref, inv_ref, low_jac, *rest):
            came, (sweep_ref, change_ref, x_side, y_side) = rest[:-4], rest[-4:]
            fast = None
            if short:
                first, far, matrix_ref, near, *fast = came

            def keep(z, at, result):
                before = planes_of(prev_ref, z, at)
                for var in range(VARS):
                    sweep_ref[z, var, :, at] = result[var]
                    change_ref[z, var, :, at] = result[var] - before[var]

            def work(fast):
                if short:
                    starts = tuple(arrived((first, near), matrix_ref, far, at) for at in spans)
                else:
                    starts = tuple(incoming(came, at) for at in spans)
                forward_sweep(source_ref, inv_ref, low_jac, starts, keep, fast)

            either(lambda me: me == 3, work, fast)
            write_faces(change_ref, x_side, y_side, nz)

        def turn_kernel(wanted, sweep_ref, change_ref, inv_ref, sides, high_jac, x_all, *rest):
            y_rows, outs = rest[: 1 if gy == 2 else 2], rest[-2:]
            on(
                wanted,
                lambda: turn_work(
                    sweep_ref, change_ref, inv_ref, sides, high_jac, x_all, y_rows, *outs
                ),
            )

        def turn_again_kernel(wanted, *refs):
            refs[-1][...] = refs[-3][...]
            turn_kernel(wanted, *refs)

        def turn_work(
            sweep_ref, change_ref, inv_ref, sides, high_jac, x_all, y_rows, inner_ref, low_ref
        ):
            halo = halo_reader(x_all, y_rows, gx, gy)
            for tile, at in enumerate(spans):

                def step(i, later, tile=tile, at=at):
                    z = nz - 1 - i
                    inner = inplane(sides, change_ref, z, tile, tiles, halo)
                    for var in range(VARS):
                        inner_ref[z, var, :, at] = inner[var]
                    sweep = planes_of(sweep_ref, z, at)
                    return tuple(backward_plane(sweep, inner, inv_ref, high_jac, z, at, later))

                zero = tuple(jnp.zeros((ny, LANES), F32) for _ in range(VARS))
                put(low_ref, lax.fori_loop(0, nz, step, zero), at)

        def only(device, work, ref, shape):
            here = lax.axis_index("gz") == device
            pl.when(here)(work)

            @pl.when(jnp.logical_not(here))
            def _():
                ref[...] = jnp.zeros(shape, F32)

        def down_matrix(inv_ref, high_jac, matrix_ref):
            transfer(matrix_ref, inv_ref, high_jac, lambda i: nz - 1 - i)

        def forward_idle_kernel(inv_ref, high_jac, low_jac, source_ref, _, matrix_ref, step_ref, plain_ref):
            only(1, lambda: down_matrix(inv_ref, high_jac, matrix_ref), matrix_ref, matrix[0])

            @pl.when(lax.axis_index("gz") == 3)
            def _():
                def plain_of(z, at, times):
                    return times(planes_of(source_ref, z, at))

                make_fast(step_ref, plain_ref, inv_ref, low_jac, plain_of)

        def backward_idle_kernel(inv_ref, high_jac, sweep_ref, inner_ref, step_ref, plain_ref):
            me = lax.axis_index("gz")

            @pl.when(me != 3)
            def _():
                def plain_of(z, at, times):
                    moved = times(planes_of(inner_ref, z, at))
                    return [a - b for a, b in zip(planes_of(sweep_ref, z, at), moved)]

                make_fast(step_ref, plain_ref, inv_ref, high_jac, plain_of)

        def backward_kernel(sweep_ref, inner_ref, inv_ref, high_jac, *rest):
            came, low_ref = rest[:-1], rest[-1]
            starts = tuple(incoming(came, at) for at in spans)
            low = backward_sweep(sweep_ref, inner_ref, inv_ref, high_jac, starts)
            for tile, at in enumerate(spans):
                put(low_ref, low[tile], at)

        def pass_kernel(*refs):
            pass

        def backward_mid_kernel(own_ref, came_ref, step_ref, plain_ref, low_ref):
            here = lax.axis_index("gz") == 2

            @pl.when(here)
            def _():
                starts = tuple(incoming((came_ref,), at) for at in spans)
                low = backward_sweep(None, None, None, None, starts, fast=(step_ref, plain_ref))
                for tile, at in enumerate(spans):
                    put(low_ref, low[tile], at)

            @pl.when(jnp.logical_not(here))
            def _():
                low_ref[...] = own_ref[...]

        def update_kernel(sweep_ref, inner_ref, inv_ref, high_jac, *rest):
            came, (out_hbm, held, sems) = rest[:-3], rest[-3:]
            fast = None
            if short:
                first, far, matrix_ref, near, *fast = came

            def out_copy(z):
                return pltpu.make_async_copy(held.at[z], out_hbm.at[z], sems.at[z])

            def keep(z, tile, at, result):
                for var in range(VARS):
                    held[z, var, :, at] = result[var]
                if tile == tiles - 1:
                    out_copy(z).start()

            def work(fast):
                if short:
                    starts = tuple(arrived((first, near), matrix_ref, far, at) for at in spans)
                else:
                    starts = tuple(incoming(came, at) for at in spans)
                backward_sweep(sweep_ref, inner_ref, inv_ref, high_jac, starts, keep, fast)

            either(lambda me: me != 3, work, fast)
            for z in range(nz):
                out_copy(z).wait()


        inv_far = inv
        prev, inv, low_jac, x_side, y_side, *up_matrix = call(
            open_kernel,
            [volume, blocks, blocks, x_face, y_face] + [matrix] * (1 if short else 0),
            prev,
            inv,
            jac,
            cost=12 * unit,
            in_hbm=(0, 1, 2),
            scratch=[pltpu.SemaphoreType.DMA, pltpu.SemaphoreType.DMA((2, nz))],
        )
        if short:
            up_there = lax.ppermute(up_matrix[0], "gz", [(2, 3)])
        halo = exchange(x_side, y_side)
        first_args = [rhs, jac, prev, inv, low_jac, *halo]
        first_scratch = [pltpu.VMEM(rhs.shape, F32), pltpu.SemaphoreType.DMA((4, nz))]
        if short:
            n = len(first_args)
            source, top, sides, inv, low_jac = call(
                first_ahead_kernel,
                [volume, plane, side_blocks, blocks, blocks],
                *first_args,
                inv_far,
                cost=unit // 8,
                in_hbm=(0, 1, n),
                aliases={3: 3, 4: 4},
                scratch=first_scratch,
            )
            first_args[3:5] = inv, low_jac
            first = lax.ppermute(top, "gz", [(0, 1)])
            source, top, sides, high_jac = call(
                first_behind_kernel,
                [volume, plane, side_blocks, blocks],
                *first_args,
                source,
                top,
                sides,
                cost=unit // 8,
                in_hbm=(0, 1),
                aliases={n: 0, n + 2: 2},
                scratch=first_scratch + [pltpu.SemaphoreType.DMA],
            )
            (top,) = call(
                forward_mid_kernel,
                [plane],
                top,
                first,
                source,
                inv,
                low_jac,
                cost=unit // 8,
            )
            far = lax.ppermute(top, "gz", [(1, 3)])
            near = lax.ppermute(top, "gz", [(1, 2), (2, 3)])
            down_one, *fast = call(
                forward_idle_kernel,
                [matrix, steps, volume],
                inv,
                high_jac,
                low_jac,
                source,
                up_there,
                cost=unit // 8,
            )
            (down_one,) = call(
                pass_kernel, [matrix], down_one, near, far, cost=unit // 8, aliases={0: 0}
            )
            down_there = lax.ppermute(down_one, "gz", [(1, 0)])
            came = [first, far, up_there, near, *fast]
        else:
            source, top, sides, high_jac = call(
                first_kernel,
                [volume, plane, side_blocks, blocks],
                *first_args,
                cost=14 * unit,
                in_hbm=(0, 1),
                scratch=first_scratch + [pltpu.SemaphoreType.DMA],
            )
            came = []
            for hop in range(gz - 1):
                if hop:
                    (top,) = call(
                        forward_kernel, [plane], source, inv, low_jac, *came, cost=3 * unit
                    )
                came.append(lax.ppermute(top, "gz", [(hop, hop + 1)]))
        sweep, change, x_side, y_side = call(
            forward_last_kernel,
            [volume, volume, x_face, y_face],
            source,
            prev,
            inv,
            low_jac,
            *came,
            cost=4 * unit,
        )
        halo = exchange(x_side, y_side)
        if short:
            ahead, behind = (lambda device: device == 3), (lambda device: device != 3)
        turn_args = [sweep, change, inv, sides, high_jac, *halo]
        inner, low = call(
            functools.partial(turn_kernel, ahead), [volume, plane], *turn_args, cost=11 * unit
        )
        if short:
            ahead_low = low
            inner, low = call(
                functools.partial(turn_again_kernel, behind),
                [volume, plane],
                *turn_args,
                inner,
                low,
                aliases={len(turn_args): 0},
                cost=unit // 8,
            )
            first = lax.ppermute(ahead_low, "gz", [(3, 2)])
            fast = call(
                backward_idle_kernel,
                [steps, volume],
                inv,
                high_jac,
                sweep,
                inner,
                cost=unit // 8,
            )
            (low,) = call(backward_mid_kernel, [plane], low, first, *fast, cost=unit // 8)
            far = lax.ppermute(low, "gz", [(2, 0)])
            near = lax.ppermute(low, "gz", [(2, 1), (1, 0)])
            came = [first, far, down_there, near, *fast]
        else:
            came = []
            for hop in range(gz - 1, 0, -1):
                if came:
                    (low,) = call(
                        backward_kernel, [plane], sweep, inner, inv, high_jac, *came, cost=3 * unit
                    )
                came.append(lax.ppermute(low, "gz", [(hop, hop - 1)]))
        (update,) = call(
            update_kernel,
            [volume],
            sweep,
            inner,
            inv,
            high_jac,
            *came,
            cost=5 * unit,
            out_hbm=(0,),
            scratch=[pltpu.VMEM(volume[0], F32), pltpu.SemaphoreType.DMA((nz,))],
        )
        return jnp.transpose(update, (0, 2, 1, 3))

    placed = (
        P("gz", "gy", None, "gx"),
        P("gz", "gy", None, "gx"),
        P("gz", "gy", None, None, "gx"),
        P("gz", "gy", None, None, None, "gx"),
    )
    return jax.shard_map(
        body, mesh=mesh, in_specs=placed, out_specs=P("gz", "gy", None, "gx"), check_vma=False
    )
```

```python
import functools

import jax
import jax.numpy as jnp
from jax import lax
from jax.experimental import pallas as pl
from jax.experimental.pallas import tpu as pltpu
from jax.sharding import PartitionSpec as P

VARS = 6
LANES = 128
F32 = jnp.float32
WHOLE = pl.BlockSpec(memory_space=pltpu.VMEM)


def call(body, outs, *args, cost, limit=16 << 20, scratch=(), in_hbm=(), out_hbm=(), aliases={}):
    far = pl.BlockSpec(memory_space=pl.ANY)
    shapes = [
        jax.ShapeDtypeStruct(o[0], o[1]) if i in out_hbm else pltpu.VMEM(o[0], o[1])
        for i, o in enumerate(outs)
    ]
    return pl.pallas_call(
        body,
        out_shape=shapes,
        in_specs=[far if i in in_hbm else WHOLE for i in range(len(args))],
        out_specs=[far if i in out_hbm else WHOLE for i in range(len(outs))],
        scratch_shapes=scratch,
        input_output_aliases=aliases,
        cost_estimate=pl.CostEstimate(flops=0, bytes_accessed=cost, transcendentals=0),
        compiler_params=pltpu.CompilerParams(vmem_limit_bytes=limit),
    )(*[
        pltpu.with_memory_space_constraint(a, pltpu.HBM if i in in_hbm else pltpu.VMEM)
        for i, a in enumerate(args)
    ])


def lane_iota(rows):
    return lax.broadcasted_iota(jnp.int32, (rows, LANES), 1)


def row_iota(rows):
    return lax.broadcasted_iota(jnp.int32, (rows, LANES), 0)


def dot6(blocks, values):
    terms = [b.astype(F32) * v for b, v in zip(blocks, values)]
    return (terms[0] + terms[1]) + (terms[2] + terms[3]) + (terms[4] + terms[5])


def block(ref, *index, at):
    return lambda r, c: ref[(*index, r, c, slice(None), at)]


def apply_block(get, values):
    return [dot6([get(r, c) for c in range(VARS)], values) for r in range(VARS)]


def write_faces(value, x_face, y_face, z_count):
    y_count = value.shape[2]
    x_count = value.shape[3]
    lane = lane_iota(y_count)
    for group in range(x_face.shape[1]):
        faces = []
        for start, source_lane in ((0, 0), (x_count - LANES, LANES - 1)):
            held = jnp.zeros((y_count, LANES), F32)
            for slot in range(min(LANES, z_count * VARS - group * LANES)):
                z, var = divmod(group * LANES + slot, VARS)
                tile = value[z, var, :, start : start + LANES]
                moved = pltpu.roll(tile, (slot - source_lane) % LANES, 1)
                held = jnp.where(lane == slot, moved, held)
            faces.append(held)
        x_face[0, group], x_face[1, group] = faces
    if y_face.shape[0] == 1:
        first = lax.axis_index("gy") == 0
        for z in range(z_count):
            for var in range(VARS):
                low = value[z, var, 0:1, :]
                high = value[z, var, y_count - 1 : y_count, :]
                y_face[0, z, var : var + 1, :] = jnp.where(first, high, low)
    else:
        for z in range(z_count):
            for var in range(VARS):
                y_face[0, z, var : var + 1, :] = value[z, var, 0:1, :]
                y_face[1, z, var : var + 1, :] = value[z, var, y_count - 1 : y_count, :]


def halo_reader(x_all, y_rows, gx, gy):
    me_x = lax.axis_index("gx")

    def column(there, side, to_lane):
        exists = (there >= 0) & (there < gx)
        device = jnp.clip(there, 0, gx - 1)

        def read(z, var):
            j = z * VARS + var
            face = x_all[device, side, j // LANES]
            moved = pltpu.roll(face, (to_lane + LANES - j % LANES) % LANES, 1)
            return jnp.where(exists, moved, jnp.zeros_like(moved))

        return read

    def row(which):
        def read(z, var, at):
            if len(y_rows) > 1:
                return y_rows[which][z, var : var + 1, at]
            here = y_rows[0][z, var : var + 1, at]
            return jnp.where(lax.axis_index("gy") == 1 - which, here, jnp.zeros_like(here))

        return read

    return column(me_x - 1, 1, 0), column(me_x + 1, 0, LANES - 1), row(0), row(1)


def neighbours(value, z, tile, tiles, halo):
    y_count = value.shape[2]
    lane = lane_iota(y_count)
    row = row_iota(y_count)
    at = slice(tile * LANES, (tile + 1) * LANES)
    result = ([], [], [], [])
    for var in range(VARS):
        here = value[z, var, :, at]
        if tile > 0:
            before = pltpu.roll(value[z, var, :, at.start - LANES : at.start], 1, 1)
        else:
            before = halo[0](z, var)
        if tile < tiles - 1:
            after = pltpu.roll(value[z, var, :, at.stop : at.stop + LANES], LANES - 1, 1)
        else:
            after = halo[1](z, var)
        result[0].append(jnp.where(lane == 0, before, pltpu.roll(here, 1, 1)))
        result[1].append(jnp.where(lane == LANES - 1, after, pltpu.roll(here, LANES - 1, 1)))
        result[2].append(jnp.where(row == 0, halo[2](z, var, at), pltpu.roll(here, 1, 0)))
        result[3].append(
            jnp.where(row == y_count - 1, halo[3](z, var, at), pltpu.roll(here, y_count - 1, 0))
        )
    return result


def inplane(jacobians, value, z, tile, tiles, halo):
    at = slice(tile * LANES, (tile + 1) * LANES)
    total = None
    for n, values in enumerate(neighbours(value, z, tile, tiles, halo)):
        part = apply_block(block(jacobians, z, n, at=at), values)
        total = part if total is None else [a + b for a, b in zip(total, part)]
    return total


def planes_of(ref, z, at):
    return [ref[z, var, :, at] for var in range(VARS)]


def solution(mesh):
    gz, gx, gy = (mesh.shape[a] for a in ("gz", "gx", "gy"))
    short = gz == 4

    def body(right_side, previous, diag_inverse, jacobians):
        rhs = jnp.transpose(right_side, (0, 2, 1, 3))
        prev = jnp.transpose(previous, (0, 2, 1, 3))
        inv = jnp.transpose(diag_inverse, (0, 2, 3, 1, 4))
        jac = jnp.transpose(jacobians, (0, 2, 3, 4, 1, 5))
        nz, _, ny, nx = rhs.shape
        tiles = nx // LANES
        assert nx % LANES == 0
        spans = [slice(t * LANES, (t + 1) * LANES) for t in range(tiles)]
        plane = ((VARS, ny, nx), F32)
        volume = ((nz, VARS, ny, nx), F32)
        x_groups = -(-nz * VARS // LANES)
        x_face = ((2, x_groups, ny, LANES), F32)
        y_face = ((1 if gy == 2 else 2, nz, VARS, nx), F32)
        matrix = ((VARS, VARS, ny, nx), F32)
        steps = ((nz, VARS, VARS, ny, nx), F32)
        blocks = ((nz, VARS, VARS, ny, nx), jac.dtype)
        side_blocks = ((nz, 4, VARS, VARS, ny, nx), jac.dtype)
        unit = 40 * nz * ny * nx

        def exchange(x_side, y_side):
            if gy == 2:
                rows = [lax.ppermute(y_side[0], "gy", [(0, 1), (1, 0)])]
            else:
                up = [(i, i + 1) for i in range(gy - 1)]
                rows = [
                    lax.ppermute(y_side[1], "gy", up),
                    lax.ppermute(y_side[0], "gy", [(j, i) for i, j in up]),
                ]
            return lax.all_gather(x_side, "gx"), *rows


        def forward_plane(source, inv_ref, low_jac, z, at, earlier):
            lagged = apply_block(block(low_jac, z, at=at), earlier)
            return apply_block(block(inv_ref, z, at=at), [a - b for a, b in zip(source, lagged)])

        def backward_plane(sweep, inner, inv_ref, high_jac, z, at, later):
            change = apply_block(block(high_jac, z, at=at), later)
            change = apply_block(block(inv_ref, z, at=at), [a + b for a, b in zip(change, inner)])
            return [a - b for a, b in zip(sweep, change)]

        def fast_plane(step_ref, plain_ref, z, at, before):
            moved = apply_block(block(step_ref, z, at=at), before)
            return [a + b for a, b in zip(planes_of(plain_ref, z, at), moved)]

        def make_fast(step_ref, plain_ref, inv_ref, couple_ref, plain_of):
            half = VARS // 2

            def step(z, carry):
                for at in spans:
                    couple, inverse = block(couple_ref, z, at=at), block(inv_ref, z, at=at)
                    for g in range(VARS // half):
                        columns = range(g * half, (g + 1) * half)
                        held = [[couple(k, c).astype(F32) for k in range(VARS)] for c in columns]
                        for r in range(VARS):
                            row = [inverse(r, k).astype(F32) for k in range(VARS)]
                            for i, c in enumerate(columns):
                                step_ref[z, r, c, :, at] = -dot6(row, held[i])
                    plain = plain_of(z, at, lambda values: apply_block(inverse, values))
                    for var in range(VARS):
                        plain_ref[z, var, :, at] = plain[var]
                return carry

            lax.fori_loop(0, nz, step, 0)

        def put(ref, values, at):
            for var in range(VARS):
                ref[var, :, at] = values[var]

        def incoming(refs, at):
            total = [refs[0][var, :, at] for var in range(VARS)]
            for ref in refs[1:]:
                total = [a + ref[var, :, at] for var, a in enumerate(total)]
            return tuple(total)

        def planes_in(ref, at):
            return [ref[var, :, at] for var in range(VARS)]

        def apply_matrix(matrix_ref, vector, at):
            return apply_block(block(matrix_ref, at=at), vector)

        def arrived(plain, matrix_ref, vector_ref, at):
            total = apply_matrix(matrix_ref, [vector_ref[var, :, at] for var in range(VARS)], at)
            for ref in plain:
                total = [a + ref[var, :, at] for var, a in enumerate(total)]
            return tuple(total)

        def forward_sweep(source_ref, inv_ref, low_jac, starts, keep=None, fast=None):
            def step(z, earlier):
                results = []
                for tile, at in enumerate(spans):
                    if fast is not None:
                        result = fast_plane(*fast, z, at, earlier[tile])
                    else:
                        source = planes_of(source_ref, z, at)
                        result = forward_plane(source, inv_ref, low_jac, z, at, earlier[tile])
                    if keep is not None:
                        keep(z, at, result)
                    results.append(tuple(result))
                return tuple(results)

            return lax.fori_loop(0, nz, step, starts)

        def backward_sweep(sweep_ref, inner_ref, inv_ref, high_jac, starts, keep=None, fast=None):
            def step(i, later):
                z = nz - 1 - i
                results = []
                for tile, at in enumerate(spans):
                    if fast is not None:
                        result = fast_plane(*fast, z, at, later[tile])
                    else:
                        sweep, inner = planes_of(sweep_ref, z, at), planes_of(inner_ref, z, at)
                        result = backward_plane(sweep, inner, inv_ref, high_jac, z, at, later[tile])
                    if keep is not None:
                        keep(z, tile, at, result)
                    results.append(tuple(result))
                return tuple(results)

            return lax.fori_loop(0, nz, step, starts)

        def transfer(matrix_ref, inv_ref, couple_ref, wait):
            half = VARS // 2
            groups = [range(g * half, (g + 1) * half) for g in range(VARS // half)]

            def plane_step(z, at, group, vectors):
                couple, inverse = block(couple_ref, z, at=at), block(inv_ref, z, at=at)
                middle = [[] for _ in group]
                for r in range(VARS):
                    row = [couple(r, c).astype(F32) for c in range(VARS)]
                    for i in range(len(group)):
                        middle[i].append(row[group[i]] if vectors is None else dot6(row, vectors[i]))
                for r in range(VARS):
                    row = [inverse(r, c).astype(F32) for c in range(VARS)]
                    for i, c in enumerate(group):
                        matrix_ref[r, c, :, at] = -dot6(row, middle[i])

            def step(i, carry):
                z = wait(i)
                for at in spans:
                    for group in groups:
                        vectors = [[matrix_ref[r, c, :, at] for r in range(VARS)] for c in group]
                        plane_step(z, at, group, vectors)
                return carry

            z = wait(0)
            for at in spans:
                for group in groups:
                    plane_step(z, at, group, None)
            lax.fori_loop(1, nz, step, 0)


        def open_kernel(prev_hbm, inv_hbm, jac_hbm, *rest):
            prev_ref, inv_ref, low_jac, x_side, y_side, *matrices, sem, sems = rest

            def copies(z):
                return [
                    pltpu.make_async_copy(inv_hbm.at[z], inv_ref.at[z], sems.at[0, z]),
                    pltpu.make_async_copy(jac_hbm.at[z, 4], low_jac.at[z], sems.at[1, z]),
                ]

            def wait(z):
                for copy in copies(z):
                    copy.wait()
                return z

            first_copy = pltpu.make_async_copy(prev_hbm, prev_ref, sem)
            first_copy.start()
            me = lax.axis_index("gz")
            here = me == 2

            def start_copies():
                for z in range(nz):
                    for copy in copies(z):
                        copy.start()

            if matrices:
                pl.when(me != 0)(start_copies)
            else:
                start_copies()
            if matrices:

                @pl.when(here)
                def _():
                    transfer(matrices[0], inv_ref, low_jac, wait)

            first_copy.wait()
            write_faces(prev_ref, x_side, y_side, nz)

            def rest_of_copies():
                for z in range(nz):
                    wait(z)

            if matrices:

                @pl.when(jnp.logical_not(here))
                def _():
                    matrices[0][...] = jnp.zeros(matrix[0], F32)
                    pl.when(me != 0)(rest_of_copies)

            else:
                rest_of_copies()

        def on(wanted, work):
            if wanted is None:
                work()
            else:
                pl.when(wanted(lax.axis_index("gz")))(work)

        def load_high(jac_hbm, high_jac, sem):
            return pltpu.make_async_copy(jac_hbm.at[:, 5], high_jac, sem)

        def first_kernel(rhs_hbm, jac_hbm, prev_ref, inv_ref, low_jac, x_all, *rest):
            *y_rows, source_ref, top_ref, sides, high_jac, rhs_ref, sems, high_sem = rest
            high_copy = load_high(jac_hbm, high_jac, high_sem)
            first_work(
                rhs_hbm, jac_hbm, prev_ref, inv_ref, low_jac, x_all, y_rows,
                source_ref, top_ref, sides, rhs_ref, sems, high_copy,
            )
            high_copy.wait()

        def first_ahead_kernel(rhs_hbm, jac_hbm, prev_ref, _, __, x_all, *rest):
            *y_rows, inv_hbm, source_ref, top_ref, sides, inv_ref, low_jac, rhs_ref, sems = rest

            @pl.when(lax.axis_index("gz") == 0)
            def _():
                first_work(
                    rhs_hbm, jac_hbm, prev_ref, inv_ref, low_jac, x_all, y_rows,
                    source_ref, top_ref, sides, rhs_ref, sems, None, inv_hbm,
                )

        def first_behind_kernel(*refs):
            jac_hbm, high_jac, high_sem = refs[1], refs[-4], refs[-1]
            inputs, top_before = refs[: len(first_args)], refs[len(first_args) + 1]
            source_ref, top_ref, sides, _, rhs_ref, sems, _ = refs[-7:]
            high_copy = load_high(jac_hbm, high_jac, high_sem)
            here = lax.axis_index("gz") == 0

            @pl.when(here)
            def _():
                high_copy.start()
                top_ref[...] = top_before[...]

            @pl.when(jnp.logical_not(here))
            def _():
                first_work(
                    *inputs[:6], inputs[6:], source_ref, top_ref, sides, rhs_ref, sems, high_copy
                )

            high_copy.wait()

        def first_work(
            rhs_hbm, jac_hbm, prev_ref, inv_ref, low_jac, x_all, y_rows,
            source_ref, top_ref, sides, rhs_ref, sems, also, inv_hbm=None,
        ):
            halo = halo_reader(x_all, y_rows, gx, gy)

            def copies(z):
                pairs = [(jac_hbm.at[z, 0:4], sides), (rhs_hbm.at[z], rhs_ref)]
                if inv_hbm is not None:
                    pairs += [(inv_hbm.at[z], inv_ref), (jac_hbm.at[z, 4], low_jac)]
                return [
                    pltpu.make_async_copy(far, near.at[z], sems.at[i, z])
                    for i, (far, near) in enumerate(pairs)
                ]

            for z in range(nz):
                for copy in copies(z):
                    copy.start()
            if also is not None:
                also.start()

            def step(z, earlier):
                for copy in copies(z):
                    copy.wait()
                results = []
                for tile, at in enumerate(spans):
                    lagged = inplane(sides, prev_ref, z, tile, tiles, halo)
                    source = [a - b for a, b in zip(planes_of(rhs_ref, z, at), lagged)]
                    for var in range(VARS):
                        source_ref[z, var, :, at] = source[var]
                    results.append(tuple(forward_plane(source, inv_ref, low_jac, z, at, earlier[tile])))
                return tuple(results)

            zero = tuple(jnp.zeros((ny, LANES), F32) for _ in range(VARS))
            top = lax.fori_loop(0, nz, step, (zero,) * tiles)
            for tile, at in enumerate(spans):
                put(top_ref, top[tile], at)

        def forward_kernel(source_ref, inv_ref, low_jac, *rest):
            came, top_ref = rest[:-1], rest[-1]
            starts = tuple(incoming(came, at) for at in spans)
            top = forward_sweep(source_ref, inv_ref, low_jac, starts)
            for tile, at in enumerate(spans):
                put(top_ref, top[tile], at)

        def forward_mid_kernel(low_ref, came_ref, source_ref, inv_ref, low_jac, top_ref):
            top_ref[...] = low_ref[...]

            @pl.when(lax.axis_index("gz") == 1)
            def _():
                forward_kernel(source_ref, inv_ref, low_jac, came_ref, top_ref)

        def either(wanted, work, fast):
            if fast is None:
                work(None)
                return
            here = wanted(lax.axis_index("gz"))
            pl.when(here)(lambda: work(fast))
            pl.when(jnp.logical_not(here))(lambda: work(None))

        def forward_last_kernel(source_ref, prev_ref, inv_ref, low_jac, *rest):
            came, (sweep_ref, change_ref, x_side, y_side) = rest[:-4], rest[-4:]
            fast = None
            if short:
                first, far, matrix_ref, near, *fast = came

            def keep(z, at, result):
                before = planes_of(prev_ref, z, at)
                for var in range(VARS):
                    sweep_ref[z, var, :, at] = result[var]
                    change_ref[z, var, :, at] = result[var] - before[var]

            def work(fast):
                if short:
                    starts = tuple(arrived((first, near), matrix_ref, far, at) for at in spans)
                else:
                    starts = tuple(incoming(came, at) for at in spans)
                forward_sweep(source_ref, inv_ref, low_jac, starts, keep, fast)

            either(lambda me: me == 3, work, fast)
            write_faces(change_ref, x_side, y_side, nz)

        def turn_kernel(wanted, sweep_ref, change_ref, inv_ref, sides, high_jac, x_all, *rest):
            y_rows, outs = rest[: 1 if gy == 2 else 2], rest[-2:]
            on(
                wanted,
                lambda: turn_work(
                    sweep_ref, change_ref, inv_ref, sides, high_jac, x_all, y_rows, *outs
                ),
            )

        def turn_again_kernel(wanted, *refs):
            refs[-1][...] = refs[-3][...]
            turn_kernel(wanted, *refs)

        def turn_work(
            sweep_ref, change_ref, inv_ref, sides, high_jac, x_all, y_rows, inner_ref, low_ref
        ):
            halo = halo_reader(x_all, y_rows, gx, gy)
            for tile, at in enumerate(spans):

                def step(i, later, tile=tile, at=at):
                    z = nz - 1 - i
                    inner = inplane(sides, change_ref, z, tile, tiles, halo)
                    for var in range(VARS):
                        inner_ref[z, var, :, at] = inner[var]
                    sweep = planes_of(sweep_ref, z, at)
                    return tuple(backward_plane(sweep, inner, inv_ref, high_jac, z, at, later))

                zero = tuple(jnp.zeros((ny, LANES), F32) for _ in range(VARS))
                put(low_ref, lax.fori_loop(0, nz, step, zero), at)

        def only(device, work, ref, shape):
            here = lax.axis_index("gz") == device
            pl.when(here)(work)

            @pl.when(jnp.logical_not(here))
            def _():
                ref[...] = jnp.zeros(shape, F32)

        def down_matrix(inv_ref, high_jac, matrix_ref):
            transfer(matrix_ref, inv_ref, high_jac, lambda i: nz - 1 - i)

        def forward_idle_kernel(inv_ref, high_jac, low_jac, source_ref, _, matrix_ref, step_ref, plain_ref):
            only(1, lambda: down_matrix(inv_ref, high_jac, matrix_ref), matrix_ref, matrix[0])

            @pl.when(lax.axis_index("gz") == 3)
            def _():
                def plain_of(z, at, times):
                    return times(planes_of(source_ref, z, at))

                make_fast(step_ref, plain_ref, inv_ref, low_jac, plain_of)

        def backward_fast(inv_ref, high_jac, sweep_ref, inner_ref, step_ref, plain_ref):
            def plain_of(z, at, times):
                moved = times(planes_of(inner_ref, z, at))
                return [a - b for a, b in zip(planes_of(sweep_ref, z, at), moved)]

            make_fast(step_ref, plain_ref, inv_ref, high_jac, plain_of)

        def backward_idle_kernel(*refs):
            me = lax.axis_index("gz")
            pl.when((me == 0) | (me == 2))(lambda: backward_fast(*refs))

        def late_idle_kernel(inv_ref, high_jac, sweep_ref, inner_ref, _, __, ___, *outs):
            me = lax.axis_index("gz")
            pl.when(me == 1)(lambda: backward_fast(inv_ref, high_jac, sweep_ref, inner_ref, *outs))

        def backward_kernel(sweep_ref, inner_ref, inv_ref, high_jac, *rest):
            came, low_ref = rest[:-1], rest[-1]
            starts = tuple(incoming(came, at) for at in spans)
            low = backward_sweep(sweep_ref, inner_ref, inv_ref, high_jac, starts)
            for tile, at in enumerate(spans):
                put(low_ref, low[tile], at)

        def pass_kernel(*refs):
            pass

        def backward_mid_kernel(own_ref, came_ref, step_ref, plain_ref, low_ref):
            here = lax.axis_index("gz") == 2

            @pl.when(here)
            def _():
                starts = tuple(incoming((came_ref,), at) for at in spans)
                low = backward_sweep(None, None, None, None, starts, fast=(step_ref, plain_ref))
                for tile, at in enumerate(spans):
                    put(low_ref, low[tile], at)

            @pl.when(jnp.logical_not(here))
            def _():
                low_ref[...] = own_ref[...]

        def update_kernel(sweep_ref, inner_ref, inv_ref, high_jac, *rest):
            came, (out_hbm, held, sems) = rest[:-3], rest[-3:]
            fast = None
            if short:
                first, far, matrix_ref, near, *fast = came

            def out_copy(z):
                return pltpu.make_async_copy(held.at[z], out_hbm.at[z], sems.at[z])

            def keep(z, tile, at, result):
                for var in range(VARS):
                    held[z, var, :, at] = result[var]
                if tile == tiles - 1:
                    out_copy(z).start()

            def work(fast):
                if short:
                    starts = tuple(arrived((first, near), matrix_ref, far, at) for at in spans)
                else:
                    starts = tuple(incoming(came, at) for at in spans)
                backward_sweep(sweep_ref, inner_ref, inv_ref, high_jac, starts, keep, fast)

            either(lambda me: me != 3, work, fast)
            for z in range(nz):
                out_copy(z).wait()


        inv_far = inv
        prev, inv, low_jac, x_side, y_side, *up_matrix = call(
            open_kernel,
            [volume, blocks, blocks, x_face, y_face] + [matrix] * (1 if short else 0),
            prev,
            inv,
            jac,
            cost=12 * unit,
            in_hbm=(0, 1, 2),
            scratch=[pltpu.SemaphoreType.DMA, pltpu.SemaphoreType.DMA((2, nz))],
        )
        if short:
            up_there = lax.ppermute(up_matrix[0], "gz", [(2, 3)])
        halo = exchange(x_side, y_side)
        first_args = [rhs, jac, prev, inv, low_jac, *halo]
        first_scratch = [pltpu.VMEM(rhs.shape, F32), pltpu.SemaphoreType.DMA((4, nz))]
        if short:
            n = len(first_args)
            source, top, sides, inv, low_jac = call(
                first_ahead_kernel,
                [volume, plane, side_blocks, blocks, blocks],
                *first_args,
                inv_far,
                cost=unit // 8,
                in_hbm=(0, 1, n),
                aliases={3: 3, 4: 4},
                scratch=first_scratch,
            )
            first_args[3:5] = inv, low_jac
            first = lax.ppermute(top, "gz", [(0, 1)])
            source, top, sides, high_jac = call(
                first_behind_kernel,
                [volume, plane, side_blocks, blocks],
                *first_args,
                source,
                top,
                sides,
                cost=unit // 8,
                in_hbm=(0, 1),
                aliases={n: 0, n + 2: 2},
                scratch=first_scratch + [pltpu.SemaphoreType.DMA],
            )
            (top,) = call(
                forward_mid_kernel,
                [plane],
                top,
                first,
                source,
                inv,
                low_jac,
                cost=unit // 8,
            )
            far = lax.ppermute(top, "gz", [(1, 3)])
            near = lax.ppermute(top, "gz", [(1, 2), (2, 3)])
            down_one, *fast = call(
                forward_idle_kernel,
                [matrix, steps, volume],
                inv,
                high_jac,
                low_jac,
                source,
                up_there,
                cost=unit // 8,
            )
            (down_one,) = call(
                pass_kernel, [matrix], down_one, near, far, cost=unit // 8, aliases={0: 0}
            )
            down_there = lax.ppermute(down_one, "gz", [(1, 0)])
            came = [first, far, up_there, near, *fast]
        else:
            source, top, sides, high_jac = call(
                first_kernel,
                [volume, plane, side_blocks, blocks],
                *first_args,
                cost=14 * unit,
                in_hbm=(0, 1),
                scratch=first_scratch + [pltpu.SemaphoreType.DMA],
            )
            came = []
            for hop in range(gz - 1):
                if hop:
                    (top,) = call(
                        forward_kernel, [plane], source, inv, low_jac, *came, cost=3 * unit
                    )
                came.append(lax.ppermute(top, "gz", [(hop, hop + 1)]))
        sweep, change, x_side, y_side = call(
            forward_last_kernel,
            [volume, volume, x_face, y_face],
            source,
            prev,
            inv,
            low_jac,
            *came,
            cost=4 * unit,
        )
        halo = exchange(x_side, y_side)
        if short:
            ahead, behind = (lambda device: device == 3), (lambda device: device != 3)
        turn_args = [sweep, change, inv, sides, high_jac, *halo]
        inner, low = call(
            functools.partial(turn_kernel, ahead), [volume, plane], *turn_args, cost=11 * unit
        )
        if short:
            ahead_low = low
            inner, low = call(
                functools.partial(turn_again_kernel, behind),
                [volume, plane],
                *turn_args,
                inner,
                low,
                aliases={len(turn_args): 0},
                cost=unit // 8,
            )
            first = lax.ppermute(ahead_low, "gz", [(3, 2)])
            fast = call(
                backward_idle_kernel,
                [steps, volume],
                inv,
                high_jac,
                sweep,
                inner,
                cost=unit // 8,
            )
            (low,) = call(backward_mid_kernel, [plane], low, first, *fast, cost=unit // 8)
            far = lax.ppermute(low, "gz", [(2, 0)])
            near = lax.ppermute(low, "gz", [(2, 1), (1, 0)])
            fast = call(
                late_idle_kernel,
                [steps, volume],
                inv,
                high_jac,
                sweep,
                inner,
                *fast,
                low,
                cost=unit // 8,
                aliases={4: 0, 5: 1},
            )
            came = [first, far, down_there, near, *fast]
        else:
            came = []
            for hop in range(gz - 1, 0, -1):
                if came:
                    (low,) = call(
                        backward_kernel, [plane], sweep, inner, inv, high_jac, *came, cost=3 * unit
                    )
                came.append(lax.ppermute(low, "gz", [(hop, hop - 1)]))
        (update,) = call(
            update_kernel,
            [volume],
            sweep,
            inner,
            inv,
            high_jac,
            *came,
            cost=5 * unit,
            out_hbm=(0,),
            scratch=[pltpu.VMEM(volume[0], F32), pltpu.SemaphoreType.DMA((nz,))],
        )
        return jnp.transpose(update, (0, 2, 1, 3))

    placed = (
        P("gz", "gy", None, "gx"),
        P("gz", "gy", None, "gx"),
        P("gz", "gy", None, None, "gx"),
        P("gz", "gy", None, None, None, "gx"),
    )
    return jax.shard_map(
        body, mesh=mesh, in_specs=placed, out_specs=P("gz", "gy", None, "gx"), check_vma=False
    )
```
